256 devices in a mesh: grp: 2 (over z_hi), lat: 128 (over x, y, z_lo, core).
Axes of the slice: x: 4, y: 4, z: 8 (z_hi: 2, z_lo: 4; z = z_hi * 4 + z_lo), core: 2. Of those that a mesh axis runs over, the one named last changes fastest.
Arguments:
- fields: bfloat16 [2, 256, 128, 384], P('grp', 'lat'), may hold values from -6 to 6
- cotangent: bfloat16 [2, 256, 128, 384], P('grp', 'lat'), may hold values from -6 to 6
- ocean_kernels: bfloat16 [2, 3, 3, 192, 192], replicated, may hold values from -0.15625 to 0.15625
- atmos_kernels: bfloat16 [2, 3, 3, 384, 384], replicated, may hold values from -0.109375 to 0.109375
- ocean_surface: bfloat16 [192, 4], replicated, may hold values from -0.4375 to 0.4375
- ocean_coupling: bfloat16 [4, 192], replicated, may hold values from -3 to 3
- atmos_flux: bfloat16 [384, 4], replicated, may hold values from -0.3125 to 0.3125
- atmos_coupling: bfloat16 [4, 384], replicated, may hold values from -3 to 3
- row_map: int32 [256], P('lat'), may hold values from 0 to 255, as said below
- wet_mask: int32 [256, 256], P('lat'), may hold values 0 or 1
Outputs:
- next_fields: bfloat16 [2, 256, 128, 384], P('grp', 'lat')
- field_grads: bfloat16 [2, 256, 128, 384], P('grp', 'lat')
- ocean_kernel_grad: float32 [663552], P(('grp', 'lat'))
- atmos_kernel_grad: float32 [2654208], P(('grp', 'lat'))
The draws below stay inside these ranges and needn't reach their ends.
Inputs may be any that keep to these rules, and one draw needn't show every extreme that they name: row_map never falls, keeps each ocean row in its own band of 2 rows, and maps the first and last row of every band to that band's first and last row.
All inputs are finite; a program needn't handle non-finite values. No bound on the sum of `wet_mask` on one device may be relied on, other than what follows from the above.
Results may differ from the reference program's by a relative error of at most 0.0065.
Values may be sent and summed in bfloat16 or wider, within the bound.
A program may use at most 128 MiB of HBM per device.

```python
import math
import jax
import jax.numpy as jnp
from jax import lax

BAND = 2
LON = 128
COCEAN = 192
CATMOS = 384
NSURF = 4
ROWS = 256


def draw_row_map(key, part):
    key = jax.random.fold_in(key, 11)
    band_total = ROWS // BAND
    picks = jax.random.randint(key, (band_total, BAND), 0, BAND)
    picks = jnp.sort(picks, axis=1)
    picks = picks.at[:, 0].set(0).at[:, BAND - 1].set(BAND - 1)
    starts = (jnp.arange(band_total, dtype=jnp.int32) * BAND)[:, None]
    return (picks + starts).reshape(ROWS).astype(jnp.int32)


def touch_ends(entries, key, smallest, largest):
    longest = entries.shape.index(max(entries.shape))
    spots = []
    for shift in (0, 1):
        where = [jax.random.randint(jax.random.fold_in(key, axis), (), 0, length) for axis, length in enumerate(entries.shape)]
        where[longest] = (where[longest] + shift) % entries.shape[longest]
        spots.append(tuple(where))
    return entries.at[spots[0]].set(smallest).at[spots[1]].set(largest)


def block_levels(rng, dims, shards, smallest, top_value):
    level = 1.0
    for position, parts in shards:
        steps = jax.random.uniform(jax.random.fold_in(jax.random.fold_in(rng, 6), position), (parts,), jnp.float32, smallest / len(shards), top_value / len(shards))
        level = level * jnp.repeat(jnp.exp(steps), dims[position] // parts).reshape((-1,) + (1,) * (len(dims) - 1 - position))
    return level


def scatter_about(stream_key, dims, scale, reach, cuts=(), kind=jnp.bfloat16):
    entries = jax.random.normal(stream_key, dims, jnp.float32) * scale
    if len(cuts) > 0:
        entries = block_levels(stream_key, dims, cuts, -0.22, 0.18) * entries
    return jnp.clip(entries, min=-reach, max=reach).astype(kind)


def setup_inputs(seed: int = 0) -> dict:
    streams_of = jax.random.split(jax.random.key(seed), 11)
    return {
        "fields": scatter_about(streams_of[0], (2, ROWS, LON, CATMOS), 1.0, 6.0, ((0, 2), (1, 128))),
        "cotangent": scatter_about(streams_of[1], (2, ROWS, LON, CATMOS), 1.0, 6.0, ((0, 2), (1, 128))),
        "ocean_kernels": scatter_about(streams_of[2], (2, 3, 3, COCEAN, COCEAN), (9 * COCEAN) ** -0.5, 0.15625),
        "atmos_kernels": scatter_about(streams_of[3], (2, 3, 3, CATMOS, CATMOS), (9 * CATMOS) ** -0.5, 0.109375),
        "ocean_surface": scatter_about(streams_of[4], (COCEAN, NSURF), COCEAN ** -0.5, 0.4375),
        "ocean_coupling": scatter_about(streams_of[5], (NSURF, COCEAN), NSURF ** -0.5, 3.0),
        "atmos_flux": scatter_about(streams_of[6], (CATMOS, NSURF), CATMOS ** -0.5, 0.3125),
        "atmos_coupling": scatter_about(streams_of[7], (NSURF, CATMOS), NSURF ** -0.5, 3.0),
        "row_map": draw_row_map(jax.random.fold_in(streams_of[10], 71), 0),
        "wet_mask": touch_ends((jax.random.randint(streams_of[9], (ROWS, 2 * LON), 0, 4) < 3).astype(jnp.int32), jax.random.fold_in(streams_of[9], 1), 0, 1),
    }


HIGHEST = lax.Precision.HIGHEST
GELU_SCALE = 0.7978845608028654
GELU_CUBIC = 0.044715

def gelu_value(inputs):
    inside = GELU_SCALE * (inputs + GELU_CUBIC * inputs * inputs * inputs)
    return 0.5 * inputs * (1.0 + jnp.tanh(inside))

def gelu_slope(inputs):
    tangent = jnp.tanh(GELU_SCALE * (inputs + GELU_CUBIC * inputs * inputs * inputs))
    return 0.5 * (1.0 + tangent) + 0.5 * inputs * (1.0 - tangent * tangent) * GELU_SCALE * (1.0 + 3.0 * GELU_CUBIC * inputs * inputs)

def rank_terms(weights, matrix):
    total = weights[0][:, None] * matrix[0][None, :]
    for index in range(1, matrix.shape[0]):
        total = total + weights[index][:, None] * matrix[index][None, :]
    return total

def project_rows(values, matrix):
    return jnp.stack([lax.optimization_barrier(jnp.sum(values * matrix[index][None, :], axis=1)) for index in range(matrix.shape[0])])

def narrow_dot(values, matrix):
    return jnp.dot(values.astype(jnp.float32), matrix.astype(jnp.float32), precision=HIGHEST, preferred_element_type=jnp.float32)

def convolve(values, kernel):
    row_count, col_count, channels = values.shape
    padded = jnp.pad(values, ((1, 1), (1, 1), (0, 0)))
    total = jnp.zeros((row_count * col_count, kernel.shape[3]), jnp.float32)
    for row_tap in range(3):
        for col_tap in range(3):
            piece = padded[row_tap:row_tap + row_count, col_tap:col_tap + col_count].reshape(row_count * col_count, channels)
            total = total + jnp.dot(piece, kernel[row_tap, col_tap], preferred_element_type=jnp.float32)
    return total.reshape(row_count, col_count, kernel.shape[3])

def kernel_grad(values, outgrad, factor):
    row_count, col_count, channels = values.shape
    padded = jnp.pad(values, ((1, 1), (1, 1), (0, 0))).astype(jnp.float32)
    flat_grad = outgrad.reshape(row_count * col_count, -1).astype(jnp.float32)
    blocks = []
    for row_tap in range(3):
        for col_tap in range(3):
            piece = padded[row_tap:row_tap + row_count, col_tap:col_tap + col_count].reshape(row_count * col_count, channels)
            blocks.append(lax.dot_general(piece, flat_grad, (((0,), (0,)), ((), ())), precision=HIGHEST, preferred_element_type=jnp.float32))
    return jnp.stack(blocks).reshape(-1) * factor

def flip_kernel(kernel):
    return jnp.flip(kernel, (0, 1)).transpose(0, 1, 3, 2)

def component(values, outgrad, kernels, factor):
    first_out = convolve(values, kernels[0])
    hidden = gelu_value(first_out).astype(jnp.bfloat16)
    next_values = (values.astype(jnp.float32) + convolve(hidden, kernels[1])).astype(jnp.bfloat16)
    back_hidden = convolve(outgrad, flip_kernel(kernels[1]))
    first_grad = (back_hidden * gelu_slope(first_out)).astype(jnp.bfloat16)
    input_grad = outgrad.astype(jnp.float32) + convolve(first_grad, flip_kernel(kernels[0]))
    grads = jnp.concatenate([kernel_grad(values, first_grad, factor), kernel_grad(hidden, outgrad, factor)])
    return (next_values, input_grad, grads)

def reference(fields, cotangent, ocean_kernels, atmos_kernels, ocean_surface, ocean_coupling, atmos_flux, atmos_coupling, row_map, wet_mask):
    ocean_field = fields[0].reshape(ROWS, 2 * LON, COCEAN)
    atmos_field = fields[1]
    select = (row_map[None, :] == jnp.arange(ROWS, dtype=jnp.int32)[:, None]).astype(jnp.float32)
    wetness = wet_mask.astype(jnp.float32).reshape(ROWS, LON, 2)
    covered = jnp.einsum('ar,rlt->al', select, wetness, precision=HIGHEST)
    inverse = 1.0 / jnp.maximum(covered, 1.0)
    projected = narrow_dot(ocean_field.reshape(-1, COCEAN), ocean_surface).T
    summed = lax.optimization_barrier(jnp.sum(projected.reshape(NSURF, ROWS, LON, 2) * wetness[None], axis=3))
    surface = jnp.einsum('ar,frl->fal', select, summed, precision=HIGHEST) * inverse[None]
    flux_out = narrow_dot(atmos_field.reshape(-1, CATMOS), atmos_flux).T.reshape(NSURF, ROWS, LON)
    rows_flux = jnp.einsum('ar,fal->frl', select, flux_out, precision=HIGHEST)
    spread = (rows_flux[..., None] * wetness[None]).reshape(NSURF, -1)
    ocean_term = rank_terms(spread, ocean_coupling.astype(jnp.float32))
    ocean_in = (ocean_field.reshape(-1, COCEAN).astype(jnp.float32) + ocean_term).astype(jnp.bfloat16).reshape(ROWS, 2 * LON, COCEAN)
    atmos_term = rank_terms(surface.reshape(NSURF, -1), atmos_coupling.astype(jnp.float32))
    atmos_in = (atmos_field.reshape(-1, CATMOS).astype(jnp.float32) + atmos_term).astype(jnp.bfloat16).reshape(ROWS, LON, CATMOS)
    ocean_next, ocean_back, ocean_grads = component(ocean_in, cotangent[0].reshape(ROWS, 2 * LON, COCEAN), ocean_kernels, 1.0 / math.sqrt(ROWS * 2 * LON))
    atmos_next, atmos_back, atmos_grads = component(atmos_in, cotangent[1], atmos_kernels, 1.0 / math.sqrt(ROWS * LON))
    weighted = project_rows(ocean_back.reshape(-1, COCEAN), ocean_coupling.astype(jnp.float32))
    weighted_sum = lax.optimization_barrier(jnp.sum(weighted.reshape(NSURF, ROWS, LON, 2) * wetness[None], axis=3))
    flux_grad = jnp.einsum('ar,frl->fal', select, weighted_sum, precision=HIGHEST)
    surface_grad = project_rows(atmos_back.reshape(-1, CATMOS), atmos_coupling.astype(jnp.float32)).reshape(NSURF, ROWS, LON)
    rows_back = jnp.einsum('ar,fal->frl', select, surface_grad * inverse[None], precision=HIGHEST)
    spread_back = (rows_back[..., None] * wetness[None]).reshape(NSURF, -1)
    ocean_extra = rank_terms(spread_back, ocean_surface.astype(jnp.float32).T)
    ocean_grad = (ocean_back.reshape(-1, COCEAN) + ocean_extra).astype(jnp.bfloat16).reshape(ROWS, LON, CATMOS)
    atmos_extra = rank_terms(flux_grad.reshape(NSURF, -1), atmos_flux.astype(jnp.float32).T)
    atmos_grad = (atmos_back.reshape(-1, CATMOS) + atmos_extra).astype(jnp.bfloat16).reshape(ROWS, LON, CATMOS)
    next_fields = jnp.stack([ocean_next.reshape(ROWS, LON, CATMOS), atmos_next])
    field_grads = jnp.stack([ocean_grad, atmos_grad])
    return (next_fields, field_grads, ocean_grads, atmos_grads)
```

```python
import math

import jax
import jax.numpy as jnp
from jax import lax
from jax.experimental import pallas as pl
from jax.experimental.pallas import tpu as pltpu
from jax.sharding import PartitionSpec as P

MESH = pl.DeviceIdType.MESH
F32 = jnp.float32
BF16 = jnp.bfloat16
GELU_SCALE = 0.7978845608028654
GELU_CUBIC = 0.044715
CH = 384
COLS = 128
WIN = 224
NSEM = 64


def nt_dot(a, b):
    return lax.dot_general(a, b, (((1,), (1,)), ((), ())), preferred_element_type=F32)


def tn_dot(a, b):
    return lax.dot_general(a, b, (((0,), (0,)), ((), ())), preferred_element_type=F32)


def mm(a, b):
    return jnp.dot(a, b, preferred_element_type=F32)


def split_pair(values):
    high = values.astype(BF16).astype(F32)
    return jnp.concatenate([high, values - high], axis=0).astype(BF16)


def body(
    x_ref, g_ref, ak_ref, ok_ref, m_ref, c_ref, wm_ref,
    next_ref, fgrad_ref, grads_ref,
    w, okv, xp, gp, hp, fp, up, gcat, ucat, hcat, fcat,
    wmp, trs, trp, tr2s, tr2r, first, bh, ig,
    s_a, r_a, s_b, r_b, b4, b4s, at, at2,
    part, rec1, rec2, part2, rec3, rec4, dsum, zrec, esum, fin, out,
    wsem, ssem, rsem,
):
    g = lax.axis_index("grp")
    lat = lax.axis_index("lat")
    core = lat % 2
    z = (lat // 2) % 4
    y = (lat // 8) % 4
    x = lat // 32

    def spot(xx, yy, zz, cc):
        return xx * 32 + yy * 8 + zz * 2 + cc

    dn = (lat + 1) % 128
    up_lat = (lat + 127) % 128
    x_plus, x_minus = spot((x + 1) % 4, y, z, core), spot((x + 3) % 4, y, z, core)
    y_plus, y_minus = spot(x, (y + 1) % 4, z, core), spot(x, (y + 3) % 4, z, core)
    z_other = [spot(x, y, (z + k) % 4, core) for k in (1, 2, 3)]
    mate = lat + 1 - 2 * core
    has_top = jnp.where(lat > 0, 1.0, 0.0).astype(F32)
    has_low = jnp.where(lat < 127, 1.0, 0.0).astype(F32)
    edge = [has_top, None, None, has_low]

    atmos_copy = pltpu.make_async_copy(ak_ref, w, wsem.at[0])
    ocean_copy = pltpu.make_async_copy(ok_ref, okv, wsem.at[1])

    @pl.when(g == 1)
    def _():
        atmos_copy.start()

    @pl.when(g == 0)
    def _():
        ocean_copy.start()

    barrier = pltpu.get_barrier_semaphore()
    partners = [(g, dn), (g, up_lat), (1 - g, lat), (1 - g, dn), (1 - g, up_lat)]
    partners += [(g, other) for other in (x_plus, x_minus, y_plus, y_minus, *z_other)]
    for device in partners:
        pl.semaphore_signal(barrier, inc=1, device_id=device, device_id_type=MESH)
    pl.semaphore_wait(barrier, len(partners))

    used = []

    def send(src, dst, device):
        index = len(used)
        copy = pltpu.make_async_remote_copy(
            src_ref=src, dst_ref=dst, send_sem=ssem.at[index], recv_sem=rsem.at[index],
            device_id=device, device_id_type=MESH,
        )
        copy.start()
        used.append(copy)
        return copy

    g_low = send(g_ref.at[1], gp.at[0], (g, dn))
    g_top = send(g_ref.at[0], gp.at[3], (g, up_lat))
    x_low = send(x_ref.at[1], xp.at[0], (g, dn))
    x_top = send(x_ref.at[0], xp.at[3], (g, up_lat))
    m_low = send(wm_ref.at[1, 0], wmp.at[0], (g, dn))
    m_top = send(wm_ref.at[0, 0], wmp.at[3], (g, up_lat))

    for row in range(2):
        shown = nt_dot(m_ref[...], x_ref[row])[0:8] * wm_ref[row, 0]
        trs[row] = (shown + pltpu.roll(shown, 4, 0)) * wm_ref[row, 1]
    t_mid = send(trs, trp.at[pl.ds(1, 2)], (1 - g, lat))
    t_low = send(trs.at[1], trp.at[0], (1 - g, dn))
    t_top = send(trs.at[0], trp.at[3], (1 - g, up_lat))

    column = lax.broadcasted_iota(jnp.int32, (COLS, CH), 0)

    def put_cat(dst, index, values):
        dst[index, :, CH:2 * CH] = values.astype(BF16)
        dst[index, :, 0:CH] = jnp.where(column > 0, pltpu.roll(values, 1, 0), 0.0).astype(BF16)
        dst[index, :, 2 * CH:3 * CH] = jnp.where(
            column < COLS - 1, pltpu.roll(values, COLS - 1, 0), 0.0
        ).astype(BF16)

    def conv(cat, layer):
        total = None
        for p in range(3):
            term = mm(cat[p:p + 2].reshape(2 * COLS, 3 * CH), w[layer, p])
            total = term if total is None else total + term
        return total

    def conv_back(cat, layer):
        total = None
        for p in range(3):
            for q in range(3):
                rows = cat[p:p + 2, :, q * CH:(q + 1) * CH].reshape(2 * COLS, CH)
                term = nt_dot(rows, w[layer, 2 - p, (2 - q) * CH:(3 - q) * CH, :])
                total = term if total is None else total + term
        return total

    @pl.when(g == 0)
    def _():
        ocean_copy.wait()
        half = CH // 2
        row_id = lax.broadcasted_iota(jnp.int32, (half, CH), 0)
        lane_id = lax.broadcasted_iota(jnp.int32, (half, CH), 1)
        lower = jnp.where(row_id == lane_id, 1.0, 0.0).astype(BF16)
        upper = jnp.where(row_id + half == lane_id, 1.0, 0.0).astype(BF16)
        zero = jnp.zeros((half, CH), BF16)
        for layer in range(2):
            for p in range(3):
                taps = [okv[layer, p, half * q:half * (q + 1), :] for q in range(3)]
                low = [mm(tap, lower) for tap in taps]
                high = [mm(tap, upper) for tap in taps]
                blocks = [low[0], low[1] + high[0], low[2] + high[1], high[2]]
                w[layer, p, 0:half, :] = zero
                w[layer, p, 5 * half:6 * half, :] = zero
                for index, block in enumerate(blocks):
                    w[layer, p, (index + 1) * half:(index + 2) * half, :] = block.astype(BF16)

    @pl.when(g == 1)
    def _():
        atmos_copy.wait()

    for row in range(2):
        put_cat(gcat, row + 1, g_ref[row].astype(F32))
    g_low.wait_recv()
    g_top.wait_recv()
    put_cat(gcat, 0, gp[0].astype(F32) * has_top)
    put_cat(gcat, 3, gp[3].astype(F32) * has_low)
    bh[...] = conv_back(gcat, 1)

    for copy in (x_low, x_top, m_low, m_top, t_mid, t_low, t_top):
        copy.wait_recv()
    for index in range(4):
        values = xp[index] if index in (0, 3) else x_ref[index - 1]
        mask = wmp[index] if index in (0, 3) else wm_ref[index - 1, 0]
        term = tn_dot(split_pair(mask * trp[index]), c_ref[...])
        total = (values.astype(F32) + term).astype(BF16).astype(F32)
        if edge[index] is not None:
            total = total * edge[index]
        up[index] = total.astype(BF16)
        put_cat(ucat, index, total)
    zed = conv(ucat, 0)
    tangent = jnp.tanh(GELU_SCALE * (zed + GELU_CUBIC * zed * zed * zed))
    hidden = (0.5 * zed * (1.0 + tangent)).astype(BF16).reshape(2, COLS, CH)
    slope = 0.5 * (1.0 + tangent) + 0.5 * zed * (1.0 - tangent * tangent) * GELU_SCALE * (
        1.0 + 3.0 * GELU_CUBIC * zed * zed
    )
    first_grad = (bh[...] * slope).astype(BF16).reshape(2, COLS, CH)
    hp[1:3] = hidden
    fp[1:3] = first_grad
    h_low = send(hp.at[2], hp.at[0], (g, dn))
    h_top = send(hp.at[1], hp.at[3], (g, up_lat))
    f_low = send(fp.at[2], fp.at[0], (g, dn))
    f_top = send(fp.at[1], fp.at[3], (g, up_lat))

    @pl.when(core == 0)
    def _():
        s_b[...] = g_ref[...]

    @pl.when(core == 1)
    def _():
        s_b[...] = fp[1:3]

    pair_b = send(s_b, r_b, (g, mate))
    for row in (1, 2):
        put_cat(hcat, row, hp[row].astype(F32))
        put_cat(fcat, row, fp[row].astype(F32))
    h_low.wait_recv()
    h_top.wait_recv()
    put_cat(hcat, 0, hp[0].astype(F32) * has_top)
    put_cat(hcat, 3, hp[3].astype(F32) * has_low)

    @pl.when(core == 0)
    def _():
        s_a[...] = hcat[0:2, :, CH:2 * CH]

    @pl.when(core == 1)
    def _():
        s_a[...] = up[2:4]

    pair_a = send(s_a, r_a, (g, mate))
    next_ref[...] = (up[1:3].astype(F32) + conv(hcat, 1).reshape(2, COLS, CH)).astype(BF16)
    pair_b.wait_recv()
    pair_a.wait_recv()

    @pl.when(core == 0)
    def _():
        b4[0:256] = fp[1:3].reshape(256, CH)
        b4[256:512] = r_b[...].reshape(256, CH)

    @pl.when(core == 1)
    def _():
        b4[0:256] = r_b[...].reshape(256, CH)
        b4[256:512] = g_ref[...].reshape(256, CH)

    put_cat(gcat, 0, r_a[0].astype(F32))
    put_cat(gcat, 1, r_a[1].astype(F32))

    def put_turned(index, source):
        turned = source.astype(F32).T.astype(BF16)

        @pl.when(g == 1)
        def _():
            for p in range(3):
                k = index - p
                if 0 <= k <= 3:
                    at[3 * CH * p:3 * CH * (p + 1), k * COLS:(k + 1) * COLS] = turned

        @pl.when(g == 0)
        def _():
            for p in range(3):
                k = index - p
                if 0 <= k <= 3:
                    at[576 * p:576 * (p + 1), k * COLS:(k + 1) * COLS] = turned[192:768]
                    at2[576 * p:576 * (p + 1), k * COLS:(k + 1) * COLS] = turned[384:960]

    @pl.when(core == 0)
    def _():
        for index in range(6):
            put_turned(index, ucat[index] if index < 4 else gcat[index - 4])

    @pl.when(core == 1)
    def _():
        for index in range(6):
            put_turned(index, gcat[index] if index < 2 else hcat[index - 2])

    def lane2(xq, yq):
        return xq + core * (yq - xq), yq + core * (xq - yq)

    @pl.when(g == 1)
    def _():
        def window(index, carry):
            xq, yq = index // 4, index % 4
            start = pl.multiple_of(index * 216 - 8 * (index % 2), 16)
            made = mm(at[pl.ds(start, WIN), :], b4[...]).astype(BF16)
            a2, b2 = lane2(xq, yq)
            part[0, xq, pl.ds(pl.multiple_of(yq * WIN, 16), WIN), :] = made[:, 0:128]
            part[1, yq, pl.ds(pl.multiple_of(xq * WIN, 16), WIN), :] = made[:, 128:256]
            part[2, a2, pl.ds(pl.multiple_of(b2 * WIN, 16), WIN), :] = made[:, 256:384]
            return carry

        lax.fori_loop(0, 16, window, 0)

    @pl.when(g == 0)
    def _():
        row_id = lax.broadcasted_iota(jnp.int32, (CH, 256), 0)
        lane_id = lax.broadcasted_iota(jnp.int32, (CH, 256), 1)
        swap = jnp.where(row_id == lane_id + 192, 1.0, 0.0).astype(BF16)
        b4s[...] = mm(b4[...], swap).astype(BF16)

        def window(index, carry):
            xq, yq = index // 4, index % 4
            start = pl.multiple_of(index * 108 - (12 * index) % 16, 16)
            made = mm(at[pl.ds(start, 128), :], b4[:, 0:256])
            made = (made + mm(at2[pl.ds(start, 128), :], b4s[...])).astype(BF16)
            part[0, xq, pl.ds(pl.multiple_of(yq * WIN, 16), 128), :] = made[:, 0:128]
            part[1, yq, pl.ds(pl.multiple_of(xq * WIN, 16), 128), :] = made[:, 128:256]
            return carry

        lax.fori_loop(0, 16, window, 0)

    ids_x, ids_y = (x, x_plus, x_minus), (y, y_plus, y_minus)
    mixed_a = tuple(a + core * (b - a) for a, b in zip(ids_x, ids_y))
    mixed_b = tuple(b + core * (a - b) for a, b in zip(ids_x, ids_y))
    orders = [(ids_x, ids_y), (ids_y, ids_x), (mixed_a, mixed_b)]

    def ring_start(lane, ids, source, near, far, rows):
        me, plus, minus = ids
        half = rows // 2
        low, high = pl.ds(0, half), pl.ds(half, half)
        ahead, behind, across = (me + 1) % 4, (me + 3) % 4, (me + 2) % 4
        one_p = send(source.at[lane, across, low], near.at[lane, 0], (g, plus))
        one_m = send(source.at[lane, across, high], near.at[lane, 1], (g, minus))
        two_p = send(source.at[lane, ahead, high], far.at[lane, 0, high], (g, plus))
        two_m = send(source.at[lane, behind, low], far.at[lane, 1, low], (g, minus))
        return one_p, one_m, two_p, two_m

    def ring_relay(lane, ids, source, near, far, rows, early):
        me, plus, minus = ids
        half = rows // 2
        low, high = pl.ds(0, half), pl.ds(half, half)
        ahead, behind = (me + 1) % 4, (me + 3) % 4
        early[0].wait_recv()
        source[lane, ahead, low, :] = (
            source[lane, ahead, low, :].astype(F32) + near[lane, 0].astype(F32)
        ).astype(BF16)
        three_p = send(source.at[lane, ahead, low], far.at[lane, 0, low], (g, plus))
        early[1].wait_recv()
        source[lane, behind, high, :] = (
            source[lane, behind, high, :].astype(F32) + near[lane, 1].astype(F32)
        ).astype(BF16)
        three_m = send(source.at[lane, behind, high], far.at[lane, 1, high], (g, minus))
        return early[2], early[3], three_p, three_m

    def ring_sum(lane, ids, source, far, late):
        for copy in late:
            copy.wait_recv()
        me = ids[0]
        return (
            source[lane, me].astype(F32) + far[lane, 0].astype(F32) + far[lane, 1].astype(F32)
        ).astype(BF16)

    begun = [ring_start(k, orders[k][0], part, rec1, rec2, 4 * WIN) for k in range(3)]

    f_low.wait_recv()
    f_top.wait_recv()
    put_cat(fcat, 0, fp[0].astype(F32) * has_top)
    put_cat(fcat, 3, fp[3].astype(F32) * has_low)
    ig[...] = g_ref[...].reshape(2 * COLS, CH).astype(F32) + conv_back(fcat, 0)

    begun = [ring_relay(k, orders[k][0], part, rec1, rec2, 4 * WIN, begun[k]) for k in range(3)]

    for row in range(2):
        grad = ig[row * COLS:(row + 1) * COLS, :]
        high = grad.astype(BF16)
        low = (grad - high.astype(F32)).astype(BF16)
        shown = (nt_dot(c_ref[...], high) + nt_dot(c_ref[...], low))[0:8] * wm_ref[row, 0]
        tr2s[row] = shown + pltpu.roll(shown, 4, 0)
    back = send(tr2s, tr2r, (1 - g, lat))

    begun2 = []
    for k in range(3):
        part2[k] = ring_sum(k, orders[k][0], part, rec2, begun[k]).reshape(4, WIN, 128)
        begun2.append(ring_start(k, orders[k][1], part2, rec3, rec4, WIN))

    back.wait_recv()
    for row in range(2):
        left = split_pair(wm_ref[row, 0] * wm_ref[row, 1] * tr2r[row])
        total = ig[row * COLS:(row + 1) * COLS, :] + tn_dot(left, m_ref[...])
        fgrad_ref[row] = total.astype(BF16)

    begun2 = [ring_relay(k, orders[k][1], part2, rec3, rec4, WIN, begun2[k]) for k in range(3)]
    for k in range(3):
        dsum[k] = ring_sum(k, orders[k][1], part2, rec4, begun2[k])

    def z_place(zz):
        place = g * (8 * (y % 2) + 54 * zz) + (1 - g) * ((12 * y) % 16 + 27 * zz)
        start = (place // 16) * 16 - 16 * g * (zz // 3)
        return place, pl.multiple_of(start, 16)

    z_copies = []
    for k in range(3):
        _, start = z_place((z + k + 1) % 4)
        z_copies.append(send(dsum.at[:, pl.ds(start, 80), :], zrec.at[k], (g, z_other[k])))
    place, start = z_place(z)
    total = dsum[:, pl.ds(start, 80), :].astype(F32)
    for k in range(3):
        z_copies[k].wait_recv()
        total = total + zrec[k].astype(F32)
    esum[:, 0:80, :] = total
    esum[:, 80:88, :] = jnp.zeros((3, 8, 128), F32)
    for target in range(2):
        fin[target] = esum[:, pl.ds(place - start + 27 * target * g, 32), :]

    def final_copy(source, comp, device, s_index, r_index):
        return pltpu.make_async_remote_copy(
            src_ref=fin.at[source], dst_ref=out.at[comp], send_sem=ssem.at[s_index],
            recv_sem=rsem.at[r_index], device_id=device, device_id_type=MESH,
        )

    base = len(used)
    base_lat = lat - core
    near_copy = final_copy(1 - core, g, (g, mate), base, base)
    far_zero = final_copy(0, g, (1 - g, base_lat), base + 1, base + 1)
    far_one = final_copy(1, g, (1 - g, base_lat + 1), base + 2, base + 1)

    @pl.when(core == g)
    def _():
        near_copy.start()
        out[g] = fin[core]
        near_copy.wait_send()

    @pl.when(core != g)
    def _():
        far_zero.start()
        far_one.start()
        far_zero.wait_send()
        far_one.wait_send()
        final_copy(0, g, (g, mate), base, base).wait_recv()

    final_copy(0, 1 - g, (1 - g, lat), base + 1, base + 1).wait_recv()
    grads_ref[...] = out[...]
    for copy in used:
        copy.wait_send()


def local(
    fields, cotangent, ocean_kernels, atmos_kernels, ocean_surface, ocean_coupling,
    atmos_flux, atmos_coupling, row_map, wet_mask,
):
    del row_map
    is_ocean = lax.axis_index("grp") == 0
    core = lax.axis_index("lat") % 2

    def paired(rows):
        none = jnp.zeros_like(rows)
        return jnp.concatenate(
            [jnp.concatenate([rows, none], axis=1), jnp.concatenate([none, rows], axis=1)], axis=0
        )

    def single(rows):
        return jnp.concatenate([rows, jnp.zeros_like(rows)], axis=0)

    def twice(rows):
        return jnp.concatenate([rows, rows], axis=0)

    m16 = twice(jnp.where(is_ocean, paired(ocean_surface.T), single(atmos_flux.T)))
    c16 = twice(jnp.where(is_ocean, paired(ocean_coupling), single(atmos_coupling)))
    wet = wet_mask.astype(F32).reshape(2, COLS, 2)
    covered = wet[:, :, 0] + wet[:, :, 1]
    inverse = jnp.where(is_ocean, 1.0 / jnp.maximum(covered, 1.0), 1.0)
    wet0 = jnp.where(is_ocean, wet[:, :, 0], 1.0)
    wet1 = jnp.where(is_ocean, wet[:, :, 1], 0.0)
    masks = jnp.stack([wet0, wet1], axis=1)[:, :, None, :]
    masks = jnp.broadcast_to(masks, (2, 2, 4, COLS)).reshape(2, 8, COLS)
    wm = jnp.stack([masks, jnp.broadcast_to(inverse[:, None, :], (2, 8, COLS))], axis=1)

    vmem = pl.BlockSpec(memory_space=pltpu.VMEM)
    hbm = pl.BlockSpec(memory_space=pl.ANY)
    rows4 = pltpu.VMEM((4, COLS, CH), BF16)
    rows2 = pltpu.VMEM((2, COLS, CH), BF16)
    cat4 = pltpu.VMEM((4, COLS, 3 * CH), BF16)
    wide = pltpu.VMEM((2 * COLS, CH), F32)
    small2, small4 = pltpu.VMEM((2, 8, COLS), F32), pltpu.VMEM((4, 8, COLS), F32)

    def buf(*shape):
        return pltpu.VMEM(shape, BF16)

    next_field, field_grad, grads = pl.pallas_call(
        body,
        out_shape=(
            jax.ShapeDtypeStruct((2, COLS, CH), BF16),
            jax.ShapeDtypeStruct((2, COLS, CH), BF16),
            jax.ShapeDtypeStruct((2, 3, 32, 128), F32),
        ),
        in_specs=[vmem, vmem, hbm, hbm, vmem, vmem, vmem],
        out_specs=(vmem, vmem, vmem),
        scratch_shapes=[
            buf(2, 3, 3 * CH, CH), buf(2, 3, 576, 192),
            rows4, rows4, rows4, rows4, rows4, cat4, cat4, cat4, cat4,
            small4, small2, small4, small2, small2, wide, wide, wide,
            rows2, rows2, rows2, rows2, buf(512, CH), buf(512, 256), buf(3456, 512), buf(1856, 512),
            buf(3, 4, 4 * WIN, 128), buf(3, 2, 2 * WIN, 128), buf(3, 2, 4 * WIN, 128),
            buf(3, 4, WIN, 128), buf(3, 2, WIN // 2, 128), buf(3, 2, WIN, 128),
            buf(3, WIN, 128), buf(3, 3, 80, 128),
            pltpu.VMEM((3, 88, 128), F32), pltpu.VMEM((2, 3, 32, 128), F32),
            pltpu.VMEM((2, 3, 32, 128), F32),
            pltpu.SemaphoreType.DMA((2,)), pltpu.SemaphoreType.DMA((NSEM,)),
            pltpu.SemaphoreType.DMA((NSEM,)),
        ],
        compiler_params=pltpu.CompilerParams(
            collective_id=0, has_side_effects=True, vmem_limit_bytes=56 * 1024 * 1024
        ),
        cost_estimate=pl.CostEstimate(
            flops=4_100_000_000, bytes_accessed=8_000_000, transcendentals=100_000
        ),
    )(
        fields[0], cotangent[0], atmos_kernels.reshape(2, 3, 3 * CH, CH),
        ocean_kernels.reshape(2, 3, 576, 192), m16, c16, wm,
    )
    flat = grads.transpose(0, 2, 1, 3).reshape(2, 32, CH)
    atmos_total = flat[1, :27].reshape(-1) * (1.0 / math.sqrt(256 * 128))
    ocean_pair = flat[0, :27, :192].reshape(2, 2592)
    ocean_total = jnp.where(core == 0, ocean_pair[0], ocean_pair[1]) * (1.0 / 256.0)
    return (next_field[None], field_grad[None], ocean_total, atmos_total)


def solution(mesh):
    in_specs = (
        P("grp", "lat", None, None),
        P("grp", "lat", None, None),
        P(),
        P(),
        P(),
        P(),
        P(),
        P(),
        P("lat"),
        P("lat", None),
    )
    out_specs = (
        P("grp", "lat", None, None),
        P("grp", "lat", None, None),
        P(("grp", "lat")),
        P(("grp", "lat")),
    )
    return jax.shard_map(local, mesh=mesh, in_specs=in_specs, out_specs=out_specs, check_vma=False)
```

```python
import math

import jax
import jax.numpy as jnp
from jax import lax
from jax.experimental import pallas as pl
from jax.experimental.pallas import tpu as pltpu
from jax.sharding import PartitionSpec as P

MESH = pl.DeviceIdType.MESH
F32 = jnp.float32
BF16 = jnp.bfloat16
GELU_SCALE = 0.7978845608028654
GELU_CUBIC = 0.044715
CH = 384
COLS = 128
WIN = 224
NSEM = 64


def nt_dot(a, b):
    return lax.dot_general(a, b, (((1,), (1,)), ((), ())), preferred_element_type=F32)


def tn_dot(a, b):
    return lax.dot_general(a, b, (((0,), (0,)), ((), ())), preferred_element_type=F32)


def mm(a, b):
    return jnp.dot(a, b, preferred_element_type=F32)


def split_pair(values):
    high = values.astype(BF16).astype(F32)
    return jnp.concatenate([high, values - high], axis=0).astype(BF16)


def body(
    x_ref, g_ref, ak_ref, ok_ref, os_ref, oc_ref, af_ref, ac_ref, wet_ref,
    next_ref, fgrad_ref, grads_ref,
    w, okv, xp, gp, hp, fp, up, gcat, ucat, hcat, fcat, acat,
    m8, c8, m16, c16, wm, wmp, trs, trp, tr2s, tr2r, bh, ig,
    s_a, r_a, s_b, r_b, b6, b6s, at, at2,
    part, rec1, rec2, part2, rec3, rec4, dsum, zsend, zrec,
    wsem, ssem, rsem,
):
    g = lax.axis_index("grp")
    lat = lax.axis_index("lat")
    core = lat % 2
    z = (lat // 2) % 4
    y = (lat // 8) % 4
    x = lat // 32

    def spot(xx, yy, zz, cc):
        return xx * 32 + yy * 8 + zz * 2 + cc

    dn = (lat + 1) % 128
    up_lat = (lat + 127) % 128
    x_plus, x_minus = spot((x + 1) % 4, y, z, core), spot((x + 3) % 4, y, z, core)
    y_plus, y_minus = spot(x, (y + 1) % 4, z, core), spot(x, (y + 3) % 4, z, core)
    mate = lat + 1 - 2 * core
    has_top = jnp.where(lat > 0, 1.0, 0.0).astype(F32)
    has_low = jnp.where(lat < 127, 1.0, 0.0).astype(F32)
    edge = [has_top, None, None, has_low]

    atmos_copy = pltpu.make_async_copy(ak_ref, w, wsem.at[0])
    ocean_copy = pltpu.make_async_copy(ok_ref, okv, wsem.at[1])

    @pl.when(g == 1)
    def _():
        atmos_copy.start()

    @pl.when(g == 0)
    def _():
        ocean_copy.start()

    barrier = pltpu.get_barrier_semaphore()
    partners = [(g, dn), (g, up_lat), (1 - g, dn), (1 - g, up_lat)]
    partners += [(g, other) for other in (x_plus, x_minus, y_plus, y_minus)]
    for step in range(16):
        if step > 0:
            hop = (step // 2) % 4
            partners.append(
                ((g + step // 8) % 2, spot(x, y, (z + hop) % 4, (core + step) % 2))
            )
    for device in partners:
        pl.semaphore_signal(barrier, inc=1, device_id=device, device_id_type=MESH)

    half = CH // 2
    row_id = lax.broadcasted_iota(jnp.int32, (half, CH), 0)
    lane_id = lax.broadcasted_iota(jnp.int32, (half, CH), 1)
    lower = jnp.where(row_id == lane_id, 1.0, 0.0).astype(BF16)
    upper = jnp.where(row_id + half == lane_id, 1.0, 0.0).astype(BF16)
    is_atmos = g.astype(F32)
    is_ocean = 1.0 - is_atmos
    for dst, ocean, atmos in ((m8, os_ref, af_ref), (c8, oc_ref, ac_ref)):
        dst[0:4] = mm(ocean[...], lower) * is_ocean + atmos[...].astype(F32) * is_atmos
        dst[4:8] = mm(ocean[...], upper) * is_ocean
    for dst, src in ((m16, m8), (c16, c8)):
        dst[...] = jnp.concatenate([src[...], src[...]], axis=0).astype(BF16)
    pick_row = lax.broadcasted_iota(jnp.int32, (256, 256), 0)
    pick_lane = lax.broadcasted_iota(jnp.int32, (256, 256), 1)
    pick_lane = jnp.where(pick_lane < COLS, 2 * pick_lane, 2 * pick_lane - 255)
    pick = jnp.where(pick_row == pick_lane, 1.0, 0.0).astype(BF16)
    first_half = lax.broadcasted_iota(jnp.int32, (8, COLS), 0) < 4
    for row in range(2):
        wet = jnp.broadcast_to(wet_ref[row:row + 1, :].astype(F32), (8, 256)).astype(BF16)
        apart = mm(wet, pick)
        even, odd = apart[:, 0:COLS], apart[:, COLS:]
        inverse = 1.0 / jnp.maximum(even + odd, 1.0)
        wm[row, 0] = jnp.where(
            first_half, even * is_ocean + is_atmos, odd * is_ocean
        )
        wm[row, 1] = inverse * is_ocean + is_atmos

    for row in range(2):
        shown = nt_dot(m16[...], x_ref[row])[0:8] * wm[row, 0]
        trs[row] = (shown + pltpu.roll(shown, 4, 0)) * wm[row, 1]
    pl.semaphore_wait(barrier, len(partners))

    used = []

    def arrive(copy):
        copy.wait_recv()

    def send(src, dst, device):
        index = len(used)
        copy = pltpu.make_async_remote_copy(
            src_ref=src, dst_ref=dst, send_sem=ssem.at[index], recv_sem=rsem.at[index],
            device_id=device, device_id_type=MESH,
        )
        copy.start()
        used.append(copy)
        return copy

    t_mid = send(trs, trp.at[pl.ds(1, 2)], (1 - g, lat))
    t_low = send(trs.at[1], trp.at[0], (1 - g, dn))
    t_top = send(trs.at[0], trp.at[3], (1 - g, up_lat))
    m_low = send(wm.at[1, 0], wmp.at[0], (g, dn))
    m_top = send(wm.at[0, 0], wmp.at[3], (g, up_lat))
    x_low = send(x_ref.at[1], xp.at[0], (g, dn))
    x_top = send(x_ref.at[0], xp.at[3], (g, up_lat))
    g_low = send(g_ref.at[1], gp.at[0], (g, dn))
    g_top = send(g_ref.at[0], gp.at[3], (g, up_lat))

    column = lax.broadcasted_iota(jnp.int32, (COLS, CH), 0)

    def put_cat(dst, index, values):
        dst[index, :, CH:2 * CH] = values.astype(BF16)
        dst[index, :, 0:CH] = jnp.where(column > 0, pltpu.roll(values, 1, 0), 0.0).astype(BF16)
        dst[index, :, 2 * CH:3 * CH] = jnp.where(
            column < COLS - 1, pltpu.roll(values, COLS - 1, 0), 0.0
        ).astype(BF16)

    def conv(cat, layer):
        total = None
        for p in range(3):
            term = mm(cat[p:p + 2].reshape(2 * COLS, 3 * CH), w[layer, p])
            total = term if total is None else total + term
        return total

    def back_rows(cat, layer, p, row, count):
        total = None
        for q in range(3):
            rows = cat[row:row + count, :, q * CH:(q + 1) * CH].reshape(count * COLS, CH)
            term = nt_dot(rows, w[layer, 2 - p, (2 - q) * CH:(3 - q) * CH, :])
            total = term if total is None else total + term
        return total

    @pl.when(g == 0)
    def _():
        ocean_copy.wait()
        for layer in range(2):
            for p in range(3):
                low = mm(okv[layer, p], lower)
                high = mm(okv[layer, p], upper)
                none = jnp.zeros((half, CH), F32)
                both = jnp.concatenate([low, none], axis=0) + jnp.concatenate([none, high], axis=0)
                w[layer, p, 0:half, :] = none.astype(BF16)
                w[layer, p, half:5 * half, :] = both.astype(BF16)
                w[layer, p, 5 * half:6 * half, :] = none.astype(BF16)

    @pl.when(g == 1)
    def _():
        atmos_copy.wait()

    for row in range(2):
        put_cat(gcat, row + 1, g_ref[row].astype(F32))
    bh[...] = back_rows(gcat, 1, 1, 1, 2)
    bh[0:COLS] += back_rows(gcat, 1, 2, 2, 1)
    bh[COLS:] += back_rows(gcat, 1, 0, 1, 1)

    for copy in (m_low, m_top, t_mid, t_low, t_top, x_low, x_top):
        arrive(copy)
    for index in range(4):
        values = xp[index] if index in (0, 3) else x_ref[index - 1]
        mask = wmp[index] if index in (0, 3) else wm[index - 1, 0]
        term = tn_dot(split_pair(mask * trp[index]), c16[...])
        total = (values.astype(F32) + term).astype(BF16).astype(F32)
        if edge[index] is not None:
            total = total * edge[index]
        up[index] = total.astype(BF16)
        put_cat(ucat, index, total)
    zed = conv(ucat, 0)

    arrive(g_low)
    arrive(g_top)
    top_values = gp[0].astype(F32) * has_top
    low_values = gp[3].astype(F32) * has_low
    gp[0] = top_values.astype(BF16)
    gp[3] = low_values.astype(BF16)
    put_cat(gcat, 0, top_values)
    put_cat(gcat, 3, low_values)

    @pl.when(core == 0)
    def _():
        s_a[0] = gp[0]
        s_a[1] = g_ref[0]

    @pl.when(core == 1)
    def _():
        s_a[...] = up[2:4]

    pair_a = send(s_a, r_a, (g, mate))
    bh[0:COLS] += back_rows(gcat, 1, 0, 0, 1)
    bh[COLS:] += back_rows(gcat, 1, 2, 3, 1)

    tangent = jnp.tanh(GELU_SCALE * (zed + GELU_CUBIC * zed * zed * zed))
    hidden = (0.5 * zed * (1.0 + tangent)).astype(BF16).reshape(2, COLS, CH)
    slope = 0.5 * (1.0 + tangent) + 0.5 * zed * (1.0 - tangent * tangent) * GELU_SCALE * (
        1.0 + 3.0 * GELU_CUBIC * zed * zed
    )
    first_grad = (bh[...] * slope).astype(BF16).reshape(2, COLS, CH)
    hp[1:3] = hidden
    fp[1:3] = first_grad

    @pl.when(core == 0)
    def _():
        s_b[...] = hp[1:3]

    @pl.when(core == 1)
    def _():
        s_b[...] = fp[1:3]

    pair_b = send(s_b, r_b, (g, mate))
    h_low = send(hp.at[2], hp.at[0], (g, dn))
    h_top = send(hp.at[1], hp.at[3], (g, up_lat))
    f_low = send(fp.at[2], fp.at[0], (g, dn))
    f_top = send(fp.at[1], fp.at[3], (g, up_lat))

    def put_turned(source, places):
        turned = source.astype(F32).T.astype(BF16)

        @pl.when(g == 1)
        def _():
            for block, k in places:
                at[3 * CH * block:3 * CH * (block + 1), k * COLS:(k + 1) * COLS] = turned

        @pl.when(g == 0)
        def _():
            for block, k in places:
                at[576 * block:576 * (block + 1), k * COLS:(k + 1) * COLS] = turned[192:768]
                at2[576 * block:576 * (block + 1), k * COLS:(k + 1) * COLS] = turned[384:960]

    for row in (1, 2):
        put_cat(hcat, row, hp[row].astype(F32))

    arrive(pair_a)

    @pl.when(core == 0)
    def _():
        put_cat(acat, 0, r_a[0].astype(F32))
        put_cat(acat, 1, r_a[1].astype(F32))
        for index in range(6):
            places = [(p, index - p) for p in range(3) if 0 <= index - p <= 3]
            put_turned(ucat[index] if index < 4 else acat[index - 4], places)
        b6[0:256] = fp[1:3].reshape(256, CH)

    @pl.when(core == 1)
    def _():
        for row in (1, 2):
            put_turned(hcat[row], [(0, row + 1)])
        b6[0:256] = r_a[...].reshape(256, CH)
        b6[256:384] = gp[0]
        b6[384:640] = g_ref[...].reshape(256, CH)
        b6[640:768] = gp[3]

    arrive(pair_b)

    @pl.when(core == 0)
    def _():
        b6[256:512] = r_b[...].reshape(256, CH)

    @pl.when(core == 1)
    def _():
        for row in range(2):
            put_cat(acat, row, r_b[row].astype(F32))
            put_turned(acat[row], [(0, row)])

    @pl.when(g == 0)
    def _():
        swap_row = lax.broadcasted_iota(jnp.int32, (CH, 256), 0)
        swap_lane = lax.broadcasted_iota(jnp.int32, (CH, 256), 1)
        swap = jnp.where(swap_row == swap_lane + 192, 1.0, 0.0).astype(BF16)
        b6s[...] = mm(b6[...], swap).astype(BF16)


    ids_x, ids_y = (x, x_plus, x_minus), (y, y_plus, y_minus)
    mixed_a = tuple(a + core * (b - a) for a, b in zip(ids_x, ids_y))
    mixed_b = tuple(b + core * (a - b) for a, b in zip(ids_x, ids_y))
    orders = [(ids_x, ids_y), (ids_y, ids_x), (mixed_a, mixed_b)]

    atmos_pieces = [
        [(0, 0, 0, 224), (208, 1, 0, 80)],
        [(0, 1, 80, 144), (144, 2, 0, 144)],
        [(0, 2, 144, 80), (64, 3, 0, 224)],
    ]
    ocean_pieces = [
        [(0, 0, 0, 112), (96, 1, 0, 48)],
        [(0, 1, 48, 80), (64, 2, 0, 80)],
        [(0, 2, 80, 48), (32, 3, 0, 112)],
    ]

    def gradient_block(xq):
        def place(j, rows):
            m = 3 * xq + j
            start = rows * (m + core * (m % 4 - m))
            return (
                pl.ds(pl.multiple_of(start, 16), rows),
                pl.ds(pl.multiple_of(core * (2 - m // 4) * COLS, 16), 512),
            )

        def store(lane, made, pieces):
            for src, yq, dst, count in pieces:
                if lane == 0:
                    a, b = xq, yq
                elif lane == 1:
                    a, b = yq, xq
                else:
                    a, b = xq + core * (yq - xq), yq + core * (xq - yq)
                rows = pl.ds(pl.multiple_of(b * WIN + dst, 16), count)
                part[lane, a, rows, :] = made[src:src + count]

        @pl.when(g == 1)
        def _():
            for j in range(3):
                left, right = place(j, 288)
                made = mm(at[left, :], b6[right, :]).astype(BF16)
                for lane in range(3):
                    store(lane, made[:, 128 * lane:128 * (lane + 1)], atmos_pieces[j])

        @pl.when(g == 0)
        def _():
            for j in range(3):
                left, right = place(j, 144)
                made = mm(at[left, :], b6[right, 0:256]) + mm(at2[left, :], b6s[right, :])
                made = made.astype(BF16)
                for lane in range(2):
                    store(lane, made[:, 128 * lane:128 * (lane + 1)], ocean_pieces[j])

    def parts_of(rows):
        return pl.ds(0, rows // 2), pl.ds(rows // 2, rows // 2)

    def ring_one(lane, ids, source, near, rows):
        me, plus, minus = ids
        low, high = parts_of(rows)
        across = (me + 2) % 4
        one_p = send(source.at[lane, across, low], near.at[lane, 0], (g, plus))
        one_m = send(source.at[lane, across, high], near.at[lane, 1], (g, minus))
        return one_p, one_m

    def ring_two(lane, ids, source, far, rows, plus_side):
        me, plus, minus = ids
        low, high = parts_of(rows)
        if plus_side:
            return send(source.at[lane, (me + 1) % 4, high], far.at[lane, 0, high], (g, plus))
        return send(source.at[lane, (me + 3) % 4, low], far.at[lane, 1, low], (g, minus))

    def ring_relay(lane, ids, source, near, far, rows, early):
        me, plus, minus = ids
        low, high = parts_of(rows)
        ahead, behind = (me + 1) % 4, (me + 3) % 4
        arrive(early[0])
        source[lane, ahead, low, :] = (
            source[lane, ahead, low, :].astype(F32) + near[lane, 0].astype(F32)
        ).astype(BF16)
        three_p = send(source.at[lane, ahead, low], far.at[lane, 0, low], (g, plus))
        arrive(early[1])
        source[lane, behind, high, :] = (
            source[lane, behind, high, :].astype(F32) + near[lane, 1].astype(F32)
        ).astype(BF16)
        three_m = send(source.at[lane, behind, high], far.at[lane, 1, high], (g, minus))
        return three_p, three_m

    def ring_sum(lane, ids, source, far, late):
        for copy in late:
            arrive(copy)
        me = ids[0]
        return source[lane, me].astype(F32) + far[lane, 0].astype(F32) + far[lane, 1].astype(F32)

    early, middle, late = [None] * 3, [None] * 3, [None] * 3
    gradient_block((x + 2) % 4)
    early[0] = ring_one(0, orders[0][0], part, rec1, 4 * WIN)
    gradient_block((x + 1) % 4)
    gradient_block((x + 3) % 4)
    gradient_block(x)
    for k in (1, 2):
        early[k] = ring_one(k, orders[k][0], part, rec1, 4 * WIN)
    for k in range(3):
        middle[k] = tuple(
            ring_two(k, orders[k][0], part, rec2, 4 * WIN, side) for side in (True, False)
        )

    arrive(h_low)
    arrive(h_top)
    put_cat(hcat, 0, hp[0].astype(F32) * has_top)
    put_cat(hcat, 3, hp[3].astype(F32) * has_low)
    next_ref[...] = (up[1:3].astype(F32) + conv(hcat, 1).reshape(2, COLS, CH)).astype(BF16)
    for k in range(3):
        late[k] = ring_relay(k, orders[k][0], part, rec1, rec2, 4 * WIN, early[k])

    for row in (1, 2):
        put_cat(fcat, row, fp[row].astype(F32))
    arrive(f_low)
    arrive(f_top)
    put_cat(fcat, 0, fp[0].astype(F32) * has_top)
    put_cat(fcat, 3, fp[3].astype(F32) * has_low)
    total = g_ref[...].reshape(2 * COLS, CH).astype(F32)
    for p in range(3):
        total = total + back_rows(fcat, 0, p, p, 2)
    ig[...] = total

    for row in range(2):
        grad = ig[row * COLS:(row + 1) * COLS, :]
        high = grad.astype(BF16)
        low = (grad - high.astype(F32)).astype(BF16)
        shown = (nt_dot(c16[...], high) + nt_dot(c16[...], low))[0:8] * wm[row, 0]
        tr2s[row] = shown + pltpu.roll(shown, 4, 0)
    back = send(tr2s, tr2r, (1 - g, lat))

    early2, middle2 = [], []
    for k in range(3):
        made = ring_sum(k, orders[k][0], part, rec2, middle[k] + late[k])
        part2[k] = made.astype(BF16).reshape(4, WIN, 128)
        early2.append(ring_one(k, orders[k][1], part2, rec3, WIN))
        middle2.append(tuple(
            ring_two(k, orders[k][1], part2, rec4, WIN, side) for side in (True, False)
        ))
    late2 = [
        ring_relay(k, orders[k][1], part2, rec3, rec4, WIN, early2[k]) for k in range(3)
    ]
    for k in range(3):
        dsum[k, 0:WIN] = ring_sum(k, orders[k][1], part2, rec4, middle2[k] + late2[k])

    base = len(used)

    def z_copy(slot, comp, k, device, index):
        return pltpu.make_async_remote_copy(
            src_ref=zsend.at[slot], dst_ref=zrec.at[comp, k], send_sem=ssem.at[base + index],
            recv_sem=rsem.at[base + comp * 4 + k], device_id=device, device_id_type=MESH,
        )

    dsum[:, WIN:WIN + 16] = jnp.zeros((3, 16, 128), F32)
    for hop in range(4):
        zz = (z + hop) % 4
        place = g * (8 * (y % 2) + 54 * zz) + (1 - g) * ((12 * y) % 16 + 27 * zz)
        for cc in range(2):
            slot = 2 * hop + cc
            zsend[slot] = dsum[:, pl.ds(place + 27 * cc * g, 32), :].astype(BF16)
            copy = z_copy(slot, g, (4 - hop) % 4, (core, spot(x, y, zz, cc)), slot)
            if hop > 0:
                copy.start()
            else:
                @pl.when((core != g) | (core != cc))
                def _():
                    copy.start()

    for row in range(2):
        if row == 0:
            arrive(back)
        left = split_pair(wm[row, 0] * wm[row, 1] * tr2r[row])
        total = ig[row * COLS:(row + 1) * COLS, :] + tn_dot(left, m16[...])
        fgrad_ref[row] = total.astype(BF16)

    @pl.when(core == g)
    def _():
        zrec[g, 0] = zsend[core]

    for comp in range(2):
        for k in range(4):
            copy = z_copy(0, comp, k, (g, mate), 0)
            if k > 0:
                copy.wait_recv()
            else:
                @pl.when((core != g) | (g != comp))
                def _():
                    copy.wait_recv()

        total = zrec[comp, 0].astype(F32)
        for k in range(1, 4):
            total = total + zrec[comp, k].astype(F32)
        grads_ref[comp] = total
    for hop in range(4):
        for cc in range(2):
            slot = 2 * hop + cc
            copy = z_copy(slot, g, 0, (g, mate), slot)
            if hop > 0:
                copy.wait_send()
            else:
                @pl.when((core != g) | (core != cc))
                def _():
                    copy.wait_send()
    for copy in used:
        copy.wait_send()


def finish_body(next_in, fgrad_in, grads_in, next_out, fgrad_out, ocean_out, atmos_out, flat):
    next_out[0] = next_in[...]
    fgrad_out[0] = fgrad_in[...]
    atmos_factor = 1.0 / math.sqrt(256 * 128)
    for lane in range(3):
        atmos_out[pl.ds(lane, 27, stride=3), :] = grads_in[1, lane, 0:27, :] * atmos_factor
    left = lax.broadcasted_iota(jnp.int32, (14, 128), 1) < 64

    def rows(lane, start):
        return grads_in[0, lane, pl.ds(start, 14, stride=2), :] * (1.0 / 256.0)

    even_0, even_1, odd_0, odd_1 = rows(0, 0), rows(1, 0), rows(0, 1), rows(1, 1)
    odd_0, odd_1 = pltpu.roll(odd_0, 64, 1), pltpu.roll(odd_1, 64, 1)
    flat[pl.ds(0, 14, stride=3), :] = even_0
    flat[pl.ds(1, 14, stride=3), :] = jnp.where(left, even_1, odd_0)
    flat[pl.ds(2, 14, stride=3), :] = jnp.where(left, odd_0, odd_1)
    core = lax.axis_index("lat") % 2

    @pl.when(core == 0)
    def _():
        ocean_out[...] = flat[0:21]

    @pl.when(core == 1)
    def _():
        here = pltpu.roll(flat[20:41], 96, 1)
        after = pltpu.roll(flat[21:42], 96, 1)
        lanes = lax.broadcasted_iota(jnp.int32, (21, 128), 1)
        ocean_out[...] = jnp.where(lanes < 96, here, after)


def local(
    fields, cotangent, ocean_kernels, atmos_kernels, ocean_surface, ocean_coupling,
    atmos_flux, atmos_coupling, row_map, wet_mask,
):
    del row_map
    vmem = pl.BlockSpec(memory_space=pltpu.VMEM)
    hbm = pl.BlockSpec(memory_space=pl.ANY)
    rows4 = pltpu.VMEM((4, COLS, CH), BF16)
    rows2 = pltpu.VMEM((2, COLS, CH), BF16)
    cat4 = pltpu.VMEM((4, COLS, 3 * CH), BF16)
    wide = pltpu.VMEM((2 * COLS, CH), F32)
    small2, small4 = pltpu.VMEM((2, 8, COLS), F32), pltpu.VMEM((4, 8, COLS), F32)

    def buf(*shape):
        return pltpu.VMEM(shape, BF16)

    limits = dict(vmem_limit_bytes=56 * 1024 * 1024)
    next_field, field_grad, grads = pl.pallas_call(
        body,
        out_shape=(
            jax.ShapeDtypeStruct((2, COLS, CH), BF16),
            jax.ShapeDtypeStruct((2, COLS, CH), BF16),
            jax.ShapeDtypeStruct((2, 3, 32, 128), F32),
        ),
        in_specs=[vmem, vmem, hbm, hbm, vmem, vmem, vmem, vmem, vmem],
        out_specs=(vmem, vmem, vmem),
        scratch_shapes=[
            buf(2, 3, 3 * CH, CH), buf(2, 3, 576, 192),
            rows4, rows4, rows4, rows4, rows4, cat4, cat4, cat4, cat4,
            buf(2, COLS, 3 * CH),
            pltpu.VMEM((8, CH), F32), pltpu.VMEM((8, CH), F32), buf(16, CH), buf(16, CH),
            pltpu.VMEM((2, 2, 8, COLS), F32), small4, small2, small4, small2, small2, wide, wide,
            rows2, rows2, rows2, rows2, buf(768, CH), buf(768, 256), buf(3456, 512), buf(1728, 512),
            buf(3, 4, 4 * WIN, 128), buf(3, 2, 2 * WIN, 128), buf(3, 2, 4 * WIN, 128),
            buf(3, 4, WIN, 128), buf(3, 2, WIN // 2, 128), buf(3, 2, WIN, 128),
            pltpu.VMEM((3, 240, 128), F32), buf(8, 3, 32, 128), buf(2, 4, 3, 32, 128),
            pltpu.SemaphoreType.DMA((2,)), pltpu.SemaphoreType.DMA((NSEM,)),
            pltpu.SemaphoreType.DMA((NSEM,)),
        ],
        compiler_params=pltpu.CompilerParams(
            collective_id=0, has_side_effects=True, **limits
        ),
        cost_estimate=pl.CostEstimate(
            flops=4_100_000_000, bytes_accessed=8_000_000, transcendentals=100_000
        ),
    )(
        fields[0], cotangent[0], atmos_kernels.reshape(2, 3, 3 * CH, CH),
        ocean_kernels.reshape(2, 3, 576, 192), ocean_surface.T, ocean_coupling, atmos_flux.T,
        atmos_coupling, wet_mask,
    )
    next_field, field_grad, ocean_rows, atmos_rows = pl.pallas_call(
        finish_body,
        out_shape=(
            jax.ShapeDtypeStruct((1, 2, COLS, CH), BF16),
            jax.ShapeDtypeStruct((1, 2, COLS, CH), BF16),
            jax.ShapeDtypeStruct((21, 128), F32),
            jax.ShapeDtypeStruct((81, 128), F32),
        ),
        in_specs=[vmem, vmem, vmem],
        out_specs=(vmem, vmem, vmem, vmem),
        scratch_shapes=[pltpu.VMEM((48, 128), F32)],
    )(next_field, field_grad, grads)
    return (next_field, field_grad, ocean_rows.reshape(-1)[:2592], atmos_rows.reshape(-1))


def solution(mesh):
    in_specs = (
        P("grp", "lat", None, None),
        P("grp", "lat", None, None),
        P(),
        P(),
        P(),
        P(),
        P(),
        P(),
        P("lat"),
        P("lat", None),
    )
    out_specs = (
        P("grp", "lat", None, None),
        P("grp", "lat", None, None),
        P(("grp", "lat")),
        P(("grp", "lat")),
    )
    return jax.shard_map(local, mesh=mesh, in_specs=in_specs, out_specs=out_specs, check_vma=False)
```

```python
import math

import jax
import jax.numpy as jnp
from jax import lax
from jax.experimental import pallas as pl
from jax.experimental.pallas import tpu as pltpu
from jax.sharding import PartitionSpec as P

MESH = pl.DeviceIdType.MESH
F32 = jnp.float32
BF16 = jnp.bfloat16
GELU_SCALE = 0.7978845608028654
GELU_CUBIC = 0.044715
CH = 384
COLS = 128
WIN = 224
NSEM = 80


def nt_dot(a, b):
    return lax.dot_general(a, b, (((1,), (1,)), ((), ())), preferred_element_type=F32)


def tn_dot(a, b):
    return lax.dot_general(a, b, (((0,), (0,)), ((), ())), preferred_element_type=F32)


def mm(a, b):
    return jnp.dot(a, b, preferred_element_type=F32)


def split_pair(values):
    high = values.astype(BF16).astype(F32)
    return jnp.concatenate([high, values - high], axis=0).astype(BF16)


def body(
    x_ref, g_ref, ak_ref, ok_ref, os_ref, oc_ref, af_ref, ac_ref, wet_ref,
    next_ref, fgrad_ref, grads_ref,
    w, okv, xp, gp, hp, fp, up, gcat, ucat, hcat, fcat, acat,
    m8, c8, m16, c16, wm, wmp, trs, trp, tr2s, tr2r, bh, ig,
    s_a, r_a, s_b, r_b, b6, b6s, at, at2,
    part, rec1, rec2, part2, rec3, rec4, dsum, zsend, zrec,
    wsem, ssem, rsem,
):
    g = lax.axis_index("grp")
    lat = lax.axis_index("lat")
    core = lat % 2
    z = (lat // 2) % 4
    y = (lat // 8) % 4
    x = lat // 32

    def spot(xx, yy, zz, cc):
        return xx * 32 + yy * 8 + zz * 2 + cc

    dn = (lat + 1) % 128
    up_lat = (lat + 127) % 128
    x_plus, x_minus = spot((x + 1) % 4, y, z, core), spot((x + 3) % 4, y, z, core)
    y_plus, y_minus = spot(x, (y + 1) % 4, z, core), spot(x, (y + 3) % 4, z, core)
    mate = lat + 1 - 2 * core
    has_top = jnp.where(lat > 0, 1.0, 0.0).astype(F32)
    has_low = jnp.where(lat < 127, 1.0, 0.0).astype(F32)
    edge = [has_top, None, None, has_low]

    atmos_copy = pltpu.make_async_copy(ak_ref, w, wsem.at[0])
    ocean_copy = pltpu.make_async_copy(ok_ref, okv, wsem.at[1])

    @pl.when(g == 1)
    def _():
        atmos_copy.start()

    @pl.when(g == 0)
    def _():
        ocean_copy.start()

    barrier = pltpu.get_barrier_semaphore()
    partners = [(g, dn), (g, up_lat), (1 - g, dn), (1 - g, up_lat)]
    partners += [(g, other) for other in (x_plus, x_minus, y_plus, y_minus)]
    for step in range(16):
        if step > 0:
            hop = (step // 2) % 4
            partners.append(
                ((g + step // 8) % 2, spot(x, y, (z + hop) % 4, (core + step) % 2))
            )
    for device in partners:
        pl.semaphore_signal(barrier, inc=1, device_id=device, device_id_type=MESH)

    half = CH // 2
    row_id = lax.broadcasted_iota(jnp.int32, (half, CH), 0)
    lane_id = lax.broadcasted_iota(jnp.int32, (half, CH), 1)
    lower = jnp.where(row_id == lane_id, 1.0, 0.0).astype(BF16)
    upper = jnp.where(row_id + half == lane_id, 1.0, 0.0).astype(BF16)
    is_atmos = g.astype(F32)
    is_ocean = 1.0 - is_atmos
    for dst, ocean, atmos in ((m8, os_ref, af_ref), (c8, oc_ref, ac_ref)):
        dst[0:4] = mm(ocean[...], lower) * is_ocean + atmos[...].astype(F32) * is_atmos
        dst[4:8] = mm(ocean[...], upper) * is_ocean
    for dst, src in ((m16, m8), (c16, c8)):
        dst[...] = jnp.concatenate([src[...], src[...]], axis=0).astype(BF16)
    pick_row = lax.broadcasted_iota(jnp.int32, (256, 256), 0)
    pick_lane = lax.broadcasted_iota(jnp.int32, (256, 256), 1)
    pick_lane = jnp.where(pick_lane < COLS, 2 * pick_lane, 2 * pick_lane - 255)
    pick = jnp.where(pick_row == pick_lane, 1.0, 0.0).astype(BF16)
    first_half = lax.broadcasted_iota(jnp.int32, (8, COLS), 0) < 4
    for row in range(2):
        wet = jnp.broadcast_to(wet_ref[row:row + 1, :].astype(F32), (8, 256)).astype(BF16)
        apart = mm(wet, pick)
        even, odd = apart[:, 0:COLS], apart[:, COLS:]
        inverse = 1.0 / jnp.maximum(even + odd, 1.0)
        wm[row, 0] = jnp.where(
            first_half, even * is_ocean + is_atmos, odd * is_ocean
        )
        wm[row, 1] = inverse * is_ocean + is_atmos

    for row in range(2):
        shown = nt_dot(m16[...], x_ref[row])[0:8] * wm[row, 0]
        trs[row] = (shown + pltpu.roll(shown, 4, 0)) * wm[row, 1]
    pl.semaphore_wait(barrier, len(partners))

    used = []

    def arrive(copy):
        copy.wait_recv()

    def send(src, dst, device):
        index = len(used)
        copy = pltpu.make_async_remote_copy(
            src_ref=src, dst_ref=dst, send_sem=ssem.at[index], recv_sem=rsem.at[index],
            device_id=device, device_id_type=MESH,
        )
        copy.start()
        used.append(copy)
        return copy

    t_mid = send(trs, trp.at[pl.ds(1, 2)], (1 - g, lat))
    t_low = send(trs.at[1], trp.at[0], (1 - g, dn))
    t_top = send(trs.at[0], trp.at[3], (1 - g, up_lat))
    m_low = send(wm.at[1, 0], wmp.at[0], (g, dn))
    m_top = send(wm.at[0, 0], wmp.at[3], (g, up_lat))
    x_low = send(x_ref.at[1], xp.at[0], (g, dn))
    x_top = send(x_ref.at[0], xp.at[3], (g, up_lat))
    g_low = send(g_ref.at[1], gp.at[0], (g, dn))
    g_top = send(g_ref.at[0], gp.at[3], (g, up_lat))

    column = lax.broadcasted_iota(jnp.int32, (COLS, CH), 0)

    def put_cat(dst, index, values):
        dst[index, :, CH:2 * CH] = values.astype(BF16)
        dst[index, :, 0:CH] = jnp.where(column > 0, pltpu.roll(values, 1, 0), 0.0).astype(BF16)
        dst[index, :, 2 * CH:3 * CH] = jnp.where(
            column < COLS - 1, pltpu.roll(values, COLS - 1, 0), 0.0
        ).astype(BF16)

    def conv(cat, layer):
        total = None
        for p in range(3):
            term = mm(cat[p:p + 2].reshape(2 * COLS, 3 * CH), w[layer, p])
            total = term if total is None else total + term
        return total

    def back_rows(cat, layer, p, row, count):
        total = None
        for q in range(3):
            rows = cat[row:row + count, :, q * CH:(q + 1) * CH].reshape(count * COLS, CH)
            term = nt_dot(rows, w[layer, 2 - p, (2 - q) * CH:(3 - q) * CH, :])
            total = term if total is None else total + term
        return total

    @pl.when(g == 0)
    def _():
        ocean_copy.wait()
        for layer in range(2):
            for p in range(3):
                low = mm(okv[layer, p], lower)
                high = mm(okv[layer, p], upper)
                none = jnp.zeros((half, CH), F32)
                both = jnp.concatenate([low, none], axis=0) + jnp.concatenate([none, high], axis=0)
                w[layer, p, 0:half, :] = none.astype(BF16)
                w[layer, p, half:5 * half, :] = both.astype(BF16)
                w[layer, p, 5 * half:6 * half, :] = none.astype(BF16)

    @pl.when(g == 1)
    def _():
        atmos_copy.wait()

    for row in range(2):
        put_cat(gcat, row + 1, g_ref[row].astype(F32))
    bh[...] = back_rows(gcat, 1, 1, 1, 2)
    bh[0:COLS] += back_rows(gcat, 1, 2, 2, 1)
    bh[COLS:] += back_rows(gcat, 1, 0, 1, 1)

    def layer_input(index):
        values = xp[index] if index in (0, 3) else x_ref[index - 1]
        mask = wmp[index] if index in (0, 3) else wm[index - 1, 0]
        term = tn_dot(split_pair(mask * trp[index]), c16[...])
        total = (values.astype(F32) + term).astype(BF16).astype(F32)
        if edge[index] is not None:
            total = total * edge[index]
        up[index] = total.astype(BF16)
        put_cat(ucat, index, total)

    arrive(t_mid)
    layer_input(1)
    layer_input(2)
    ig[...] = mm(ucat[1:3].reshape(2 * COLS, 3 * CH), w[0, 1])
    ig[0:COLS] += mm(ucat[2], w[0, 2])
    ig[COLS:] += mm(ucat[1], w[0, 0])
    for copy in (m_low, m_top, t_low, t_top, x_low, x_top):
        arrive(copy)
    layer_input(0)
    layer_input(3)
    ig[0:COLS] += mm(ucat[0], w[0, 0])
    ig[COLS:] += mm(ucat[3], w[0, 2])

    arrive(g_low)
    arrive(g_top)
    top_values = gp[0].astype(F32) * has_top
    low_values = gp[3].astype(F32) * has_low
    gp[0] = top_values.astype(BF16)
    gp[3] = low_values.astype(BF16)
    put_cat(gcat, 0, top_values)
    put_cat(gcat, 3, low_values)

    @pl.when(core == 0)
    def _():
        s_a[0] = gp[0]
        s_a[1] = g_ref[0]

    @pl.when(core == 1)
    def _():
        s_a[...] = up[2:4]

    pair_a = send(s_a, r_a, (g, mate))
    bh[0:COLS] += back_rows(gcat, 1, 0, 0, 1)
    bh[COLS:] += back_rows(gcat, 1, 2, 3, 1)

    zed = ig[...]
    tangent = jnp.tanh(GELU_SCALE * (zed + GELU_CUBIC * zed * zed * zed))
    hidden = (0.5 * zed * (1.0 + tangent)).astype(BF16).reshape(2, COLS, CH)
    slope = 0.5 * (1.0 + tangent) + 0.5 * zed * (1.0 - tangent * tangent) * GELU_SCALE * (
        1.0 + 3.0 * GELU_CUBIC * zed * zed
    )
    first_grad = (bh[...] * slope).astype(BF16).reshape(2, COLS, CH)
    hp[1:3] = hidden
    fp[1:3] = first_grad

    @pl.when(core == 0)
    def _():
        s_b[...] = hp[1:3]

    @pl.when(core == 1)
    def _():
        s_b[...] = fp[1:3]

    pair_b = send(s_b, r_b, (g, mate))
    h_low = send(hp.at[2], hp.at[0], (g, dn))
    h_top = send(hp.at[1], hp.at[3], (g, up_lat))
    f_low = send(fp.at[2], fp.at[0], (g, dn))
    f_top = send(fp.at[1], fp.at[3], (g, up_lat))

    def put_turned(source, places):
        turned = source.astype(F32).T.astype(BF16)

        @pl.when(g == 1)
        def _():
            for block, k in places:
                at[3 * CH * block:3 * CH * (block + 1), k * COLS:(k + 1) * COLS] = turned

        @pl.when(g == 0)
        def _():
            for block, k in places:
                at[576 * block:576 * (block + 1), k * COLS:(k + 1) * COLS] = turned[192:768]
                at2[576 * block:576 * (block + 1), k * COLS:(k + 1) * COLS] = turned[384:960]

    for row in (1, 2):
        put_cat(hcat, row, hp[row].astype(F32))

    arrive(pair_a)

    @pl.when(core == 0)
    def _():
        put_cat(acat, 0, r_a[0].astype(F32))
        put_cat(acat, 1, r_a[1].astype(F32))
        for index in range(6):
            places = [(p, index - p) for p in range(3) if 0 <= index - p <= 3]
            put_turned(ucat[index] if index < 4 else acat[index - 4], places)
        b6[0:256] = fp[1:3].reshape(256, CH)

    @pl.when(core == 1)
    def _():
        for row in (1, 2):
            put_turned(hcat[row], [(0, row + 1)])
        b6[0:256] = r_a[...].reshape(256, CH)
        b6[256:384] = gp[0]
        b6[384:640] = g_ref[...].reshape(256, CH)
        b6[640:768] = gp[3]

    arrive(pair_b)

    @pl.when(core == 0)
    def _():
        b6[256:512] = r_b[...].reshape(256, CH)

    @pl.when(core == 1)
    def _():
        for row in range(2):
            put_cat(acat, row, r_b[row].astype(F32))
            put_turned(acat[row], [(0, row)])

    @pl.when(g == 0)
    def _():
        swap_row = lax.broadcasted_iota(jnp.int32, (CH, 256), 0)
        swap_lane = lax.broadcasted_iota(jnp.int32, (CH, 256), 1)
        swap = jnp.where(swap_row == swap_lane + 192, 1.0, 0.0).astype(BF16)
        b6s[...] = mm(b6[...], swap).astype(BF16)


    ids_x, ids_y = (x, x_plus, x_minus), (y, y_plus, y_minus)
    mixed_a = tuple(a + core * (b - a) for a, b in zip(ids_x, ids_y))
    mixed_b = tuple(b + core * (a - b) for a, b in zip(ids_x, ids_y))
    orders = [(ids_x, ids_y), (ids_y, ids_x), (mixed_a, mixed_b)]

    atmos_pieces = [
        [(0, 0, 0, 224), (208, 1, 0, 80)],
        [(0, 1, 80, 144), (144, 2, 0, 144)],
        [(0, 2, 144, 80), (64, 3, 0, 224)],
    ]
    ocean_pieces = [
        [(0, 0, 0, 112), (96, 1, 0, 48)],
        [(0, 1, 48, 80), (64, 2, 0, 80)],
        [(0, 2, 80, 48), (32, 3, 0, 112)],
    ]

    def gradient_block(xq):
        def place(j, rows):
            m = 3 * xq + j
            start = rows * (m + core * (m % 4 - m))
            return (
                pl.ds(pl.multiple_of(start, 16), rows),
                pl.ds(pl.multiple_of(core * (2 - m // 4) * COLS, 16), 512),
            )

        def store(lane, made, pieces):
            for src, yq, dst, count in pieces:
                if lane == 0:
                    a, b = xq, yq
                elif lane == 1:
                    a, b = yq, xq
                else:
                    a, b = xq + core * (yq - xq), yq + core * (xq - yq)
                rows = pl.ds(pl.multiple_of(b * WIN + dst, 16), count)
                part[lane, a, rows, :] = made[src:src + count]

        @pl.when(g == 1)
        def _():
            for j in range(3):
                left, right = place(j, 288)
                made = mm(at[left, :], b6[right, :]).astype(BF16)
                for lane in range(3):
                    store(lane, made[:, 128 * lane:128 * (lane + 1)], atmos_pieces[j])

        @pl.when(g == 0)
        def _():
            for j in range(3):
                left, right = place(j, 144)
                made = mm(at[left, :], b6[right, 0:256]) + mm(at2[left, :], b6s[right, :])
                made = made.astype(BF16)
                for lane in range(2):
                    store(lane, made[:, 128 * lane:128 * (lane + 1)], ocean_pieces[j])

    def parts_of(rows):
        return pl.ds(0, rows // 2), pl.ds(rows // 2, rows // 2)

    def ring_one(lane, ids, source, near, rows):
        me, plus, minus = ids
        low, high = parts_of(rows)
        across = (me + 2) % 4
        one_p = send(source.at[lane, across, low], near.at[lane, 0], (g, plus))
        one_m = send(source.at[lane, across, high], near.at[lane, 1], (g, minus))
        return one_p, one_m

    def ring_two(lane, ids, source, far, rows, plus_side):
        me, plus, minus = ids
        low, high = parts_of(rows)
        if plus_side:
            return send(source.at[lane, (me + 1) % 4, high], far.at[lane, 0, high], (g, plus))
        return send(source.at[lane, (me + 3) % 4, low], far.at[lane, 1, low], (g, minus))

    def ring_relay(lane, ids, source, near, far, rows, early):
        me, plus, minus = ids
        low, high = parts_of(rows)
        ahead, behind = (me + 1) % 4, (me + 3) % 4
        arrive(early[0])
        source[lane, ahead, low, :] = (
            source[lane, ahead, low, :].astype(F32) + near[lane, 0].astype(F32)
        ).astype(BF16)
        three_p = send(source.at[lane, ahead, low], far.at[lane, 0, low], (g, plus))
        arrive(early[1])
        source[lane, behind, high, :] = (
            source[lane, behind, high, :].astype(F32) + near[lane, 1].astype(F32)
        ).astype(BF16)
        three_m = send(source.at[lane, behind, high], far.at[lane, 1, high], (g, minus))
        return three_p, three_m

    def ring_sum(lane, ids, source, far, late):
        for copy in late:
            arrive(copy)
        me = ids[0]
        return source[lane, me].astype(F32) + far[lane, 0].astype(F32) + far[lane, 1].astype(F32)

    early, middle, late = [None] * 3, [None] * 3, [None] * 3
    early2, middle2, late2 = [None] * 3, [None] * 3, [None] * 3

    def first_two(k):
        middle[k] = tuple(
            ring_two(k, orders[k][0], part, rec2, 4 * WIN, side) for side in (True, False)
        )

    def first_relay(k):
        late[k] = ring_relay(k, orders[k][0], part, rec1, rec2, 4 * WIN, early[k])

    def second_start(k):
        made = ring_sum(k, orders[k][0], part, rec2, middle[k] + late[k])
        part2[k] = made.astype(BF16).reshape(4, WIN, 128)
        early2[k] = ring_one(k, orders[k][1], part2, rec3, WIN)
        middle2[k] = tuple(
            ring_two(k, orders[k][1], part2, rec4, WIN, side) for side in (True, False)
        )

    def second_relay(k):
        late2[k] = ring_relay(k, orders[k][1], part2, rec3, rec4, WIN, early2[k])

    base = 56

    def z_copy(lane, slot, comp, k, device):
        return pltpu.make_async_remote_copy(
            src_ref=zsend.at[lane, slot], dst_ref=zrec.at[comp, k, lane],
            send_sem=ssem.at[base + lane * 8 + slot],
            recv_sem=rsem.at[base + lane * 8 + comp * 4 + k],
            device_id=device, device_id_type=MESH,
        )

    def third_start(k):
        dsum[0:WIN] = ring_sum(k, orders[k][1], part2, rec4, middle2[k] + late2[k])
        dsum[WIN:WIN + 16] = jnp.zeros((16, 128), F32)
        for hop in (2, 1, 3, 0):
            zz = (z + hop) % 4
            place = g * (8 * (y % 2) + 54 * zz) + (1 - g) * ((12 * y) % 16 + 27 * zz)
            for cc in range(2):
                slot = 2 * hop + cc
                zsend[k, slot] = dsum[pl.ds(place + 27 * cc * g, 32), :].astype(BF16)
                copy = z_copy(k, slot, g, (4 - hop) % 4, (core, spot(x, y, zz, cc)))
                if hop > 0:
                    copy.start()
                else:
                    @pl.when((core != g) | (core != cc))
                    def _():
                        copy.start()

    def third_end(k):
        @pl.when(core == g)
        def _():
            zrec[g, 0, k] = zsend[k, core]

        for comp in range(2):
            for source in range(4):
                copy = z_copy(k, 0, comp, source, (g, mate))
                if source > 0:
                    copy.wait_recv()
                else:
                    @pl.when((core != g) | (g != comp))
                    def _():
                        copy.wait_recv()

            total = zrec[comp, 0, k].astype(F32)
            for source in range(1, 4):
                total = total + zrec[comp, source, k].astype(F32)
            grads_ref[comp, k] = total
        for hop in range(4):
            for cc in range(2):
                slot = 2 * hop + cc
                copy = z_copy(k, slot, g, 0, (g, mate))
                if hop > 0:
                    copy.wait_send()
                else:
                    @pl.when((core != g) | (core != cc))
                    def _():
                        copy.wait_send()

    gradient_block((x + 2) % 4)
    early[0] = ring_one(0, orders[0][0], part, rec1, 4 * WIN)
    gradient_block((x + 1) % 4)
    gradient_block((x + 3) % 4)
    gradient_block(x)
    early[1] = ring_one(1, orders[1][0], part, rec1, 4 * WIN)
    first_two(0)
    first_two(1)
    early[2] = ring_one(2, orders[2][0], part, rec1, 4 * WIN)

    arrive(h_low)
    arrive(h_top)
    put_cat(hcat, 0, hp[0].astype(F32) * has_top)
    put_cat(hcat, 3, hp[3].astype(F32) * has_low)
    next_ref[...] = (up[1:3].astype(F32) + conv(hcat, 1).reshape(2, COLS, CH)).astype(BF16)
    first_relay(0)
    first_relay(1)
    first_two(2)

    for row in (1, 2):
        put_cat(fcat, row, fp[row].astype(F32))
    arrive(f_low)
    arrive(f_top)
    put_cat(fcat, 0, fp[0].astype(F32) * has_top)
    put_cat(fcat, 3, fp[3].astype(F32) * has_low)
    total = g_ref[...].reshape(2 * COLS, CH).astype(F32)
    for p in range(3):
        total = total + back_rows(fcat, 0, p, p, 2)
    ig[...] = total

    for row in range(2):
        grad = ig[row * COLS:(row + 1) * COLS, :]
        high = grad.astype(BF16)
        low = (grad - high.astype(F32)).astype(BF16)
        shown = (nt_dot(c16[...], high) + nt_dot(c16[...], low))[0:8] * wm[row, 0]
        tr2s[row] = shown + pltpu.roll(shown, 4, 0)
    back = send(tr2s, tr2r, (1 - g, lat))
    first_relay(2)
    second_start(0)
    second_start(1)
    second_relay(0)
    second_relay(1)
    second_start(2)
    third_start(0)
    third_start(1)
    second_relay(2)
    arrive(back)
    for row in range(2):
        left = split_pair(wm[row, 0] * wm[row, 1] * tr2r[row])
        total = ig[row * COLS:(row + 1) * COLS, :] + tn_dot(left, m16[...])
        fgrad_ref[row] = total.astype(BF16)
    third_start(2)
    assert len(used) <= base
    for k in range(3):
        third_end(k)
    for copy in used:
        copy.wait_send()


def finish_body(next_in, fgrad_in, grads_in, next_out, fgrad_out, ocean_out, atmos_out, flat, sems):
    copies = [
        pltpu.make_async_copy(next_in, next_out.at[0], sems.at[0]),
        pltpu.make_async_copy(fgrad_in, fgrad_out.at[0], sems.at[1]),
    ]
    for copy in copies:
        copy.start()
    atmos_factor = 1.0 / math.sqrt(256 * 128)
    for lane in range(3):
        atmos_out[pl.ds(lane, 27, stride=3), :] = grads_in[1, lane, 0:27, :] * atmos_factor
    left = lax.broadcasted_iota(jnp.int32, (14, 128), 1) < 64

    def rows(lane, start):
        return grads_in[0, lane, pl.ds(start, 14, stride=2), :] * (1.0 / 256.0)

    even_0, even_1, odd_0, odd_1 = rows(0, 0), rows(1, 0), rows(0, 1), rows(1, 1)
    odd_0, odd_1 = pltpu.roll(odd_0, 64, 1), pltpu.roll(odd_1, 64, 1)
    flat[pl.ds(0, 14, stride=3), :] = even_0
    flat[pl.ds(1, 14, stride=3), :] = jnp.where(left, even_1, odd_0)
    flat[pl.ds(2, 14, stride=3), :] = jnp.where(left, odd_0, odd_1)
    core = lax.axis_index("lat") % 2

    @pl.when(core == 0)
    def _():
        ocean_out[...] = flat[0:21]

    @pl.when(core == 1)
    def _():
        here = pltpu.roll(flat[20:41], 96, 1)
        after = pltpu.roll(flat[21:42], 96, 1)
        lanes = lax.broadcasted_iota(jnp.int32, (21, 128), 1)
        ocean_out[...] = jnp.where(lanes < 96, here, after)

    for copy in copies:
        copy.wait()


def local(
    fields, cotangent, ocean_kernels, atmos_kernels, ocean_surface, ocean_coupling,
    atmos_flux, atmos_coupling, row_map, wet_mask,
):
    del row_map
    vmem = pl.BlockSpec(memory_space=pltpu.VMEM)
    hbm = pl.BlockSpec(memory_space=pl.ANY)
    rows4 = pltpu.VMEM((4, COLS, CH), BF16)
    rows2 = pltpu.VMEM((2, COLS, CH), BF16)
    cat4 = pltpu.VMEM((4, COLS, 3 * CH), BF16)
    wide = pltpu.VMEM((2 * COLS, CH), F32)
    small2, small4 = pltpu.VMEM((2, 8, COLS), F32), pltpu.VMEM((4, 8, COLS), F32)

    def buf(*shape):
        return pltpu.VMEM(shape, BF16)

    limits = dict(vmem_limit_bytes=56 * 1024 * 1024)
    next_field, field_grad, grads = pl.pallas_call(
        body,
        out_shape=(
            jax.ShapeDtypeStruct((2, COLS, CH), BF16),
            jax.ShapeDtypeStruct((2, COLS, CH), BF16),
            jax.ShapeDtypeStruct((2, 3, 32, 128), F32),
        ),
        in_specs=[vmem, vmem, hbm, hbm, vmem, vmem, vmem, vmem, vmem],
        out_specs=(vmem, vmem, vmem),
        scratch_shapes=[
            buf(2, 3, 3 * CH, CH), buf(2, 3, 576, 192),
            rows4, rows4, rows4, rows4, rows4, cat4, cat4, cat4, cat4,
            buf(2, COLS, 3 * CH),
            pltpu.VMEM((8, CH), F32), pltpu.VMEM((8, CH), F32), buf(16, CH), buf(16, CH),
            pltpu.VMEM((2, 2, 8, COLS), F32), small4, small2, small4, small2, small2, wide, wide,
            rows2, rows2, rows2, rows2, buf(768, CH), buf(768, 256), buf(3456, 512), buf(1728, 512),
            buf(3, 4, 4 * WIN, 128), buf(3, 2, 2 * WIN, 128), buf(3, 2, 4 * WIN, 128),
            buf(3, 4, WIN, 128), buf(3, 2, WIN // 2, 128), buf(3, 2, WIN, 128),
            pltpu.VMEM((240, 128), F32), buf(3, 8, 32, 128), buf(2, 4, 3, 32, 128),
            pltpu.SemaphoreType.DMA((2,)), pltpu.SemaphoreType.DMA((NSEM,)),
            pltpu.SemaphoreType.DMA((NSEM,)),
        ],
        compiler_params=pltpu.CompilerParams(
            collective_id=0, has_side_effects=True, **limits
        ),
        cost_estimate=pl.CostEstimate(
            flops=4_100_000_000, bytes_accessed=8_000_000, transcendentals=100_000
        ),
    )(
        fields[0], cotangent[0], atmos_kernels.reshape(2, 3, 3 * CH, CH),
        ocean_kernels.reshape(2, 3, 576, 192), ocean_surface.T, ocean_coupling, atmos_flux.T,
        atmos_coupling, wet_mask,
    )
    next_field, field_grad, ocean_rows, atmos_rows = pl.pallas_call(
        finish_body,
        out_shape=(
            jax.ShapeDtypeStruct((1, 2, COLS, CH), BF16),
            jax.ShapeDtypeStruct((1, 2, COLS, CH), BF16),
            jax.ShapeDtypeStruct((21, 128), F32),
            jax.ShapeDtypeStruct((81, 128), F32),
        ),
        in_specs=[hbm, hbm, vmem],
        out_specs=(hbm, hbm, vmem, vmem),
        scratch_shapes=[pltpu.VMEM((48, 128), F32), pltpu.SemaphoreType.DMA((2,))],
    )(next_field, field_grad, grads)
    return (next_field, field_grad, ocean_rows.reshape(-1)[:2592], atmos_rows.reshape(-1))


def solution(mesh):
    in_specs = (
        P("grp", "lat", None, None),
        P("grp", "lat", None, None),
        P(),
        P(),
        P(),
        P(),
        P(),
        P(),
        P("lat"),
        P("lat", None),
    )
    out_specs = (
        P("grp", "lat", None, None),
        P("grp", "lat", None, None),
        P(("grp", "lat")),
        P(("grp", "lat")),
    )
    return jax.shard_map(local, mesh=mesh, in_specs=in_specs, out_specs=out_specs, check_vma=False)
```

```python
import math

import jax
import jax.numpy as jnp
from jax import lax
from jax.experimental import pallas as pl
from jax.experimental.pallas import tpu as pltpu
from jax.sharding import PartitionSpec as P

MESH = pl.DeviceIdType.MESH
F32 = jnp.float32
BF16 = jnp.bfloat16
GELU_SCALE = 0.7978845608028654
GELU_CUBIC = 0.044715
CH = 384
COLS = 128
WIN = 224
NSEM = 80


def nt_dot(a, b):
    return lax.dot_general(a, b, (((1,), (1,)), ((), ())), preferred_element_type=F32)


def tn_dot(a, b):
    return lax.dot_general(a, b, (((0,), (0,)), ((), ())), preferred_element_type=F32)


def mm(a, b):
    return jnp.dot(a, b, preferred_element_type=F32)


def split_pair(values):
    high = values.astype(BF16).astype(F32)
    return jnp.concatenate([high, values - high], axis=0).astype(BF16)


def body(
    x_hbm, g_hbm, ak_ref, ok_ref, os_ref, oc_ref, af_ref, ac_ref, wet_ref,
    next_ref, fgrad_ref, grads_ref,
    x_ref, g_ref, w, okv, xp, gp, hp, fp, up, gcat, ucat, hcat,
    wt, ft, m8, c8, m16, c16, wm, wmp, trs, trp, tr2s, tr2r, bh, ig,
    s_a, r_a, s_b, r_b, b6, b6s, at6,
    part, rec1, rec2, part2, rec3, rec4, dsum, zsend, zrec,
    wsem, ssem, rsem,
):
    g = lax.axis_index("grp")
    lat = lax.axis_index("lat")
    core = lat % 2
    z = (lat // 2) % 4
    y = (lat // 8) % 4
    x = lat // 32

    def spot(xx, yy, zz, cc):
        return xx * 32 + yy * 8 + zz * 2 + cc

    dn = (lat + 1) % 128
    up_lat = (lat + 127) % 128
    x_plus, x_minus = spot((x + 1) % 4, y, z, core), spot((x + 3) % 4, y, z, core)
    y_plus, y_minus = spot(x, (y + 1) % 4, z, core), spot(x, (y + 3) % 4, z, core)
    mate = lat + 1 - 2 * core
    has_top = jnp.where(lat > 0, 1.0, 0.0).astype(F32)
    has_low = jnp.where(lat < 127, 1.0, 0.0).astype(F32)
    edge = [has_top, None, None, has_low]

    x_copy = pltpu.make_async_copy(x_hbm, x_ref, wsem.at[2])
    g_copy = pltpu.make_async_copy(g_hbm, g_ref, wsem.at[3])
    x_copy.start()
    g_copy.start()

    barrier = pltpu.get_barrier_semaphore()
    partners = [(g, dn), (g, up_lat), (1 - g, dn), (1 - g, up_lat)]
    partners += [(g, other) for other in (x_plus, x_minus, y_plus, y_minus)]
    for step in range(16):
        if step > 0:
            hop = (step // 2) % 4
            partners.append(
                ((g + step // 8) % 2, spot(x, y, (z + hop) % 4, (core + step) % 2))
            )
    for device in partners:
        pl.semaphore_signal(barrier, inc=1, device_id=device, device_id_type=MESH)

    atmos_copy = pltpu.make_async_copy(ak_ref, w, wsem.at[0])
    ocean_copy = pltpu.make_async_copy(ok_ref, okv, wsem.at[1])

    @pl.when(g == 1)
    def _():
        atmos_copy.start()

    @pl.when(g == 0)
    def _():
        ocean_copy.start()

    half = CH // 2
    row_id = lax.broadcasted_iota(jnp.int32, (half, CH), 0)
    lane_id = lax.broadcasted_iota(jnp.int32, (half, CH), 1)
    lower = jnp.where(row_id == lane_id, 1.0, 0.0).astype(BF16)
    upper = jnp.where(row_id + half == lane_id, 1.0, 0.0).astype(BF16)
    is_atmos = g.astype(F32)
    is_ocean = 1.0 - is_atmos
    for dst, ocean, atmos in ((m8, os_ref, af_ref), (c8, oc_ref, ac_ref)):
        dst[0:4] = mm(ocean[...], lower) * is_ocean + atmos[...].astype(F32) * is_atmos
        dst[4:8] = mm(ocean[...], upper) * is_ocean
    for dst, src in ((m16, m8), (c16, c8)):
        dst[...] = jnp.concatenate([src[...], src[...]], axis=0).astype(BF16)
    pick_row = lax.broadcasted_iota(jnp.int32, (256, 256), 0)
    pick_lane = lax.broadcasted_iota(jnp.int32, (256, 256), 1)
    pick_lane = jnp.where(pick_lane < COLS, 2 * pick_lane, 2 * pick_lane - 255)
    pick = jnp.where(pick_row == pick_lane, 1.0, 0.0).astype(BF16)
    first_half = lax.broadcasted_iota(jnp.int32, (8, COLS), 0) < 4
    for row in range(2):
        wet = jnp.broadcast_to(wet_ref[row:row + 1, :].astype(F32), (8, 256)).astype(BF16)
        apart = mm(wet, pick)
        even, odd = apart[:, 0:COLS], apart[:, COLS:]
        inverse = 1.0 / jnp.maximum(even + odd, 1.0)
        wm[row, 0] = jnp.where(
            first_half, even * is_ocean + is_atmos, odd * is_ocean
        )
        wm[row, 1] = inverse * is_ocean + is_atmos

    x_copy.wait()
    for row in range(2):
        shown = nt_dot(m16[...], x_ref[row])[0:8] * wm[row, 0]
        trs[row] = (shown + pltpu.roll(shown, 4, 0)) * wm[row, 1]
    g_copy.wait()
    pl.semaphore_wait(barrier, len(partners))

    used = []

    def arrive(copy):
        copy.wait_recv()

    def send(src, dst, device):
        index = len(used)
        copy = pltpu.make_async_remote_copy(
            src_ref=src, dst_ref=dst, send_sem=ssem.at[index], recv_sem=rsem.at[index],
            device_id=device, device_id_type=MESH,
        )
        copy.start()
        used.append(copy)
        return copy

    t_mid = send(trs, trp.at[pl.ds(1, 2)], (1 - g, lat))
    t_low = send(trs.at[1], trp.at[0], (1 - g, dn))
    t_top = send(trs.at[0], trp.at[3], (1 - g, up_lat))
    m_low = send(wm.at[1, 0], wmp.at[0], (g, dn))
    m_top = send(wm.at[0, 0], wmp.at[3], (g, up_lat))
    x_low = send(x_ref.at[1], xp.at[0], (g, dn))
    x_top = send(x_ref.at[0], xp.at[3], (g, up_lat))
    g_low = send(g_ref.at[1], gp.at[0], (g, dn))
    g_top = send(g_ref.at[0], gp.at[3], (g, up_lat))

    column = lax.broadcasted_iota(jnp.int32, (COLS, CH), 0)

    def put_cat(dst, index, values):
        dst[index, :, CH:2 * CH] = values.astype(BF16)
        dst[index, :, 0:CH] = jnp.where(column > 0, pltpu.roll(values, 1, 0), 0.0).astype(BF16)
        dst[index, :, 2 * CH:3 * CH] = jnp.where(
            column < COLS - 1, pltpu.roll(values, COLS - 1, 0), 0.0
        ).astype(BF16)

    def conv(cat, layer):
        total = None
        for p in range(3):
            term = mm(cat[p:p + 2].reshape(2 * COLS, 3 * CH), w[layer, p])
            total = term if total is None else total + term
        return total

    def back_rows(p, row, count):
        return mm(gcat[row:row + count].reshape(count * COLS, 3 * CH), wt[p])

    lane_of = lax.broadcasted_iota(jnp.int32, (CH, COLS), 1)

    def turn(values):
        return values.astype(F32).T

    def lane_shifts(turned):
        earlier = jnp.where(lane_of > 0, pltpu.roll(turned, 1, 1), 0.0)
        later = jnp.where(lane_of < COLS - 1, pltpu.roll(turned, COLS - 1, 1), 0.0)
        return [part.astype(BF16) for part in (earlier, turned, later)]

    def put_turned(index, values):
        at6[index] = jnp.concatenate(lane_shifts(turn(values)), axis=0)

    @pl.when(g == 0)
    def _():
        ocean_copy.wait()
        for layer in range(2):
            for p in range(3):
                low = mm(okv[layer, p], lower)
                high = mm(okv[layer, p], upper)
                none = jnp.zeros((half, CH), F32)
                both = jnp.concatenate([low, none], axis=0) + jnp.concatenate([none, high], axis=0)
                w[layer, p, 0:half, :] = none.astype(BF16)
                w[layer, p, half:5 * half, :] = both.astype(BF16)
                w[layer, p, 5 * half:6 * half, :] = none.astype(BF16)

    @pl.when(g == 1)
    def _():
        atmos_copy.wait()

    for row in range(2):
        put_cat(gcat, row + 1, g_ref[row].astype(F32))
    for p in range(3):
        for q in range(3):
            wt[p, q * CH:(q + 1) * CH, :] = w[1, 2 - p, (2 - q) * CH:(3 - q) * CH, :].T
    bh[...] = back_rows(1, 1, 2)
    bh[0:COLS] += back_rows(2, 2, 1)
    bh[COLS:] += back_rows(0, 1, 1)

    def layer_input(index):
        values = xp[index] if index in (0, 3) else x_ref[index - 1]
        mask = wmp[index] if index in (0, 3) else wm[index - 1, 0]
        term = tn_dot(split_pair(mask * trp[index]), c16[...])
        total = (values.astype(F32) + term).astype(BF16).astype(F32)
        if edge[index] is not None:
            total = total * edge[index]
        up[index] = total.astype(BF16)
        put_cat(ucat, index, total)
        put_turned(index, total)

    arrive(t_mid)
    layer_input(1)
    layer_input(2)
    ig[...] = mm(ucat[1:3].reshape(2 * COLS, 3 * CH), w[0, 1])
    ig[0:COLS] += mm(ucat[2], w[0, 2])
    ig[COLS:] += mm(ucat[1], w[0, 0])
    for copy in (m_low, m_top, t_low, t_top, x_low, x_top):
        arrive(copy)
    layer_input(0)
    layer_input(3)
    ig[0:COLS] += mm(ucat[0], w[0, 0])
    ig[COLS:] += mm(ucat[3], w[0, 2])

    arrive(g_low)
    arrive(g_top)
    top_values = gp[0].astype(F32) * has_top
    low_values = gp[3].astype(F32) * has_low
    gp[0] = top_values.astype(BF16)
    gp[3] = low_values.astype(BF16)
    put_cat(gcat, 0, top_values)
    put_cat(gcat, 3, low_values)

    @pl.when(core == 0)
    def _():
        s_a[0] = gp[0]
        s_a[1] = g_ref[0]

    @pl.when(core == 1)
    def _():
        s_a[...] = up[2:4]

    pair_a = send(s_a, r_a, (g, mate))
    bh[0:COLS] += back_rows(0, 0, 1)
    bh[COLS:] += back_rows(2, 3, 1)

    zed = ig[...]
    tangent = jnp.tanh(GELU_SCALE * (zed + GELU_CUBIC * zed * zed * zed))
    hidden = (0.5 * zed * (1.0 + tangent)).astype(BF16).reshape(2, COLS, CH)
    slope = 0.5 * (1.0 + tangent) + 0.5 * zed * (1.0 - tangent * tangent) * GELU_SCALE * (
        1.0 + 3.0 * GELU_CUBIC * zed * zed
    )
    first_grad = (bh[...] * slope).astype(BF16).reshape(2, COLS, CH)
    hp[1:3] = hidden
    fp[1:3] = first_grad

    @pl.when(core == 0)
    def _():
        s_b[...] = hp[1:3]

    @pl.when(core == 1)
    def _():
        s_b[...] = fp[1:3]

    pair_b = send(s_b, r_b, (g, mate))
    h_low = send(hp.at[2], hp.at[0], (g, dn))
    h_top = send(hp.at[1], hp.at[3], (g, up_lat))
    f_low = send(fp.at[2], fp.at[0], (g, dn))
    f_top = send(fp.at[1], fp.at[3], (g, up_lat))

    for row in (1, 2):
        put_cat(hcat, row, hp[row].astype(F32))

    arrive(pair_a)
    for row in range(2):
        put_turned(4 - 2 * core + row, jnp.where(core == 0, r_a[row], hp[row + 1]))

    @pl.when(core == 0)
    def _():
        b6[0:256] = fp[1:3].reshape(256, CH)

    @pl.when(core == 1)
    def _():
        b6[0:256] = r_a[...].reshape(256, CH)
        b6[256:384] = gp[0]
        b6[384:640] = g_ref[...].reshape(256, CH)
        b6[640:768] = gp[3]

    arrive(pair_b)

    @pl.when(core == 0)
    def _():
        b6[256:512] = r_b[...].reshape(256, CH)

    @pl.when(core == 1)
    def _():
        for row in range(2):
            put_turned(row, r_b[row])

    @pl.when(g == 0)
    def _():
        swap_row = lax.broadcasted_iota(jnp.int32, (CH, 256), 0)
        swap_lane = lax.broadcasted_iota(jnp.int32, (CH, 256), 1)
        swap = jnp.where(swap_row == swap_lane + 192, 1.0, 0.0).astype(BF16)
        b6s[...] = mm(b6[...], swap).astype(BF16)


    ids_x, ids_y = (x, x_plus, x_minus), (y, y_plus, y_minus)
    mixed_a = tuple(a + core * (b - a) for a, b in zip(ids_x, ids_y))
    mixed_b = tuple(b + core * (a - b) for a, b in zip(ids_x, ids_y))
    orders = [(ids_x, ids_y), (ids_y, ids_x), (mixed_a, mixed_b)]

    atmos_pieces = [
        [(0, 0, 0, 224), (208, 1, 0, 80)],
        [(0, 1, 80, 144), (144, 2, 0, 144)],
        [(0, 2, 144, 80), (64, 3, 0, 224)],
    ]
    ocean_pieces = [
        [(0, 0, 0, 112), (96, 1, 0, 48)],
        [(0, 1, 48, 80), (64, 2, 0, 80)],
        [(0, 2, 80, 48), (32, 3, 0, 112)],
    ]

    def gradient_block(xq):
        def operands(j, rows, shift):
            m = 3 * xq + j
            p = m // 4
            left = pl.ds(pl.multiple_of((m % 4) * rows + shift, 16), rows)
            lead = (1 - core) * p
            turned = jnp.concatenate([at6[lead + k, left, :] for k in range(4)], axis=1)
            return turned, pl.ds(pl.multiple_of(core * (2 - p) * COLS, 16), 512)

        def store(lane, made, pieces):
            for src, yq, dst, count in pieces:
                if lane == 0:
                    a, b = xq, yq
                elif lane == 1:
                    a, b = yq, xq
                else:
                    a, b = xq + core * (yq - xq), yq + core * (xq - yq)
                rows = pl.ds(pl.multiple_of(b * WIN + dst, 16), count)
                part[lane, a, rows, :] = made[src:src + count]

        @pl.when(g == 1)
        def _():
            for j in range(3):
                turned, right = operands(j, 288, 0)
                made = mm(turned, b6[right, :]).astype(BF16)
                for lane in range(3):
                    store(lane, made[:, 128 * lane:128 * (lane + 1)], atmos_pieces[j])

        @pl.when(g == 0)
        def _():
            for j in range(3):
                even, right = operands(j, 144, 192)
                odd, _ = operands(j, 144, 384)
                made = mm(even, b6[right, 0:256]) + mm(odd, b6s[right, :])
                made = made.astype(BF16)
                for lane in range(2):
                    store(lane, made[:, 128 * lane:128 * (lane + 1)], ocean_pieces[j])

    def parts_of(rows):
        return pl.ds(0, rows // 2), pl.ds(rows // 2, rows // 2)

    def ring_one(lane, ids, source, near, rows):
        me, plus, minus = ids
        low, high = parts_of(rows)
        across = (me + 2) % 4
        one_p = send(source.at[lane, across, low], near.at[lane, 0], (g, plus))
        one_m = send(source.at[lane, across, high], near.at[lane, 1], (g, minus))
        return one_p, one_m

    def ring_two(lane, ids, source, far, rows, plus_side):
        me, plus, minus = ids
        low, high = parts_of(rows)
        if plus_side:
            return send(source.at[lane, (me + 1) % 4, high], far.at[lane, 0, high], (g, plus))
        return send(source.at[lane, (me + 3) % 4, low], far.at[lane, 1, low], (g, minus))

    def ring_relay(lane, ids, source, near, far, rows, early):
        me, plus, minus = ids
        low, high = parts_of(rows)
        ahead, behind = (me + 1) % 4, (me + 3) % 4
        arrive(early[0])
        source[lane, ahead, low, :] = (
            source[lane, ahead, low, :].astype(F32) + near[lane, 0].astype(F32)
        ).astype(BF16)
        three_p = send(source.at[lane, ahead, low], far.at[lane, 0, low], (g, plus))
        arrive(early[1])
        source[lane, behind, high, :] = (
            source[lane, behind, high, :].astype(F32) + near[lane, 1].astype(F32)
        ).astype(BF16)
        three_m = send(source.at[lane, behind, high], far.at[lane, 1, high], (g, minus))
        return three_p, three_m

    def ring_sum(lane, ids, source, far, late):
        for copy in late:
            arrive(copy)
        me = ids[0]
        return source[lane, me].astype(F32) + far[lane, 0].astype(F32) + far[lane, 1].astype(F32)

    early, middle, late = [None] * 3, [None] * 3, [None] * 3
    early2, middle2, late2 = [None] * 3, [None] * 3, [None] * 3

    def first_two(k):
        middle[k] = tuple(
            ring_two(k, orders[k][0], part, rec2, 4 * WIN, side) for side in (True, False)
        )

    def first_relay(k):
        late[k] = ring_relay(k, orders[k][0], part, rec1, rec2, 4 * WIN, early[k])

    def second_start(k):
        made = ring_sum(k, orders[k][0], part, rec2, middle[k] + late[k])
        part2[k] = made.astype(BF16).reshape(4, WIN, 128)
        early2[k] = ring_one(k, orders[k][1], part2, rec3, WIN)
        middle2[k] = tuple(
            ring_two(k, orders[k][1], part2, rec4, WIN, side) for side in (True, False)
        )

    def second_relay(k):
        late2[k] = ring_relay(k, orders[k][1], part2, rec3, rec4, WIN, early2[k])

    base = 56

    def z_copy(lane, slot, comp, k, device):
        return pltpu.make_async_remote_copy(
            src_ref=zsend.at[lane, slot], dst_ref=zrec.at[comp, k, lane],
            send_sem=ssem.at[base + lane * 8 + slot],
            recv_sem=rsem.at[base + lane * 8 + comp * 4 + k],
            device_id=device, device_id_type=MESH,
        )

    def third_start(k):
        dsum[0:WIN] = ring_sum(k, orders[k][1], part2, rec4, middle2[k] + late2[k])
        dsum[WIN:WIN + 16] = jnp.zeros((16, 128), F32)
        for hop in (2, 1, 3, 0):
            zz = (z + hop) % 4
            place = g * (8 * (y % 2) + 54 * zz) + (1 - g) * ((12 * y) % 16 + 27 * zz)
            for cc in range(2):
                slot = 2 * hop + cc
                zsend[k, slot] = dsum[pl.ds(place + 27 * cc * g, 32), :].astype(BF16)
                copy = z_copy(k, slot, g, (4 - hop) % 4, (core, spot(x, y, zz, cc)))
                if hop > 0:
                    copy.start()
                else:
                    @pl.when((core != g) | (core != cc))
                    def _():
                        copy.start()

    def third_end(k):
        @pl.when(core == g)
        def _():
            zrec[g, 0, k] = zsend[k, core]

        for comp in range(2):
            for source in range(4):
                copy = z_copy(k, 0, comp, source, (g, mate))
                if source > 0:
                    copy.wait_recv()
                else:
                    @pl.when((core != g) | (g != comp))
                    def _():
                        copy.wait_recv()

            total = zrec[comp, 0, k].astype(F32)
            for source in range(1, 4):
                total = total + zrec[comp, source, k].astype(F32)
            grads_ref[comp, k] = total
        for hop in range(4):
            for cc in range(2):
                slot = 2 * hop + cc
                copy = z_copy(k, slot, g, 0, (g, mate))
                if hop > 0:
                    copy.wait_send()
                else:
                    @pl.when((core != g) | (core != cc))
                    def _():
                        copy.wait_send()

    def forward_output():
        h_low.wait_recv()
        h_top.wait_recv()
        put_cat(hcat, 0, hp[0].astype(F32) * has_top)
        put_cat(hcat, 3, hp[3].astype(F32) * has_low)
        next_ref[...] = (up[1:3].astype(F32) + conv(hcat, 1).reshape(2, COLS, CH)).astype(BF16)

    def backward_output():
        f_low.wait_recv()
        f_top.wait_recv()
        for row in range(4):
            values = fp[row].astype(F32)
            if edge[row] is not None:
                values = values * edge[row]
            for q, shifted in enumerate(lane_shifts(turn(values))):
                ft[q, :, row * COLS:(row + 1) * COLS] = shifted
        total = None
        for p in range(3):
            for q in range(3):
                term = mm(
                    w[0, 2 - p, (2 - q) * CH:(3 - q) * CH, :],
                    ft[q, :, p * COLS:(p + 2) * COLS],
                )
                total = term if total is None else total + term
        ig[...] = g_ref[...].reshape(2 * COLS, CH).astype(F32) + total.T
        for row in range(2):
            grad = ig[row * COLS:(row + 1) * COLS, :]
            high = grad.astype(BF16)
            low = (grad - high.astype(F32)).astype(BF16)
            shown = (nt_dot(c16[...], high) + nt_dot(c16[...], low))[0:8] * wm[row, 0]
            tr2s[row] = shown + pltpu.roll(shown, 4, 0)

    gradient_block((x + 2) % 4)
    early[0] = ring_one(0, orders[0][0], part, rec1, 4 * WIN)
    gradient_block((x + 1) % 4)
    gradient_block((x + 3) % 4)
    gradient_block(x)

    for k in (1, 2):
        early[k] = ring_one(k, orders[k][0], part, rec1, 4 * WIN)
    for k in range(3):
        first_two(k)

    forward_output()
    for k in range(3):
        first_relay(k)

    backward_output()
    back = send(tr2s, tr2r, (1 - g, lat))
    for k in range(3):
        second_start(k)
    for k in range(3):
        second_relay(k)
    for k in range(3):
        third_start(k)
    arrive(back)
    for row in range(2):
        left = split_pair(wm[row, 0] * wm[row, 1] * tr2r[row])
        total = ig[row * COLS:(row + 1) * COLS, :] + tn_dot(left, m16[...])
        fgrad_ref[row] = total.astype(BF16)
    assert len(used) <= base
    for k in range(3):
        third_end(k)
    for copy in used:
        copy.wait_send()


def finish_body(next_in, fgrad_in, grads_in, next_out, fgrad_out, ocean_out, atmos_out, flat):
    next_out[0] = next_in[...]
    fgrad_out[0] = fgrad_in[...]
    atmos_factor = 1.0 / math.sqrt(256 * 128)
    for lane in range(3):
        atmos_out[pl.ds(lane, 27, stride=3), :] = grads_in[1, lane, 0:27, :] * atmos_factor
    left = lax.broadcasted_iota(jnp.int32, (14, 128), 1) < 64

    def rows(lane, start):
        return grads_in[0, lane, pl.ds(start, 14, stride=2), :] * (1.0 / 256.0)

    even_0, even_1, odd_0, odd_1 = rows(0, 0), rows(1, 0), rows(0, 1), rows(1, 1)
    odd_0, odd_1 = pltpu.roll(odd_0, 64, 1), pltpu.roll(odd_1, 64, 1)
    flat[pl.ds(0, 14, stride=3), :] = even_0
    flat[pl.ds(1, 14, stride=3), :] = jnp.where(left, even_1, odd_0)
    flat[pl.ds(2, 14, stride=3), :] = jnp.where(left, odd_0, odd_1)
    core = lax.axis_index("lat") % 2

    @pl.when(core == 0)
    def _():
        ocean_out[...] = flat[0:21]

    @pl.when(core == 1)
    def _():
        here = pltpu.roll(flat[20:41], 96, 1)
        after = pltpu.roll(flat[21:42], 96, 1)
        lanes = lax.broadcasted_iota(jnp.int32, (21, 128), 1)
        ocean_out[...] = jnp.where(lanes < 96, here, after)


def local(
    fields, cotangent, ocean_kernels, atmos_kernels, ocean_surface, ocean_coupling,
    atmos_flux, atmos_coupling, row_map, wet_mask,
):
    del row_map
    vmem = pl.BlockSpec(memory_space=pltpu.VMEM)
    hbm = pl.BlockSpec(memory_space=pl.ANY)
    rows4 = pltpu.VMEM((4, COLS, CH), BF16)
    rows2 = pltpu.VMEM((2, COLS, CH), BF16)
    cat4 = pltpu.VMEM((4, COLS, 3 * CH), BF16)
    wide = pltpu.VMEM((2 * COLS, CH), F32)
    small2, small4 = pltpu.VMEM((2, 8, COLS), F32), pltpu.VMEM((4, 8, COLS), F32)

    def buf(*shape):
        return pltpu.VMEM(shape, BF16)

    limits = dict(vmem_limit_bytes=56 * 1024 * 1024)
    next_field, field_grad, grads = pl.pallas_call(
        body,
        out_shape=(
            jax.ShapeDtypeStruct((2, COLS, CH), BF16),
            jax.ShapeDtypeStruct((2, COLS, CH), BF16),
            jax.ShapeDtypeStruct((2, 3, 32, 128), F32),
        ),
        in_specs=[hbm, hbm, hbm, hbm, vmem, vmem, vmem, vmem, vmem],
        out_specs=(vmem, vmem, vmem),
        scratch_shapes=[
            rows2, rows2, buf(2, 3, 3 * CH, CH), buf(2, 3, 576, 192),
            rows4, rows4, rows4, rows4, rows4, cat4, cat4, cat4,
            buf(3, 3 * CH, CH), buf(3, CH, 4 * COLS),
            pltpu.VMEM((8, CH), F32), pltpu.VMEM((8, CH), F32), buf(16, CH), buf(16, CH),
            pltpu.VMEM((2, 2, 8, COLS), F32), small4, small2, small4, small2, small2, wide, wide,
            rows2, rows2, rows2, rows2, buf(768, CH), buf(768, 256), buf(6, 3 * CH, COLS),
            buf(3, 4, 4 * WIN, 128), buf(3, 2, 2 * WIN, 128), buf(3, 2, 4 * WIN, 128),
            buf(3, 4, WIN, 128), buf(3, 2, WIN // 2, 128), buf(3, 2, WIN, 128),
            pltpu.VMEM((240, 128), F32), buf(3, 8, 32, 128), buf(2, 4, 3, 32, 128),
            pltpu.SemaphoreType.DMA((4,)), pltpu.SemaphoreType.DMA((NSEM,)),
            pltpu.SemaphoreType.DMA((NSEM,)),
        ],
        compiler_params=pltpu.CompilerParams(
            collective_id=0, has_side_effects=True, **limits
        ),
        cost_estimate=pl.CostEstimate(
            flops=4_100_000_000, bytes_accessed=8_000_000, transcendentals=100_000
        ),
    )(
        fields[0], cotangent[0], atmos_kernels.reshape(2, 3, 3 * CH, CH),
        ocean_kernels.reshape(2, 3, 576, 192), ocean_surface.T, ocean_coupling, atmos_flux.T,
        atmos_coupling, wet_mask,
    )
    next_field, field_grad, ocean_rows, atmos_rows = pl.pallas_call(
        finish_body,
        out_shape=(
            jax.ShapeDtypeStruct((1, 2, COLS, CH), BF16),
            jax.ShapeDtypeStruct((1, 2, COLS, CH), BF16),
            jax.ShapeDtypeStruct((21, 128), F32),
            jax.ShapeDtypeStruct((81, 128), F32),
        ),
        in_specs=[vmem, vmem, vmem],
        out_specs=(vmem, vmem, vmem, vmem),
        scratch_shapes=[pltpu.VMEM((48, 128), F32)],
    )(next_field, field_grad, grads)
    return (next_field, field_grad, ocean_rows.reshape(-1)[:2592], atmos_rows.reshape(-1))


def solution(mesh):
    in_specs = (
        P("grp", "lat", None, None),
        P("grp", "lat", None, None),
        P(),
        P(),
        P(),
        P(),
        P(),
        P(),
        P("lat"),
        P("lat", None),
    )
    out_specs = (
        P("grp", "lat", None, None),
        P("grp", "lat", None, None),
        P(("grp", "lat")),
        P(("grp", "lat")),
    )
    return jax.shard_map(local, mesh=mesh, in_specs=in_specs, out_specs=out_specs, check_vma=False)
```

```python
import math

import jax
import jax.numpy as jnp
from jax import lax
from jax.experimental import pallas as pl
from jax.experimental.pallas import tpu as pltpu
from jax.sharding import PartitionSpec as P

MESH = pl.DeviceIdType.MESH
F32 = jnp.float32
BF16 = jnp.bfloat16
GELU_SCALE = 0.7978845608028654
GELU_CUBIC = 0.044715
CH = 384
COLS = 128
WIN = 224
NSEM = 80


def nt_dot(a, b):
    return lax.dot_general(a, b, (((1,), (1,)), ((), ())), preferred_element_type=F32)


def tn_dot(a, b):
    return lax.dot_general(a, b, (((0,), (0,)), ((), ())), preferred_element_type=F32)


def mm(a, b):
    return jnp.dot(a, b, preferred_element_type=F32)


def split_pair(values):
    high = values.astype(BF16).astype(F32)
    return jnp.concatenate([high, values - high], axis=0).astype(BF16)


def body(
    x_hbm, g_hbm, ak_ref, ok_ref, os_hbm, oc_hbm, af_hbm, ac_hbm, wet_hbm,
    next_hbm, fgrad_hbm, grads_ref,
    os_ref, oc_ref, af_ref, ac_ref, wet_ref, next_ref, fgrad_ref, x_ref, g_ref, w, okv, xp, gp, hp, fp, up, gcat, ucat, hcat,
    wt, ft, m8, c8, m16, c16, wm, wmp, trs, trp, tr2s, tr2r, bh, ig,
    s_a, r_a, s_b, r_b, b6, b6s, at6,
    part, rec1, rec2, part2, rec5, rec4, dsum, zsend, zrec,
    wsem, ssem, rsem,
):
    g = lax.axis_index("grp")
    lat = lax.axis_index("lat")
    core = lat % 2
    z = (lat // 2) % 4
    y = (lat // 8) % 4
    x = lat // 32

    def spot(xx, yy, zz, cc):
        return xx * 32 + yy * 8 + zz * 2 + cc

    dn = (lat + 1) % 128
    up_lat = (lat + 127) % 128
    x_plus, x_minus = spot((x + 1) % 4, y, z, core), spot((x + 3) % 4, y, z, core)
    y_plus, y_minus = spot(x, (y + 1) % 4, z, core), spot(x, (y + 3) % 4, z, core)
    x_far, y_far = spot((x + 2) % 4, y, z, core), spot(x, (y + 2) % 4, z, core)
    mate = lat + 1 - 2 * core
    has_top = jnp.where(lat > 0, 1.0, 0.0).astype(F32)
    has_low = jnp.where(lat < 127, 1.0, 0.0).astype(F32)
    edge = [has_top, None, None, has_low]

    x_copy = pltpu.make_async_copy(x_hbm, x_ref, wsem.at[2])
    g_copy = pltpu.make_async_copy(g_hbm, g_ref, wsem.at[3])
    maps = [
        pltpu.make_async_copy(src, dst, wsem.at[4 + index])
        for index, (src, dst) in enumerate((
            (os_hbm, os_ref), (oc_hbm, oc_ref), (af_hbm, af_ref), (ac_hbm, ac_ref),
            (wet_hbm, wet_ref),
        ))
    ]
    for copy in (*maps, x_copy, g_copy):
        copy.start()

    barrier = pltpu.get_barrier_semaphore()
    partners = [(g, dn), (g, up_lat), (1 - g, dn), (1 - g, up_lat)]
    partners += [(g, other) for other in (x_plus, x_minus, x_far, y_plus, y_minus, y_far)]
    for step in range(16):
        if step > 0:
            hop = (step // 2) % 4
            partners.append(
                ((g + step // 8) % 2, spot(x, y, (z + hop) % 4, (core + step) % 2))
            )
    for device in partners:
        pl.semaphore_signal(barrier, inc=1, device_id=device, device_id_type=MESH)

    atmos_copy = pltpu.make_async_copy(ak_ref, w, wsem.at[0])
    ocean_copy = pltpu.make_async_copy(ok_ref, okv, wsem.at[1])

    @pl.when(g == 1)
    def _():
        atmos_copy.start()

    @pl.when(g == 0)
    def _():
        ocean_copy.start()

    half = CH // 2
    row_id = lax.broadcasted_iota(jnp.int32, (half, CH), 0)
    lane_id = lax.broadcasted_iota(jnp.int32, (half, CH), 1)
    lower = jnp.where(row_id == lane_id, 1.0, 0.0).astype(BF16)
    upper = jnp.where(row_id + half == lane_id, 1.0, 0.0).astype(BF16)
    for copy in maps:
        copy.wait()
    is_atmos = g.astype(F32)
    is_ocean = 1.0 - is_atmos
    for dst, ocean, atmos in ((m8, os_ref, af_ref), (c8, oc_ref, ac_ref)):
        dst[0:4] = mm(ocean[...], lower) * is_ocean + atmos[...].astype(F32) * is_atmos
        dst[4:8] = mm(ocean[...], upper) * is_ocean
    for dst, src in ((m16, m8), (c16, c8)):
        dst[...] = jnp.concatenate([src[...], src[...]], axis=0).astype(BF16)
    pick_row = lax.broadcasted_iota(jnp.int32, (256, 256), 0)
    pick_lane = lax.broadcasted_iota(jnp.int32, (256, 256), 1)
    pick_lane = jnp.where(pick_lane < COLS, 2 * pick_lane, 2 * pick_lane - 255)
    pick = jnp.where(pick_row == pick_lane, 1.0, 0.0).astype(BF16)
    first_half = lax.broadcasted_iota(jnp.int32, (8, COLS), 0) < 4
    for row in range(2):
        wet = jnp.broadcast_to(wet_ref[row:row + 1, :].astype(F32), (8, 256)).astype(BF16)
        apart = mm(wet, pick)
        even, odd = apart[:, 0:COLS], apart[:, COLS:]
        inverse = 1.0 / jnp.maximum(even + odd, 1.0)
        wm[row, 0] = jnp.where(
            first_half, even * is_ocean + is_atmos, odd * is_ocean
        )
        wm[row, 1] = inverse * is_ocean + is_atmos

    x_copy.wait()
    for row in range(2):
        shown = nt_dot(m16[...], x_ref[row])[0:8] * wm[row, 0]
        trs[row] = (shown + pltpu.roll(shown, 4, 0)) * wm[row, 1]
    g_copy.wait()
    pl.semaphore_wait(barrier, len(partners))

    used = []

    def arrive(copy):
        copy.wait_recv()

    def send(src, dst, device):
        index = len(used)
        copy = pltpu.make_async_remote_copy(
            src_ref=src, dst_ref=dst, send_sem=ssem.at[index], recv_sem=rsem.at[index],
            device_id=device, device_id_type=MESH,
        )
        copy.start()
        used.append(copy)
        return copy

    t_mid = send(trs, trp.at[pl.ds(1, 2)], (1 - g, lat))
    t_low = send(trs.at[1], trp.at[0], (1 - g, dn))
    t_top = send(trs.at[0], trp.at[3], (1 - g, up_lat))
    m_low = send(wm.at[1, 0], wmp.at[0], (g, dn))
    m_top = send(wm.at[0, 0], wmp.at[3], (g, up_lat))
    x_low = send(x_ref.at[1], xp.at[0], (g, dn))
    x_top = send(x_ref.at[0], xp.at[3], (g, up_lat))
    g_low = send(g_ref.at[1], gp.at[0], (g, dn))
    g_top = send(g_ref.at[0], gp.at[3], (g, up_lat))

    column = lax.broadcasted_iota(jnp.int32, (COLS, CH), 0)

    def put_cat(dst, index, values):
        dst[index, :, CH:2 * CH] = values.astype(BF16)
        dst[index, :, 0:CH] = jnp.where(column > 0, pltpu.roll(values, 1, 0), 0.0).astype(BF16)
        dst[index, :, 2 * CH:3 * CH] = jnp.where(
            column < COLS - 1, pltpu.roll(values, COLS - 1, 0), 0.0
        ).astype(BF16)

    def conv(cat, layer):
        total = None
        for p in range(3):
            term = mm(cat[p:p + 2].reshape(2 * COLS, 3 * CH), w[layer, p])
            total = term if total is None else total + term
        return total

    def back_rows(p, row, count):
        return mm(gcat[row:row + count].reshape(count * COLS, 3 * CH), wt[p])

    lane_of = lax.broadcasted_iota(jnp.int32, (CH, COLS), 1)

    def turn(values):
        return values.astype(F32).T

    def lane_shifts(turned):
        earlier = jnp.where(lane_of > 0, pltpu.roll(turned, 1, 1), 0.0)
        later = jnp.where(lane_of < COLS - 1, pltpu.roll(turned, COLS - 1, 1), 0.0)
        return [part.astype(BF16) for part in (earlier, turned, later)]

    def put_turned(index, values):
        at6[index] = jnp.concatenate(lane_shifts(turn(values)), axis=0)

    @pl.when(g == 0)
    def _():
        ocean_copy.wait()
        for layer in range(2):
            for p in range(3):
                low = mm(okv[layer, p], lower)
                high = mm(okv[layer, p], upper)
                none = jnp.zeros((half, CH), F32)
                both = jnp.concatenate([low, none], axis=0) + jnp.concatenate([none, high], axis=0)
                w[layer, p, 0:half, :] = none.astype(BF16)
                w[layer, p, half:5 * half, :] = both.astype(BF16)
                w[layer, p, 5 * half:6 * half, :] = none.astype(BF16)

    @pl.when(g == 1)
    def _():
        atmos_copy.wait()

    for row in range(2):
        put_cat(gcat, row + 1, g_ref[row].astype(F32))
    for p in range(3):
        for q in range(3):
            wt[p, q * CH:(q + 1) * CH, :] = w[1, 2 - p, (2 - q) * CH:(3 - q) * CH, :].T
    bh[...] = back_rows(1, 1, 2)
    bh[0:COLS] += back_rows(2, 2, 1)
    bh[COLS:] += back_rows(0, 1, 1)

    def layer_input(index):
        values = xp[index] if index in (0, 3) else x_ref[index - 1]
        mask = wmp[index] if index in (0, 3) else wm[index - 1, 0]
        term = tn_dot(split_pair(mask * trp[index]), c16[...])
        total = (values.astype(F32) + term).astype(BF16).astype(F32)
        if edge[index] is not None:
            total = total * edge[index]
        up[index] = total.astype(BF16)
        put_cat(ucat, index, total)
        put_turned(index, total)

    arrive(t_mid)
    layer_input(1)
    layer_input(2)
    ig[...] = mm(ucat[1:3].reshape(2 * COLS, 3 * CH), w[0, 1])
    ig[0:COLS] += mm(ucat[2], w[0, 2])
    ig[COLS:] += mm(ucat[1], w[0, 0])
    for copy in (m_low, m_top, t_low, t_top, x_low, x_top):
        arrive(copy)
    layer_input(0)
    layer_input(3)
    ig[0:COLS] += mm(ucat[0], w[0, 0])
    ig[COLS:] += mm(ucat[3], w[0, 2])

    zed = ig[...]
    tangent = jnp.tanh(GELU_SCALE * (zed + GELU_CUBIC * zed * zed * zed))
    hidden = (0.5 * zed * (1.0 + tangent)).astype(BF16).reshape(2, COLS, CH)
    hp[1:3] = hidden
    ig[...] = 0.5 * (1.0 + tangent) + 0.5 * zed * (1.0 - tangent * tangent) * GELU_SCALE * (
        1.0 + 3.0 * GELU_CUBIC * zed * zed
    )

    arrive(g_low)
    arrive(g_top)
    top_values = gp[0].astype(F32) * has_top
    low_values = gp[3].astype(F32) * has_low
    gp[0] = top_values.astype(BF16)
    gp[3] = low_values.astype(BF16)
    put_cat(gcat, 0, top_values)
    put_cat(gcat, 3, low_values)

    @pl.when(core == 0)
    def _():
        s_a[0] = gp[0]
        s_a[1] = g_ref[0]

    @pl.when(core == 1)
    def _():
        s_a[...] = up[2:4]

    pair_a = send(s_a, r_a, (g, mate))
    bh[0:COLS] += back_rows(0, 0, 1)
    bh[COLS:] += back_rows(2, 3, 1)

    first_grad = (bh[...] * ig[...]).astype(BF16).reshape(2, COLS, CH)
    fp[1:3] = first_grad

    @pl.when(core == 0)
    def _():
        s_b[...] = hp[1:3]

    @pl.when(core == 1)
    def _():
        s_b[...] = fp[1:3]

    pair_b = send(s_b, r_b, (g, mate))
    h_low = send(hp.at[2], hp.at[0], (g, dn))
    h_top = send(hp.at[1], hp.at[3], (g, up_lat))
    f_low = send(fp.at[2], fp.at[0], (g, dn))
    f_top = send(fp.at[1], fp.at[3], (g, up_lat))

    arrive(pair_a)
    for row in range(2):
        put_turned(4 - 2 * core + row, jnp.where(core == 0, r_a[row], hp[row + 1]))

    @pl.when(core == 0)
    def _():
        b6[0:256] = fp[1:3].reshape(256, CH)

    @pl.when(core == 1)
    def _():
        b6[0:256] = r_a[...].reshape(256, CH)
        b6[256:384] = gp[0]
        b6[384:640] = g_ref[...].reshape(256, CH)
        b6[640:768] = gp[3]

    arrive(pair_b)

    @pl.when(core == 0)
    def _():
        b6[256:512] = r_b[...].reshape(256, CH)

    @pl.when(core == 1)
    def _():
        for row in range(2):
            put_turned(row, r_b[row])

    @pl.when(g == 0)
    def _():
        swap_row = lax.broadcasted_iota(jnp.int32, (CH, 256), 0)
        swap_lane = lax.broadcasted_iota(jnp.int32, (CH, 256), 1)
        swap = jnp.where(swap_row == swap_lane + 192, 1.0, 0.0).astype(BF16)
        b6s[...] = mm(b6[...], swap).astype(BF16)


    ids_x, ids_y = (x, x_plus, x_minus, x_far), (y, y_plus, y_minus, y_far)
    mixed_a = tuple(a + core * (b - a) for a, b in zip(ids_x, ids_y))
    mixed_b = tuple(b + core * (a - b) for a, b in zip(ids_x, ids_y))
    orders = [(ids_x, ids_y), (ids_y, ids_x), (mixed_a, mixed_b)]

    atmos_pieces = [
        [(0, 0, 0, 224), (208, 1, 0, 80)],
        [(0, 1, 80, 144), (144, 2, 0, 144)],
        [(0, 2, 144, 80), (64, 3, 0, 224)],
    ]
    ocean_pieces = [
        [(0, 0, 0, 112), (96, 1, 0, 48)],
        [(0, 1, 48, 80), (64, 2, 0, 80)],
        [(0, 2, 80, 48), (32, 3, 0, 112)],
    ]

    def gradient_block(xq):
        def operands(j, rows, shift):
            m = 3 * xq + j
            p = m // 4
            left = pl.ds(pl.multiple_of((m % 4) * rows + shift, 16), rows)
            lead = (1 - core) * p
            turned = jnp.concatenate([at6[lead + k, left, :] for k in range(4)], axis=1)
            return turned, pl.ds(pl.multiple_of(core * (2 - p) * COLS, 16), 512)

        def store(lane, made, pieces):
            for src, yq, dst, count in pieces:
                if lane == 0:
                    a, b = xq, yq
                elif lane == 1:
                    a, b = yq, xq
                else:
                    a, b = xq + core * (yq - xq), yq + core * (xq - yq)
                rows = pl.ds(pl.multiple_of(b * WIN + dst, 16), count)
                part[lane, a, rows, :] = made[src:src + count]

        @pl.when(g == 1)
        def _():
            for j in range(3):
                turned, right = operands(j, 288, 0)
                made = mm(turned, b6[right, :]).astype(BF16)
                for lane in range(3):
                    store(lane, made[:, 128 * lane:128 * (lane + 1)], atmos_pieces[j])

        @pl.when(g == 0)
        def _():
            for j in range(3):
                even, right = operands(j, 144, 192)
                odd, _ = operands(j, 144, 384)
                made = mm(even, b6[right, 0:256]) + mm(odd, b6s[right, :])
                made = made.astype(BF16)
                for lane in range(2):
                    store(lane, made[:, 128 * lane:128 * (lane + 1)], ocean_pieces[j])

    def parts_of(rows):
        return pl.ds(0, rows // 2), pl.ds(rows // 2, rows // 2)

    def ring_one(lane, ids, source, near, rows):
        me, plus, minus, far_id = ids
        low, high = parts_of(rows)
        across = (me + 2) % 4
        one_p = send(source.at[lane, across, low], near.at[lane, 0], (g, plus))
        one_m = send(source.at[lane, across, high], near.at[lane, 1], (g, minus))
        return one_p, one_m

    def ring_two(lane, ids, source, far, rows, plus_side):
        me, plus, minus, far_id = ids
        low, high = parts_of(rows)
        if plus_side:
            return send(source.at[lane, (me + 1) % 4, high], far.at[lane, 0, high], (g, plus))
        return send(source.at[lane, (me + 3) % 4, low], far.at[lane, 1, low], (g, minus))

    def direct(lane, ids, source, far, wide, rows):
        me, plus, minus, far_id = ids
        return (
            send(source.at[lane, (me + 2) % 4], wide.at[lane], (g, far_id)),
            send(source.at[lane, (me + 1) % 4], far.at[lane, 0], (g, plus)),
            send(source.at[lane, (me + 3) % 4], far.at[lane, 1], (g, minus)),
        )

    def ring_relay(lane, ids, source, near, far, rows, early):
        me, plus, minus, far_id = ids
        low, high = parts_of(rows)
        ahead, behind = (me + 1) % 4, (me + 3) % 4
        arrive(early[0])
        source[lane, ahead, low, :] = (
            source[lane, ahead, low, :].astype(F32) + near[lane, 0].astype(F32)
        ).astype(BF16)
        three_p = send(source.at[lane, ahead, low], far.at[lane, 0, low], (g, plus))
        arrive(early[1])
        source[lane, behind, high, :] = (
            source[lane, behind, high, :].astype(F32) + near[lane, 1].astype(F32)
        ).astype(BF16)
        three_m = send(source.at[lane, behind, high], far.at[lane, 1, high], (g, minus))
        return three_p, three_m

    def ring_sum(lane, ids, source, far, late):
        for copy in late:
            arrive(copy)
        me = ids[0]
        return source[lane, me].astype(F32) + far[lane, 0].astype(F32) + far[lane, 1].astype(F32)

    early, middle, late = [None] * 3, [None] * 3, [None] * 3
    early2, middle2, late2 = [None] * 3, [None] * 3, [None] * 3

    def first_two(k):
        middle[k] = tuple(
            ring_two(k, orders[k][0], part, rec2, 4 * WIN, side) for side in (True, False)
        )

    def first_relay(k):
        late[k] = ring_relay(k, orders[k][0], part, rec1, rec2, 4 * WIN, early[k])

    def second_start(k):
        made = ring_sum(k, orders[k][0], part, rec2, middle[k] + late[k])
        part2[k] = made.astype(BF16).reshape(4, WIN, 128)
        late2[k] = direct(k, orders[k][1], part2, rec4, rec5, WIN)

    base = 56

    def z_copy(lane, slot, comp, k, device):
        return pltpu.make_async_remote_copy(
            src_ref=zsend.at[lane, slot], dst_ref=zrec.at[comp, k, lane],
            send_sem=ssem.at[base + lane * 8 + slot],
            recv_sem=rsem.at[base + lane * 8 + comp * 4 + k],
            device_id=device, device_id_type=MESH,
        )

    def third_start(k):
        dsum[0:WIN] = ring_sum(k, orders[k][1], part2, rec4, late2[k]) + rec5[k].astype(F32)
        dsum[WIN:WIN + 16] = jnp.zeros((16, 128), F32)
        for hop in (2, 1, 3, 0):
            zz = (z + hop) % 4
            place = g * (8 * (y % 2) + 54 * zz) + (1 - g) * ((12 * y) % 16 + 27 * zz)
            for cc in range(2):
                slot = 2 * hop + cc
                zsend[k, slot] = dsum[pl.ds(place + 27 * cc * g, 32), :].astype(BF16)
                copy = z_copy(k, slot, g, (4 - hop) % 4, (core, spot(x, y, zz, cc)))
                if hop > 0:
                    copy.start()
                else:
                    @pl.when((core != g) | (core != cc))
                    def _():
                        copy.start()

    def third_end(k):
        @pl.when(core == g)
        def _():
            zrec[g, 0, k] = zsend[k, core]

        for comp in range(2):
            for source in range(4):
                copy = z_copy(k, 0, comp, source, (g, mate))
                if source > 0:
                    copy.wait_recv()
                else:
                    @pl.when((core != g) | (g != comp))
                    def _():
                        copy.wait_recv()

            total = zrec[comp, 0, k].astype(F32)
            for source in range(1, 4):
                total = total + zrec[comp, source, k].astype(F32)
            grads_ref[comp, k] = total
        for hop in range(4):
            for cc in range(2):
                slot = 2 * hop + cc
                copy = z_copy(k, slot, g, 0, (g, mate))
                if hop > 0:
                    copy.wait_send()
                else:
                    @pl.when((core != g) | (core != cc))
                    def _():
                        copy.wait_send()

    def forward_output():
        for row in (1, 2):
            put_cat(hcat, row, hp[row].astype(F32))
        h_low.wait_recv()
        h_top.wait_recv()
        put_cat(hcat, 0, hp[0].astype(F32) * has_top)
        put_cat(hcat, 3, hp[3].astype(F32) * has_low)
        next_ref[...] = (up[1:3].astype(F32) + conv(hcat, 1).reshape(2, COLS, CH)).astype(BF16)

    def backward_output():
        f_low.wait_recv()
        f_top.wait_recv()
        for row in range(4):
            values = fp[row].astype(F32)
            if edge[row] is not None:
                values = values * edge[row]
            for q, shifted in enumerate(lane_shifts(turn(values))):
                ft[q, :, row * COLS:(row + 1) * COLS] = shifted
        total = None
        for p in range(3):
            for q in range(3):
                term = mm(
                    w[0, 2 - p, (2 - q) * CH:(3 - q) * CH, :],
                    ft[q, :, p * COLS:(p + 2) * COLS],
                )
                total = term if total is None else total + term
        ig[...] = g_ref[...].reshape(2 * COLS, CH).astype(F32) + total.T
        for row in range(2):
            grad = ig[row * COLS:(row + 1) * COLS, :]
            high = grad.astype(BF16)
            low = (grad - high.astype(F32)).astype(BF16)
            shown = (nt_dot(c16[...], high) + nt_dot(c16[...], low))[0:8] * wm[row, 0]
            tr2s[row] = shown + pltpu.roll(shown, 4, 0)

    gradient_block((x + 2) % 4)
    early[0] = ring_one(0, orders[0][0], part, rec1, 4 * WIN)
    gradient_block((x + 1) % 4)
    gradient_block((x + 3) % 4)
    gradient_block(x)

    for k in (1, 2):
        early[k] = ring_one(k, orders[k][0], part, rec1, 4 * WIN)
    for k in range(3):
        first_two(k)

    forward_output()
    next_copy = pltpu.make_async_copy(next_ref, next_hbm, wsem.at[2])
    next_copy.start()
    for k in range(3):
        first_relay(k)

    backward_output()
    back = send(tr2s, tr2r, (1 - g, lat))
    for k in range(3):
        second_start(k)
    for k in range(3):
        third_start(k)
    arrive(back)
    for row in range(2):
        left = split_pair(wm[row, 0] * wm[row, 1] * tr2r[row])
        total = ig[row * COLS:(row + 1) * COLS, :] + tn_dot(left, m16[...])
        fgrad_ref[row] = total.astype(BF16)
    fgrad_copy = pltpu.make_async_copy(fgrad_ref, fgrad_hbm, wsem.at[3])
    fgrad_copy.start()
    assert len(used) <= base
    for k in range(3):
        third_end(k)
    next_copy.wait()
    fgrad_copy.wait()
    for copy in used:
        copy.wait_send()


def finish_body(next_in, fgrad_in, grads_in, next_out, fgrad_out, ocean_out, atmos_out, flat):
    next_out[0] = next_in[...]
    fgrad_out[0] = fgrad_in[...]
    atmos_factor = 1.0 / math.sqrt(256 * 128)
    for lane in range(3):
        atmos_out[pl.ds(lane, 27, stride=3), :] = grads_in[1, lane, 0:27, :] * atmos_factor
    left = lax.broadcasted_iota(jnp.int32, (14, 128), 1) < 64

    def rows(lane, start):
        return grads_in[0, lane, pl.ds(start, 14, stride=2), :] * (1.0 / 256.0)

    even_0, even_1, odd_0, odd_1 = rows(0, 0), rows(1, 0), rows(0, 1), rows(1, 1)
    odd_0, odd_1 = pltpu.roll(odd_0, 64, 1), pltpu.roll(odd_1, 64, 1)
    flat[pl.ds(0, 14, stride=3), :] = even_0
    flat[pl.ds(1, 14, stride=3), :] = jnp.where(left, even_1, odd_0)
    flat[pl.ds(2, 14, stride=3), :] = jnp.where(left, odd_0, odd_1)
    core = lax.axis_index("lat") % 2

    @pl.when(core == 0)
    def _():
        ocean_out[...] = flat[0:21]

    @pl.when(core == 1)
    def _():
        here = pltpu.roll(flat[20:41], 96, 1)
        after = pltpu.roll(flat[21:42], 96, 1)
        lanes = lax.broadcasted_iota(jnp.int32, (21, 128), 1)
        ocean_out[...] = jnp.where(lanes < 96, here, after)


def local(
    fields, cotangent, ocean_kernels, atmos_kernels, ocean_surface, ocean_coupling,
    atmos_flux, atmos_coupling, row_map, wet_mask,
):
    del row_map
    vmem = pl.BlockSpec(memory_space=pltpu.VMEM)
    hbm = pl.BlockSpec(memory_space=pl.ANY)
    rows4 = pltpu.VMEM((4, COLS, CH), BF16)
    rows2 = pltpu.VMEM((2, COLS, CH), BF16)
    cat4 = pltpu.VMEM((4, COLS, 3 * CH), BF16)
    wide = pltpu.VMEM((2 * COLS, CH), F32)
    small2, small4 = pltpu.VMEM((2, 8, COLS), F32), pltpu.VMEM((4, 8, COLS), F32)

    def buf(*shape):
        return pltpu.VMEM(shape, BF16)

    limits = dict(vmem_limit_bytes=56 * 1024 * 1024)
    next_field, field_grad, grads = pl.pallas_call(
        body,
        out_shape=(
            jax.ShapeDtypeStruct((2, COLS, CH), BF16),
            jax.ShapeDtypeStruct((2, COLS, CH), BF16),
            jax.ShapeDtypeStruct((2, 3, 32, 128), F32),
        ),
        in_specs=[hbm] * 9,
        out_specs=(hbm, hbm, vmem),
        scratch_shapes=[
            buf(4, 192), buf(4, 192), buf(4, CH), buf(4, CH), pltpu.VMEM((2, 256), jnp.int32),
            rows2, rows2, rows2, rows2, buf(2, 3, 3 * CH, CH), buf(2, 3, 576, 192),
            rows4, rows4, rows4, rows4, rows4, cat4, cat4, cat4,
            buf(3, 3 * CH, CH), buf(3, CH, 4 * COLS),
            pltpu.VMEM((8, CH), F32), pltpu.VMEM((8, CH), F32), buf(16, CH), buf(16, CH),
            pltpu.VMEM((2, 2, 8, COLS), F32), small4, small2, small4, small2, small2, wide, wide,
            rows2, rows2, rows2, rows2, buf(768, CH), buf(768, 256), buf(6, 3 * CH, COLS),
            buf(3, 4, 4 * WIN, 128), buf(3, 2, 2 * WIN, 128), buf(3, 2, 4 * WIN, 128),
            buf(3, 4, WIN, 128), buf(3, WIN, 128), buf(3, 2, WIN, 128),
            pltpu.VMEM((240, 128), F32), buf(3, 8, 32, 128), buf(2, 4, 3, 32, 128),
            pltpu.SemaphoreType.DMA((9,)), pltpu.SemaphoreType.DMA((NSEM,)),
            pltpu.SemaphoreType.DMA((NSEM,)),
        ],
        compiler_params=pltpu.CompilerParams(
            collective_id=0, has_side_effects=True, **limits
        ),
        cost_estimate=pl.CostEstimate(
            flops=4_100_000_000, bytes_accessed=8_000_000, transcendentals=100_000
        ),
    )(
        fields[0], cotangent[0], atmos_kernels.reshape(2, 3, 3 * CH, CH),
        ocean_kernels.reshape(2, 3, 576, 192), ocean_surface.T, ocean_coupling, atmos_flux.T,
        atmos_coupling, wet_mask,
    )
    next_field, field_grad, ocean_rows, atmos_rows = pl.pallas_call(
        finish_body,
        out_shape=(
            jax.ShapeDtypeStruct((1, 2, COLS, CH), BF16),
            jax.ShapeDtypeStruct((1, 2, COLS, CH), BF16),
            jax.ShapeDtypeStruct((21, 128), F32),
            jax.ShapeDtypeStruct((81, 128), F32),
        ),
        in_specs=[vmem, vmem, vmem],
        out_specs=(vmem, vmem, vmem, vmem),
        scratch_shapes=[pltpu.VMEM((48, 128), F32)],
    )(next_field, field_grad, grads)
    return (next_field, field_grad, ocean_rows.reshape(-1)[:2592], atmos_rows.reshape(-1))


def solution(mesh):
    in_specs = (
        P("grp", "lat", None, None),
        P("grp", "lat", None, None),
        P(),
        P(),
        P(),
        P(),
        P(),
        P(),
        P("lat"),
        P("lat", None),
    )
    out_specs = (
        P("grp", "lat", None, None),
        P("grp", "lat", None, None),
        P(("grp", "lat")),
        P(("grp", "lat")),
    )
    return jax.shard_map(local, mesh=mesh, in_specs=in_specs, out_specs=out_specs, check_vma=False)
```

```python
import math

import jax
import jax.numpy as jnp
from jax import lax
from jax.experimental import pallas as pl
from jax.experimental.pallas import tpu as pltpu
from jax.sharding import PartitionSpec as P

MESH = pl.DeviceIdType.MESH
F32 = jnp.float32
BF16 = jnp.bfloat16
GELU_SCALE = 0.7978845608028654
GELU_CUBIC = 0.044715
CH = 384
COLS = 128
WIN = 224
NSEM = 80


def nt_dot(a, b):
    return lax.dot_general(a, b, (((1,), (1,)), ((), ())), preferred_element_type=F32)


def tn_dot(a, b):
    return lax.dot_general(a, b, (((0,), (0,)), ((), ())), preferred_element_type=F32)


def mm(a, b):
    return jnp.dot(a, b, preferred_element_type=F32)


def split_pair(values):
    high = values.astype(BF16).astype(F32)
    return jnp.concatenate([high, values - high], axis=0).astype(BF16)


def body(
    x_hbm, g_hbm, ak_ref, ok_ref, os_hbm, oc_hbm, af_hbm, ac_hbm, wet_hbm,
    next_ref, fgrad_ref, grads_ref,
    os_ref, oc_ref, af_ref, ac_ref, wet_ref, x_ref, g_ref, w, okv, xp, gp, hp, fp, up, gcat, ucat, hcat,
    wt, ft, m8, c8, m16, c16, wm, wmp, trs, trp, tr2s, tr2r, bh, ig,
    s_a, r_a, s_b, r_b, b6, b6s, at6,
    part, rec1, rec2, part2, rec5, rec4, dsum, zsend, zrec,
    wsem, ssem, rsem,
):
    g = lax.axis_index("grp")
    lat = lax.axis_index("lat")
    core = lat % 2
    z = (lat // 2) % 4
    y = (lat // 8) % 4
    x = lat // 32

    def spot(xx, yy, zz, cc):
        return xx * 32 + yy * 8 + zz * 2 + cc

    dn = (lat + 1) % 128
    up_lat = (lat + 127) % 128
    x_plus, x_minus = spot((x + 1) % 4, y, z, core), spot((x + 3) % 4, y, z, core)
    y_plus, y_minus = spot(x, (y + 1) % 4, z, core), spot(x, (y + 3) % 4, z, core)
    x_far, y_far = spot((x + 2) % 4, y, z, core), spot(x, (y + 2) % 4, z, core)
    mate = lat + 1 - 2 * core
    has_top = jnp.where(lat > 0, 1.0, 0.0).astype(F32)
    has_low = jnp.where(lat < 127, 1.0, 0.0).astype(F32)
    edge = [has_top, None, None, has_low]

    x_copy = pltpu.make_async_copy(x_hbm, x_ref, wsem.at[2])
    g_copy = pltpu.make_async_copy(g_hbm, g_ref, wsem.at[3])
    maps = [
        pltpu.make_async_copy(src, dst, wsem.at[4 + index])
        for index, (src, dst) in enumerate((
            (os_hbm, os_ref), (oc_hbm, oc_ref), (af_hbm, af_ref), (ac_hbm, ac_ref),
            (wet_hbm, wet_ref),
        ))
    ]
    for copy in (*maps, x_copy, g_copy):
        copy.start()

    barrier = pltpu.get_barrier_semaphore()
    partners = [(g, dn), (g, up_lat), (1 - g, dn), (1 - g, up_lat)]
    partners += [(g, other) for other in (x_plus, x_minus, x_far, y_plus, y_minus, y_far)]
    for step in range(16):
        if step > 0:
            hop = (step // 2) % 4
            partners.append(
                ((g + step // 8) % 2, spot(x, y, (z + hop) % 4, (core + step) % 2))
            )
    for device in partners:
        pl.semaphore_signal(barrier, inc=1, device_id=device, device_id_type=MESH)

    atmos_copy = pltpu.make_async_copy(ak_ref, w, wsem.at[0])
    ocean_copy = pltpu.make_async_copy(ok_ref, okv, wsem.at[1])

    @pl.when(g == 1)
    def _():
        atmos_copy.start()

    @pl.when(g == 0)
    def _():
        ocean_copy.start()

    half = CH // 2
    row_id = lax.broadcasted_iota(jnp.int32, (half, CH), 0)
    lane_id = lax.broadcasted_iota(jnp.int32, (half, CH), 1)
    lower = jnp.where(row_id == lane_id, 1.0, 0.0).astype(BF16)
    upper = jnp.where(row_id + half == lane_id, 1.0, 0.0).astype(BF16)
    for copy in maps:
        copy.wait()
    is_atmos = g.astype(F32)
    is_ocean = 1.0 - is_atmos
    for dst, ocean, atmos in ((m8, os_ref, af_ref), (c8, oc_ref, ac_ref)):
        dst[0:4] = mm(ocean[...], lower) * is_ocean + atmos[...].astype(F32) * is_atmos
        dst[4:8] = mm(ocean[...], upper) * is_ocean
    for dst, src in ((m16, m8), (c16, c8)):
        dst[...] = jnp.concatenate([src[...], src[...]], axis=0).astype(BF16)
    pick_row = lax.broadcasted_iota(jnp.int32, (256, 256), 0)
    pick_lane = lax.broadcasted_iota(jnp.int32, (256, 256), 1)
    pick_lane = jnp.where(pick_lane < COLS, 2 * pick_lane, 2 * pick_lane - 255)
    pick = jnp.where(pick_row == pick_lane, 1.0, 0.0).astype(BF16)
    first_half = lax.broadcasted_iota(jnp.int32, (8, COLS), 0) < 4
    for row in range(2):
        wet = jnp.broadcast_to(wet_ref[row:row + 1, :].astype(F32), (8, 256)).astype(BF16)
        apart = mm(wet, pick)
        even, odd = apart[:, 0:COLS], apart[:, COLS:]
        inverse = 1.0 / jnp.maximum(even + odd, 1.0)
        wm[row, 0] = jnp.where(
            first_half, even * is_ocean + is_atmos, odd * is_ocean
        )
        wm[row, 1] = inverse * is_ocean + is_atmos

    x_copy.wait()
    for row in range(2):
        shown = nt_dot(m16[...], x_ref[row])[0:8] * wm[row, 0]
        trs[row] = (shown + pltpu.roll(shown, 4, 0)) * wm[row, 1]
    g_copy.wait()
    pl.semaphore_wait(barrier, len(partners))

    used = []

    def arrive(copy):
        copy.wait_recv()

    def send(src, dst, device):
        index = len(used)
        copy = pltpu.make_async_remote_copy(
            src_ref=src, dst_ref=dst, send_sem=ssem.at[index], recv_sem=rsem.at[index],
            device_id=device, device_id_type=MESH,
        )
        copy.start()
        used.append(copy)
        return copy

    t_mid = send(trs, trp.at[pl.ds(1, 2)], (1 - g, lat))
    t_low = send(trs.at[1], trp.at[0], (1 - g, dn))
    t_top = send(trs.at[0], trp.at[3], (1 - g, up_lat))
    m_low = send(wm.at[1, 0], wmp.at[0], (g, dn))
    m_top = send(wm.at[0, 0], wmp.at[3], (g, up_lat))
    x_low = send(x_ref.at[1], xp.at[0], (g, dn))
    x_top = send(x_ref.at[0], xp.at[3], (g, up_lat))
    g_low = send(g_ref.at[1], gp.at[0], (g, dn))
    g_top = send(g_ref.at[0], gp.at[3], (g, up_lat))

    column = lax.broadcasted_iota(jnp.int32, (COLS, CH), 0)

    def put_cat(dst, index, values):
        dst[index, :, CH:2 * CH] = values.astype(BF16)
        dst[index, :, 0:CH] = jnp.where(column > 0, pltpu.roll(values, 1, 0), 0.0).astype(BF16)
        dst[index, :, 2 * CH:3 * CH] = jnp.where(
            column < COLS - 1, pltpu.roll(values, COLS - 1, 0), 0.0
        ).astype(BF16)

    def conv(cat, layer):
        total = None
        for p in range(3):
            term = mm(cat[p:p + 2].reshape(2 * COLS, 3 * CH), w[layer, p])
            total = term if total is None else total + term
        return total

    def back_rows(p, row, count):
        return mm(gcat[row:row + count].reshape(count * COLS, 3 * CH), wt[p])

    lane_of = lax.broadcasted_iota(jnp.int32, (CH, COLS), 1)

    def turn(values):
        return values.astype(F32).T

    def lane_shifts(turned):
        earlier = jnp.where(lane_of > 0, pltpu.roll(turned, 1, 1), 0.0)
        later = jnp.where(lane_of < COLS - 1, pltpu.roll(turned, COLS - 1, 1), 0.0)
        return [part.astype(BF16) for part in (earlier, turned, later)]

    def put_turned(index, values):
        at6[index] = jnp.concatenate(lane_shifts(turn(values)), axis=0)

    @pl.when(g == 0)
    def _():
        ocean_copy.wait()
        for layer in range(2):
            for p in range(3):
                low = mm(okv[layer, p], lower)
                high = mm(okv[layer, p], upper)
                none = jnp.zeros((half, CH), F32)
                both = jnp.concatenate([low, none], axis=0) + jnp.concatenate([none, high], axis=0)
                w[layer, p, 0:half, :] = none.astype(BF16)
                w[layer, p, half:5 * half, :] = both.astype(BF16)
                w[layer, p, 5 * half:6 * half, :] = none.astype(BF16)

    @pl.when(g == 1)
    def _():
        atmos_copy.wait()

    for row in range(2):
        put_cat(gcat, row + 1, g_ref[row].astype(F32))
    for p in range(3):
        for q in range(3):
            wt[p, q * CH:(q + 1) * CH, :] = w[1, 2 - p, (2 - q) * CH:(3 - q) * CH, :].T
    bh[...] = back_rows(1, 1, 2)
    bh[0:COLS] += back_rows(2, 2, 1)
    bh[COLS:] += back_rows(0, 1, 1)

    def layer_input(index):
        values = xp[index] if index in (0, 3) else x_ref[index - 1]
        mask = wmp[index] if index in (0, 3) else wm[index - 1, 0]
        term = tn_dot(split_pair(mask * trp[index]), c16[...])
        total = (values.astype(F32) + term).astype(BF16).astype(F32)
        if edge[index] is not None:
            total = total * edge[index]
        up[index] = total.astype(BF16)
        put_cat(ucat, index, total)
        put_turned(index, total)

    arrive(t_mid)
    layer_input(1)
    layer_input(2)
    ig[...] = mm(ucat[1:3].reshape(2 * COLS, 3 * CH), w[0, 1])
    ig[0:COLS] += mm(ucat[2], w[0, 2])
    ig[COLS:] += mm(ucat[1], w[0, 0])
    for copy in (m_low, m_top, t_low, t_top, x_low, x_top):
        arrive(copy)
    layer_input(0)
    layer_input(3)
    ig[0:COLS] += mm(ucat[0], w[0, 0])
    ig[COLS:] += mm(ucat[3], w[0, 2])

    zed = ig[...]
    tangent = jnp.tanh(GELU_SCALE * (zed + GELU_CUBIC * zed * zed * zed))
    hidden = (0.5 * zed * (1.0 + tangent)).astype(BF16).reshape(2, COLS, CH)
    hp[1:3] = hidden
    ig[...] = 0.5 * (1.0 + tangent) + 0.5 * zed * (1.0 - tangent * tangent) * GELU_SCALE * (
        1.0 + 3.0 * GELU_CUBIC * zed * zed
    )

    arrive(g_low)
    arrive(g_top)
    top_values = gp[0].astype(F32) * has_top
    low_values = gp[3].astype(F32) * has_low
    gp[0] = top_values.astype(BF16)
    gp[3] = low_values.astype(BF16)
    put_cat(gcat, 0, top_values)
    put_cat(gcat, 3, low_values)

    @pl.when(core == 0)
    def _():
        s_a[0] = gp[0]
        s_a[1] = g_ref[0]

    @pl.when(core == 1)
    def _():
        s_a[...] = up[2:4]

    pair_a = send(s_a, r_a, (g, mate))
    bh[0:COLS] += back_rows(0, 0, 1)
    bh[COLS:] += back_rows(2, 3, 1)

    first_grad = (bh[...] * ig[...]).astype(BF16).reshape(2, COLS, CH)
    fp[1:3] = first_grad

    @pl.when(core == 0)
    def _():
        s_b[...] = hp[1:3]

    @pl.when(core == 1)
    def _():
        s_b[...] = fp[1:3]

    pair_b = send(s_b, r_b, (g, mate))
    h_low = send(hp.at[2], hp.at[0], (g, dn))
    h_top = send(hp.at[1], hp.at[3], (g, up_lat))
    f_low = send(fp.at[2], fp.at[0], (g, dn))
    f_top = send(fp.at[1], fp.at[3], (g, up_lat))

    arrive(pair_a)
    for row in range(2):
        put_turned(4 - 2 * core + row, jnp.where(core == 0, r_a[row], hp[row + 1]))

    @pl.when(core == 0)
    def _():
        b6[0:256] = fp[1:3].reshape(256, CH)

    @pl.when(core == 1)
    def _():
        b6[0:256] = r_a[...].reshape(256, CH)
        b6[256:384] = gp[0]
        b6[384:640] = g_ref[...].reshape(256, CH)
        b6[640:768] = gp[3]

    arrive(pair_b)

    @pl.when(core == 0)
    def _():
        b6[256:512] = r_b[...].reshape(256, CH)

    @pl.when(core == 1)
    def _():
        for row in range(2):
            put_turned(row, r_b[row])

    @pl.when(g == 0)
    def _():
        swap_row = lax.broadcasted_iota(jnp.int32, (CH, 256), 0)
        swap_lane = lax.broadcasted_iota(jnp.int32, (CH, 256), 1)
        swap = jnp.where(swap_row == swap_lane + 192, 1.0, 0.0).astype(BF16)
        b6s[...] = mm(b6[...], swap).astype(BF16)


    ids_x, ids_y = (x, x_plus, x_minus, x_far), (y, y_plus, y_minus, y_far)
    mixed_a = tuple(a + core * (b - a) for a, b in zip(ids_x, ids_y))
    mixed_b = tuple(b + core * (a - b) for a, b in zip(ids_x, ids_y))
    orders = [(ids_x, ids_y), (ids_y, ids_x), (mixed_a, mixed_b)]

    atmos_pieces = [
        [(0, 0, 0, 224), (208, 1, 0, 80)],
        [(0, 1, 80, 144), (144, 2, 0, 144)],
        [(0, 2, 144, 80), (64, 3, 0, 224)],
    ]
    ocean_pieces = [
        [(0, 0, 0, 112), (96, 1, 0, 48)],
        [(0, 1, 48, 80), (64, 2, 0, 80)],
        [(0, 2, 80, 48), (32, 3, 0, 112)],
    ]

    def gradient_block(xq):
        def operands(j, rows, shift):
            m = 3 * xq + j
            p = m // 4
            left = pl.ds(pl.multiple_of((m % 4) * rows + shift, 16), rows)
            lead = (1 - core) * p
            turned = jnp.concatenate([at6[lead + k, left, :] for k in range(4)], axis=1)
            return turned, pl.ds(pl.multiple_of(core * (2 - p) * COLS, 16), 512)

        def store(lane, made, pieces):
            for src, yq, dst, count in pieces:
                if lane == 0:
                    a, b = xq, yq
                elif lane == 1:
                    a, b = yq, xq
                else:
                    a, b = xq + core * (yq - xq), yq + core * (xq - yq)
                rows = pl.ds(pl.multiple_of(b * WIN + dst, 16), count)
                part[lane, a, rows, :] = made[src:src + count]

        @pl.when(g == 1)
        def _():
            for j in range(3):
                turned, right = operands(j, 288, 0)
                made = mm(turned, b6[right, :]).astype(BF16)
                for lane in range(3):
                    store(lane, made[:, 128 * lane:128 * (lane + 1)], atmos_pieces[j])

        @pl.when(g == 0)
        def _():
            for j in range(3):
                even, right = operands(j, 144, 192)
                odd, _ = operands(j, 144, 384)
                made = mm(even, b6[right, 0:256]) + mm(odd, b6s[right, :])
                made = made.astype(BF16)
                for lane in range(2):
                    store(lane, made[:, 128 * lane:128 * (lane + 1)], ocean_pieces[j])

    def parts_of(rows):
        return pl.ds(0, rows // 2), pl.ds(rows // 2, rows // 2)

    def ring_one(lane, ids, source, near, rows):
        me, plus, minus, far_id = ids
        low, high = parts_of(rows)
        across = (me + 2) % 4
        one_p = send(source.at[lane, across, low], near.at[lane, 0], (g, plus))
        one_m = send(source.at[lane, across, high], near.at[lane, 1], (g, minus))
        return one_p, one_m

    def ring_two(lane, ids, source, far, rows, plus_side):
        me, plus, minus, far_id = ids
        low, high = parts_of(rows)
        if plus_side:
            return send(source.at[lane, (me + 1) % 4, high], far.at[lane, 0, high], (g, plus))
        return send(source.at[lane, (me + 3) % 4, low], far.at[lane, 1, low], (g, minus))

    def direct(lane, ids, source, far, wide, rows):
        me, plus, minus, far_id = ids
        return (
            send(source.at[lane, (me + 2) % 4], wide.at[lane], (g, far_id)),
            send(source.at[lane, (me + 1) % 4], far.at[lane, 0], (g, plus)),
            send(source.at[lane, (me + 3) % 4], far.at[lane, 1], (g, minus)),
        )

    def ring_relay(lane, ids, source, near, far, rows, early):
        me, plus, minus, far_id = ids
        low, high = parts_of(rows)
        ahead, behind = (me + 1) % 4, (me + 3) % 4
        arrive(early[0])
        source[lane, ahead, low, :] = (
            source[lane, ahead, low, :].astype(F32) + near[lane, 0].astype(F32)
        ).astype(BF16)
        three_p = send(source.at[lane, ahead, low], far.at[lane, 0, low], (g, plus))
        arrive(early[1])
        source[lane, behind, high, :] = (
            source[lane, behind, high, :].astype(F32) + near[lane, 1].astype(F32)
        ).astype(BF16)
        three_m = send(source.at[lane, behind, high], far.at[lane, 1, high], (g, minus))
        return three_p, three_m

    def ring_sum(lane, ids, source, far, late):
        for copy in late:
            arrive(copy)
        me = ids[0]
        return source[lane, me].astype(F32) + far[lane, 0].astype(F32) + far[lane, 1].astype(F32)

    early, middle, late = [None] * 3, [None] * 3, [None] * 3
    early2, middle2, late2 = [None] * 3, [None] * 3, [None] * 3

    def first_two(k):
        middle[k] = tuple(
            ring_two(k, orders[k][0], part, rec2, 4 * WIN, side) for side in (True, False)
        )

    def first_relay(k):
        late[k] = ring_relay(k, orders[k][0], part, rec1, rec2, 4 * WIN, early[k])

    def second_start(k):
        made = ring_sum(k, orders[k][0], part, rec2, middle[k] + late[k])
        part2[k] = made.astype(BF16).reshape(4, WIN, 128)
        late2[k] = direct(k, orders[k][1], part2, rec4, rec5, WIN)

    base = 56

    def z_copy(lane, slot, comp, k, device):
        return pltpu.make_async_remote_copy(
            src_ref=zsend.at[lane, slot], dst_ref=zrec.at[comp, k, lane],
            send_sem=ssem.at[base + lane * 8 + slot],
            recv_sem=rsem.at[base + lane * 8 + comp * 4 + k],
            device_id=device, device_id_type=MESH,
        )

    def z_used(k, hop, cc):
        used_here = (g == 1) if k == 2 else (g >= 0)
        if hop == 0:
            used_here = used_here & ((core != g) | (core != cc))
        return used_here

    def third_start(k):
        dsum[0:WIN] = ring_sum(k, orders[k][1], part2, rec4, late2[k]) + rec5[k].astype(F32)
        dsum[WIN:WIN + 16] = jnp.zeros((16, 128), F32)
        for hop in (0, 1, 3, 2):
            zz = (z + hop) % 4
            place = g * (8 * (y % 2) + 54 * zz) + (1 - g) * ((12 * y) % 16 + 27 * zz)
            for cc in range(2):
                slot = 2 * hop + cc
                zsend[k, slot] = dsum[pl.ds(place + 27 * cc * g, 32), :].astype(BF16)

                @pl.when(z_used(k, hop, cc))
                def _():
                    z_copy(k, slot, g, (4 - hop) % 4, (core, spot(x, y, zz, cc))).start()

    def third_end(k):
        @pl.when(core == g)
        def _():
            zrec[g, 0, k] = zsend[k, core]

        for comp in range(2):
            if comp == 0 and k == 2:
                continue
            for source in range(4):
                copy = z_copy(k, 0, comp, source, (g, mate))
                if source > 0:
                    copy.wait_recv()
                else:
                    @pl.when((core != g) | (g != comp))
                    def _():
                        copy.wait_recv()

            total = zrec[comp, 0, k].astype(F32)
            for source in range(1, 4):
                total = total + zrec[comp, source, k].astype(F32)
            grads_ref[comp, k] = total
        for hop in range(4):
            for cc in range(2):
                slot = 2 * hop + cc

                @pl.when(z_used(k, hop, cc))
                def _():
                    z_copy(k, slot, g, 0, (g, mate)).wait_send()

    def forward_output():
        for row in (1, 2):
            put_cat(hcat, row, hp[row].astype(F32))
        h_low.wait_recv()
        h_top.wait_recv()
        put_cat(hcat, 0, hp[0].astype(F32) * has_top)
        put_cat(hcat, 3, hp[3].astype(F32) * has_low)
        next_ref[...] = (up[1:3].astype(F32) + conv(hcat, 1).reshape(2, COLS, CH)).astype(BF16)

    def backward_output():
        f_low.wait_recv()
        f_top.wait_recv()
        for row in range(4):
            values = fp[row].astype(F32)
            if edge[row] is not None:
                values = values * edge[row]
            for q, shifted in enumerate(lane_shifts(turn(values))):
                ft[q, :, row * COLS:(row + 1) * COLS] = shifted
        total = None
        for p in range(3):
            for q in range(3):
                term = mm(
                    w[0, 2 - p, (2 - q) * CH:(3 - q) * CH, :],
                    ft[q, :, p * COLS:(p + 2) * COLS],
                )
                total = term if total is None else total + term
        ig[...] = g_ref[...].reshape(2 * COLS, CH).astype(F32) + total.T
        for row in range(2):
            grad = ig[row * COLS:(row + 1) * COLS, :]
            high = grad.astype(BF16)
            low = (grad - high.astype(F32)).astype(BF16)
            shown = (nt_dot(c16[...], high) + nt_dot(c16[...], low))[0:8] * wm[row, 0]
            tr2s[row] = shown + pltpu.roll(shown, 4, 0)

    gradient_block((x + 2) % 4)
    early[0] = ring_one(0, orders[0][0], part, rec1, 4 * WIN)
    gradient_block((x + 1) % 4)
    gradient_block((x + 3) % 4)
    gradient_block(x)

    for k in (1, 2):
        early[k] = ring_one(k, orders[k][0], part, rec1, 4 * WIN)
    for k in range(3):
        first_two(k)

    forward_output()
    for k in range(3):
        first_relay(k)

    backward_output()
    back = send(tr2s, tr2r, (1 - g, lat))
    for k in range(3):
        second_start(k)
    for k in range(3):
        third_start(k)
    arrive(back)
    for row in range(2):
        left = split_pair(wm[row, 0] * wm[row, 1] * tr2r[row])
        total = ig[row * COLS:(row + 1) * COLS, :] + tn_dot(left, m16[...])
        fgrad_ref[row] = total.astype(BF16)
    assert len(used) <= base
    for k in range(3):
        third_end(k)
    for copy in used:
        copy.wait_send()


def finish_body(next_in, fgrad_in, grads_in, next_out, fgrad_out, ocean_out, atmos_out, flat):
    next_out[0] = next_in[...]
    fgrad_out[0] = fgrad_in[...]
    atmos_factor = 1.0 / math.sqrt(256 * 128)
    for lane in range(3):
        atmos_out[pl.ds(lane, 27, stride=3), :] = grads_in[1, lane, 0:27, :] * atmos_factor
    left = lax.broadcasted_iota(jnp.int32, (14, 128), 1) < 64

    def rows(lane, start):
        return grads_in[0, lane, pl.ds(start, 14, stride=2), :] * (1.0 / 256.0)

    even_0, even_1, odd_0, odd_1 = rows(0, 0), rows(1, 0), rows(0, 1), rows(1, 1)
    odd_0, odd_1 = pltpu.roll(odd_0, 64, 1), pltpu.roll(odd_1, 64, 1)
    flat[pl.ds(0, 14, stride=3), :] = even_0
    flat[pl.ds(1, 14, stride=3), :] = jnp.where(left, even_1, odd_0)
    flat[pl.ds(2, 14, stride=3), :] = jnp.where(left, odd_0, odd_1)
    core = lax.axis_index("lat") % 2

    @pl.when(core == 0)
    def _():
        ocean_out[...] = flat[0:21]

    @pl.when(core == 1)
    def _():
        here = pltpu.roll(flat[20:41], 96, 1)
        after = pltpu.roll(flat[21:42], 96, 1)
        lanes = lax.broadcasted_iota(jnp.int32, (21, 128), 1)
        ocean_out[...] = jnp.where(lanes < 96, here, after)


def local(
    fields, cotangent, ocean_kernels, atmos_kernels, ocean_surface, ocean_coupling,
    atmos_flux, atmos_coupling, row_map, wet_mask,
):
    del row_map
    vmem = pl.BlockSpec(memory_space=pltpu.VMEM)
    hbm = pl.BlockSpec(memory_space=pl.ANY)
    rows4 = pltpu.VMEM((4, COLS, CH), BF16)
    rows2 = pltpu.VMEM((2, COLS, CH), BF16)
    cat4 = pltpu.VMEM((4, COLS, 3 * CH), BF16)
    wide = pltpu.VMEM((2 * COLS, CH), F32)
    small2, small4 = pltpu.VMEM((2, 8, COLS), F32), pltpu.VMEM((4, 8, COLS), F32)

    def buf(*shape):
        return pltpu.VMEM(shape, BF16)

    limits = dict(vmem_limit_bytes=56 * 1024 * 1024)
    next_field, field_grad, grads = pl.pallas_call(
        body,
        out_shape=(
            pltpu.VMEM((2, COLS, CH), BF16),
            pltpu.VMEM((2, COLS, CH), BF16),
            pltpu.VMEM((2, 3, 32, 128), F32),
        ),
        in_specs=[hbm] * 9,
        out_specs=(vmem, vmem, vmem),
        scratch_shapes=[
            buf(4, 192), buf(4, 192), buf(4, CH), buf(4, CH), pltpu.VMEM((2, 256), jnp.int32),
            rows2, rows2, buf(2, 3, 3 * CH, CH), buf(2, 3, 576, 192),
            rows4, rows4, rows4, rows4, rows4, cat4, cat4, cat4,
            buf(3, 3 * CH, CH), buf(3, CH, 4 * COLS),
            pltpu.VMEM((8, CH), F32), pltpu.VMEM((8, CH), F32), buf(16, CH), buf(16, CH),
            pltpu.VMEM((2, 2, 8, COLS), F32), small4, small2, small4, small2, small2, wide, wide,
            rows2, rows2, rows2, rows2, buf(768, CH), buf(768, 256), buf(6, 3 * CH, COLS),
            buf(3, 4, 4 * WIN, 128), buf(3, 2, 2 * WIN, 128), buf(3, 2, 4 * WIN, 128),
            buf(3, 4, WIN, 128), buf(3, WIN, 128), buf(3, 2, WIN, 128),
            pltpu.VMEM((240, 128), F32), buf(3, 8, 32, 128), buf(2, 4, 3, 32, 128),
            pltpu.SemaphoreType.DMA((9,)), pltpu.SemaphoreType.DMA((NSEM,)),
            pltpu.SemaphoreType.DMA((NSEM,)),
        ],
        compiler_params=pltpu.CompilerParams(
            collective_id=0, has_side_effects=True, **limits
        ),
        cost_estimate=pl.CostEstimate(
            flops=4_100_000_000, bytes_accessed=8_000_000, transcendentals=100_000
        ),
    )(
        fields[0], cotangent[0], atmos_kernels.reshape(2, 3, 3 * CH, CH),
        ocean_kernels.reshape(2, 3, 576, 192), ocean_surface.T, ocean_coupling, atmos_flux.T,
        atmos_coupling, wet_mask,
    )
    next_field, field_grad, ocean_rows, atmos_rows = pl.pallas_call(
        finish_body,
        out_shape=(
            jax.ShapeDtypeStruct((1, 2, COLS, CH), BF16),
            jax.ShapeDtypeStruct((1, 2, COLS, CH), BF16),
            jax.ShapeDtypeStruct((21, 128), F32),
            jax.ShapeDtypeStruct((81, 128), F32),
        ),
        in_specs=[vmem, vmem, vmem],
        out_specs=(vmem, vmem, vmem, vmem),
        scratch_shapes=[pltpu.VMEM((48, 128), F32)],
        compiler_params=pltpu.CompilerParams(vmem_limit_bytes=4 * 1024 * 1024),
    )(next_field, field_grad, grads)
    return (next_field, field_grad, ocean_rows.reshape(-1)[:2592], atmos_rows.reshape(-1))


def solution(mesh):
    in_specs = (
        P("grp", "lat", None, None),
        P("grp", "lat", None, None),
        P(),
        P(),
        P(),
        P(),
        P(),
        P(),
        P("lat"),
        P("lat", None),
    )
    out_specs = (
        P("grp", "lat", None, None),
        P("grp", "lat", None, None),
        P(("grp", "lat")),
        P(("grp", "lat")),
    )
    return jax.shard_map(local, mesh=mesh, in_specs=in_specs, out_specs=out_specs, check_vma=False)
```

```python
import math

import jax
import jax.numpy as jnp
from jax import lax
from jax.experimental import pallas as pl
from jax.experimental.pallas import tpu as pltpu
from jax.sharding import PartitionSpec as P

MESH = pl.DeviceIdType.MESH
F32 = jnp.float32
BF16 = jnp.bfloat16
GELU_SCALE = 0.7978845608028654
GELU_CUBIC = 0.044715
CH = 384
COLS = 128
WIN = 224
NSEM = 80


def nt_dot(a, b):
    return lax.dot_general(a, b, (((1,), (1,)), ((), ())), preferred_element_type=F32)


def tn_dot(a, b):
    return lax.dot_general(a, b, (((0,), (0,)), ((), ())), preferred_element_type=F32)


def mm(a, b):
    return jnp.dot(a, b, preferred_element_type=F32)


def split_pair(values):
    high = values.astype(BF16).astype(F32)
    return jnp.concatenate([high, values - high], axis=0).astype(BF16)


def body(
    x_hbm, g_hbm, ak_ref, ok_ref, os_hbm, oc_hbm, af_hbm, ac_hbm, wet_hbm,
    next_ref, fgrad_ref, grads_ref,
    os_ref, oc_ref, af_ref, ac_ref, wet_ref, x_ref, g_ref, w, okv, xp, gp, hp, fp, up, gcat, ucat, hcat,
    wt, ft, m8, c8, m16, c16, wm, wmp, trs, trp, tr2s, tr2r, bh, ig,
    s_a, r_a, s_b, r_b, b6, b6s, at6,
    part, rec1, rec2, part2, rec5, rec4, dsum, zsend, zrec,
    wsem, ssem, rsem,
):
    g = lax.axis_index("grp")
    lat = lax.axis_index("lat")
    core = lat % 2
    z = (lat // 2) % 4
    y = (lat // 8) % 4
    x = lat // 32

    def spot(xx, yy, zz, cc):
        return xx * 32 + yy * 8 + zz * 2 + cc

    dn = (lat + 1) % 128
    up_lat = (lat + 127) % 128
    x_plus, x_minus = spot((x + 1) % 4, y, z, core), spot((x + 3) % 4, y, z, core)
    y_plus, y_minus = spot(x, (y + 1) % 4, z, core), spot(x, (y + 3) % 4, z, core)
    x_far, y_far = spot((x + 2) % 4, y, z, core), spot(x, (y + 2) % 4, z, core)
    mate = lat + 1 - 2 * core
    has_top = jnp.where(lat > 0, 1.0, 0.0).astype(F32)
    has_low = jnp.where(lat < 127, 1.0, 0.0).astype(F32)
    edge = [has_top, None, None, has_low]

    x_copy = pltpu.make_async_copy(x_hbm, x_ref, wsem.at[2])
    g_copy = pltpu.make_async_copy(g_hbm, g_ref, wsem.at[3])
    maps = [
        pltpu.make_async_copy(src, dst, wsem.at[4 + index])
        for index, (src, dst) in enumerate((
            (os_hbm, os_ref), (oc_hbm, oc_ref), (af_hbm, af_ref), (ac_hbm, ac_ref),
            (wet_hbm, wet_ref),
        ))
    ]
    for copy in (*maps, x_copy, g_copy):
        copy.start()

    barrier = pltpu.get_barrier_semaphore()
    partners = [(g, dn), (g, up_lat), (1 - g, dn), (1 - g, up_lat)]
    partners += [(g, other) for other in (x_plus, x_minus, x_far, y_plus, y_minus, y_far)]
    for step in range(16):
        if step > 0:
            hop = (step // 2) % 4
            partners.append(
                ((g + step // 8) % 2, spot(x, y, (z + hop) % 4, (core + step) % 2))
            )
    for device in partners:
        pl.semaphore_signal(barrier, inc=1, device_id=device, device_id_type=MESH)

    atmos_copy = pltpu.make_async_copy(ak_ref, w, wsem.at[0])
    ocean_copy = pltpu.make_async_copy(ok_ref, okv, wsem.at[1])

    @pl.when(g == 1)
    def _():
        atmos_copy.start()

    @pl.when(g == 0)
    def _():
        ocean_copy.start()

    half = CH // 2
    row_id = lax.broadcasted_iota(jnp.int32, (half, CH), 0)
    lane_id = lax.broadcasted_iota(jnp.int32, (half, CH), 1)
    lower = jnp.where(row_id == lane_id, 1.0, 0.0).astype(BF16)
    upper = jnp.where(row_id + half == lane_id, 1.0, 0.0).astype(BF16)
    for copy in maps:
        copy.wait()
    is_atmos = g.astype(F32)
    is_ocean = 1.0 - is_atmos
    for dst, ocean, atmos in ((m8, os_ref, af_ref), (c8, oc_ref, ac_ref)):
        dst[0:4] = mm(ocean[...], lower) * is_ocean + atmos[...].astype(F32) * is_atmos
        dst[4:8] = mm(ocean[...], upper) * is_ocean
    for dst, src in ((m16, m8), (c16, c8)):
        dst[...] = jnp.concatenate([src[...], src[...]], axis=0).astype(BF16)
    pick_row = lax.broadcasted_iota(jnp.int32, (256, 256), 0)
    pick_lane = lax.broadcasted_iota(jnp.int32, (256, 256), 1)
    pick_lane = jnp.where(pick_lane < COLS, 2 * pick_lane, 2 * pick_lane - 255)
    pick = jnp.where(pick_row == pick_lane, 1.0, 0.0).astype(BF16)
    first_half = lax.broadcasted_iota(jnp.int32, (8, COLS), 0) < 4
    for row in range(2):
        wet = jnp.broadcast_to(wet_ref[row:row + 1, :].astype(F32), (8, 256)).astype(BF16)
        apart = mm(wet, pick)
        even, odd = apart[:, 0:COLS], apart[:, COLS:]
        inverse = 1.0 / jnp.maximum(even + odd, 1.0)
        wm[row, 0] = jnp.where(
            first_half, even * is_ocean + is_atmos, odd * is_ocean
        )
        wm[row, 1] = inverse * is_ocean + is_atmos

    x_copy.wait()
    for row in range(2):
        shown = nt_dot(m16[...], x_ref[row])[0:8] * wm[row, 0]
        trs[row] = (shown + pltpu.roll(shown, 4, 0)) * wm[row, 1]
    g_copy.wait()
    pl.semaphore_wait(barrier, len(partners))

    used = []

    def arrive(copy):
        copy.wait_recv()

    def send(src, dst, device):
        index = len(used)
        copy = pltpu.make_async_remote_copy(
            src_ref=src, dst_ref=dst, send_sem=ssem.at[index], recv_sem=rsem.at[index],
            device_id=device, device_id_type=MESH,
        )
        copy.start()
        used.append(copy)
        return copy

    t_mid = send(trs, trp.at[pl.ds(1, 2)], (1 - g, lat))
    t_low = send(trs.at[1], trp.at[0], (1 - g, dn))
    t_top = send(trs.at[0], trp.at[3], (1 - g, up_lat))
    m_low = send(wm.at[1, 0], wmp.at[0], (g, dn))
    m_top = send(wm.at[0, 0], wmp.at[3], (g, up_lat))
    x_low = send(x_ref.at[1], xp.at[0], (g, dn))
    x_top = send(x_ref.at[0], xp.at[3], (g, up_lat))
    g_low = send(g_ref.at[1], gp.at[0], (g, dn))
    g_top = send(g_ref.at[0], gp.at[3], (g, up_lat))

    column = lax.broadcasted_iota(jnp.int32, (COLS, CH), 0)

    def put_cat(dst, index, values):
        dst[index, :, CH:2 * CH] = values.astype(BF16)
        dst[index, :, 0:CH] = jnp.where(column > 0, pltpu.roll(values, 1, 0), 0.0).astype(BF16)
        dst[index, :, 2 * CH:3 * CH] = jnp.where(
            column < COLS - 1, pltpu.roll(values, COLS - 1, 0), 0.0
        ).astype(BF16)

    def conv(cat, layer):
        total = None
        for p in range(3):
            term = mm(cat[p:p + 2].reshape(2 * COLS, 3 * CH), w[layer, p])
            total = term if total is None else total + term
        return total

    def back_rows(p, row, count):
        return mm(gcat[row:row + count].reshape(count * COLS, 3 * CH), wt[p])

    lane_of = lax.broadcasted_iota(jnp.int32, (CH, COLS), 1)

    def turn(values):
        return values.astype(F32).T

    def lane_shifts(turned):
        earlier = jnp.where(lane_of > 0, pltpu.roll(turned, 1, 1), 0.0)
        later = jnp.where(lane_of < COLS - 1, pltpu.roll(turned, COLS - 1, 1), 0.0)
        return [part.astype(BF16) for part in (earlier, turned, later)]

    def put_turned(index, values):
        at6[index] = jnp.concatenate(lane_shifts(turn(values)), axis=0)

    @pl.when(g == 0)
    def _():
        ocean_copy.wait()
        for layer in range(2):
            for p in range(3):
                low = mm(okv[layer, p], lower)
                high = mm(okv[layer, p], upper)
                none = jnp.zeros((half, CH), F32)
                both = jnp.concatenate([low, none], axis=0) + jnp.concatenate([none, high], axis=0)
                w[layer, p, 0:half, :] = none.astype(BF16)
                w[layer, p, half:5 * half, :] = both.astype(BF16)
                w[layer, p, 5 * half:6 * half, :] = none.astype(BF16)

    @pl.when(g == 1)
    def _():
        atmos_copy.wait()

    for row in range(2):
        put_cat(gcat, row + 1, g_ref[row].astype(F32))
    for p in range(3):
        for q in range(3):
            wt[p, q * CH:(q + 1) * CH, :] = w[1, 2 - p, (2 - q) * CH:(3 - q) * CH, :].T
    bh[...] = back_rows(1, 1, 2)
    bh[0:COLS] += back_rows(2, 2, 1)
    bh[COLS:] += back_rows(0, 1, 1)

    def layer_input(index):
        values = xp[index] if index in (0, 3) else x_ref[index - 1]
        mask = wmp[index] if index in (0, 3) else wm[index - 1, 0]
        term = tn_dot(split_pair(mask * trp[index]), c16[...])
        total = (values.astype(F32) + term).astype(BF16).astype(F32)
        if edge[index] is not None:
            total = total * edge[index]
        up[index] = total.astype(BF16)
        put_cat(ucat, index, total)
        put_turned(index, total)

    arrive(t_mid)
    layer_input(1)
    layer_input(2)
    ig[...] = mm(ucat[1:3].reshape(2 * COLS, 3 * CH), w[0, 1])
    ig[0:COLS] += mm(ucat[2], w[0, 2])
    ig[COLS:] += mm(ucat[1], w[0, 0])
    for copy in (m_low, m_top, t_low, t_top, x_low, x_top):
        arrive(copy)
    layer_input(0)
    layer_input(3)
    ig[0:COLS] += mm(ucat[0], w[0, 0])
    ig[COLS:] += mm(ucat[3], w[0, 2])

    zed = ig[...]
    tangent = jnp.tanh(GELU_SCALE * (zed + GELU_CUBIC * zed * zed * zed))
    hidden = (0.5 * zed * (1.0 + tangent)).astype(BF16).reshape(2, COLS, CH)
    hp[1:3] = hidden
    ig[...] = 0.5 * (1.0 + tangent) + 0.5 * zed * (1.0 - tangent * tangent) * GELU_SCALE * (
        1.0 + 3.0 * GELU_CUBIC * zed * zed
    )

    arrive(g_low)
    arrive(g_top)
    top_values = gp[0].astype(F32) * has_top
    low_values = gp[3].astype(F32) * has_low
    gp[0] = top_values.astype(BF16)
    gp[3] = low_values.astype(BF16)
    put_cat(gcat, 0, top_values)
    put_cat(gcat, 3, low_values)

    @pl.when(core == 0)
    def _():
        s_a[0] = gp[0]
        s_a[1] = g_ref[0]

    @pl.when(core == 1)
    def _():
        s_a[...] = up[2:4]

    pair_a = send(s_a, r_a, (g, mate))
    bh[0:COLS] += back_rows(0, 0, 1)
    bh[COLS:] += back_rows(2, 3, 1)

    first_grad = (bh[...] * ig[...]).astype(BF16).reshape(2, COLS, CH)
    fp[1:3] = first_grad

    @pl.when(core == 0)
    def _():
        s_b[...] = hp[1:3]

    @pl.when(core == 1)
    def _():
        s_b[...] = fp[1:3]

    pair_b = send(s_b, r_b, (g, mate))
    h_low = send(hp.at[2], hp.at[0], (g, dn))
    h_top = send(hp.at[1], hp.at[3], (g, up_lat))
    f_low = send(fp.at[2], fp.at[0], (g, dn))
    f_top = send(fp.at[1], fp.at[3], (g, up_lat))

    arrive(pair_a)
    for row in range(2):
        put_turned(4 - 2 * core + row, jnp.where(core == 0, r_a[row], hp[row + 1]))

    @pl.when(core == 0)
    def _():
        b6[0:256] = fp[1:3].reshape(256, CH)

    @pl.when(core == 1)
    def _():
        b6[0:256] = r_a[...].reshape(256, CH)
        b6[256:384] = gp[0]
        b6[384:640] = g_ref[...].reshape(256, CH)
        b6[640:768] = gp[3]

    arrive(pair_b)

    @pl.when(core == 0)
    def _():
        b6[256:512] = r_b[...].reshape(256, CH)

    @pl.when(core == 1)
    def _():
        for row in range(2):
            put_turned(row, r_b[row])

    @pl.when(g == 0)
    def _():
        swap_row = lax.broadcasted_iota(jnp.int32, (CH, 256), 0)
        swap_lane = lax.broadcasted_iota(jnp.int32, (CH, 256), 1)
        swap = jnp.where(swap_row == swap_lane + 192, 1.0, 0.0).astype(BF16)
        b6s[...] = mm(b6[...], swap).astype(BF16)


    ids_x, ids_y = (x, x_plus, x_minus, x_far), (y, y_plus, y_minus, y_far)
    mixed_a = tuple(a + core * (b - a) for a, b in zip(ids_x, ids_y))
    mixed_b = tuple(b + core * (a - b) for a, b in zip(ids_x, ids_y))
    orders = [(ids_x, ids_y), (ids_y, ids_x), (mixed_a, mixed_b)]

    atmos_pieces = [
        [(0, 0, 0, 224), (208, 1, 0, 80)],
        [(0, 1, 80, 144), (144, 2, 0, 144)],
        [(0, 2, 144, 80), (64, 3, 0, 224)],
    ]
    ocean_pieces = [
        [(0, 0, 0, 112), (96, 1, 0, 48)],
        [(0, 1, 48, 80), (64, 2, 0, 80)],
        [(0, 2, 80, 48), (32, 3, 0, 112)],
    ]

    def gradient_block(xq):
        def operands(j, rows, shift):
            m = 3 * xq + j
            p = m // 4
            left = pl.ds(pl.multiple_of((m % 4) * rows + shift, 16), rows)
            lead = (1 - core) * p
            turned = jnp.concatenate([at6[lead + k, left, :] for k in range(4)], axis=1)
            return turned, pl.ds(pl.multiple_of(core * (2 - p) * COLS, 16), 512)

        def store(lane, made, pieces):
            for src, yq, dst, count in pieces:
                if lane == 0:
                    a, b = xq, yq
                elif lane == 1:
                    a, b = yq, xq
                else:
                    a, b = xq + core * (yq - xq), yq + core * (xq - yq)
                rows = pl.ds(pl.multiple_of(b * WIN + dst, 16), count)
                part[lane, a, rows, :] = made[src:src + count]

        @pl.when(g == 1)
        def _():
            for j in range(3):
                turned, right = operands(j, 288, 0)
                made = mm(turned, b6[right, :]).astype(BF16)
                for lane in range(3):
                    store(lane, made[:, 128 * lane:128 * (lane + 1)], atmos_pieces[j])

        @pl.when(g == 0)
        def _():
            for j in range(3):
                even, right = operands(j, 144, 192)
                odd, _ = operands(j, 144, 384)
                made = mm(even, b6[right, 0:256]) + mm(odd, b6s[right, :])
                made = made.astype(BF16)
                for lane in range(2):
                    store(lane, made[:, 128 * lane:128 * (lane + 1)], ocean_pieces[j])

    def parts_of(rows):
        return pl.ds(0, rows // 2), pl.ds(rows // 2, rows // 2)

    def ring_one(lane, ids, source, near, rows):
        me, plus, minus, far_id = ids
        low, high = parts_of(rows)
        across = (me + 2) % 4
        one_p = send(source.at[lane, across, low], near.at[lane, 0], (g, plus))
        one_m = send(source.at[lane, across, high], near.at[lane, 1], (g, minus))
        return one_p, one_m

    def ring_two(lane, ids, source, far, rows, plus_side):
        me, plus, minus, far_id = ids
        low, high = parts_of(rows)
        if plus_side:
            return send(source.at[lane, (me + 1) % 4, high], far.at[lane, 0, high], (g, plus))
        return send(source.at[lane, (me + 3) % 4, low], far.at[lane, 1, low], (g, minus))

    def direct(lane, ids, source, far, wide, rows):
        me, plus, minus, far_id = ids
        return (
            send(source.at[lane, (me + 2) % 4], wide.at[lane], (g, far_id)),
            send(source.at[lane, (me + 1) % 4], far.at[lane, 0], (g, plus)),
            send(source.at[lane, (me + 3) % 4], far.at[lane, 1], (g, minus)),
        )

    def ring_relay(lane, ids, source, near, far, rows, early):
        me, plus, minus, far_id = ids
        low, high = parts_of(rows)
        ahead, behind = (me + 1) % 4, (me + 3) % 4
        arrive(early[0])
        source[lane, ahead, low, :] = (
            source[lane, ahead, low, :].astype(F32) + near[lane, 0].astype(F32)
        ).astype(BF16)
        three_p = send(source.at[lane, ahead, low], far.at[lane, 0, low], (g, plus))
        arrive(early[1])
        source[lane, behind, high, :] = (
            source[lane, behind, high, :].astype(F32) + near[lane, 1].astype(F32)
        ).astype(BF16)
        three_m = send(source.at[lane, behind, high], far.at[lane, 1, high], (g, minus))
        return three_p, three_m

    def ring_sum(lane, ids, source, far, late):
        for copy in late:
            arrive(copy)
        me = ids[0]
        return source[lane, me].astype(F32) + far[lane, 0].astype(F32) + far[lane, 1].astype(F32)

    early, middle, late = [None] * 3, [None] * 3, [None] * 3
    early2, middle2, late2 = [None] * 3, [None] * 3, [None] * 3

    def first_two(k):
        middle[k] = tuple(
            ring_two(k, orders[k][0], part, rec2, 4 * WIN, side) for side in (True, False)
        )

    def first_relay(k):
        late[k] = ring_relay(k, orders[k][0], part, rec1, rec2, 4 * WIN, early[k])

    def second_start(k):
        made = ring_sum(k, orders[k][0], part, rec2, middle[k] + late[k])
        part2[k] = made.astype(BF16).reshape(4, WIN, 128)
        late2[k] = direct(k, orders[k][1], part2, rec4, rec5, WIN)

    base = 56

    def z_copy(lane, slot, comp, k, device):
        return pltpu.make_async_remote_copy(
            src_ref=zsend.at[lane, slot], dst_ref=zrec.at[comp, k, lane],
            send_sem=ssem.at[base + lane * 8 + slot],
            recv_sem=rsem.at[base + lane * 8 + comp * 4 + k],
            device_id=device, device_id_type=MESH,
        )

    def z_used(k, hop, cc):
        used_here = (g == 1) if k == 2 else (g >= 0)
        if hop == 0:
            used_here = used_here & ((core != g) | (core != cc))
        return used_here

    def third_start(k):
        dsum[0:WIN] = ring_sum(k, orders[k][1], part2, rec4, late2[k]) + rec5[k].astype(F32)
        dsum[WIN:WIN + 16] = jnp.zeros((16, 128), F32)
        for hop in (0, 1, 3, 2):
            zz = (z + hop) % 4
            place = g * (8 * (y % 2) + 54 * zz) + (1 - g) * ((12 * y) % 16 + 27 * zz)
            for cc in range(2):
                slot = 2 * hop + cc
                zsend[k, slot] = dsum[pl.ds(place + 27 * cc * g, 32), :].astype(BF16)

                @pl.when(z_used(k, hop, cc))
                def _():
                    z_copy(k, slot, g, (4 - hop) % 4, (core, spot(x, y, zz, cc))).start()

    def third_end(k):
        @pl.when(core == g)
        def _():
            zrec[g, 0, k] = zsend[k, core]

        for comp in range(2):
            if comp == 0 and k == 2:
                continue
            for source in range(4):
                copy = z_copy(k, 0, comp, source, (g, mate))
                if source > 0:
                    copy.wait_recv()
                else:
                    @pl.when((core != g) | (g != comp))
                    def _():
                        copy.wait_recv()

            total = zrec[comp, 0, k].astype(F32)
            for source in range(1, 4):
                total = total + zrec[comp, source, k].astype(F32)
            grads_ref[comp, k] = total
        for hop in range(4):
            for cc in range(2):
                slot = 2 * hop + cc

                @pl.when(z_used(k, hop, cc))
                def _():
                    z_copy(k, slot, g, 0, (g, mate)).wait_send()

    def forward_output():
        for row in (1, 2):
            put_cat(hcat, row, hp[row].astype(F32))
        h_low.wait_recv()
        h_top.wait_recv()
        put_cat(hcat, 0, hp[0].astype(F32) * has_top)
        put_cat(hcat, 3, hp[3].astype(F32) * has_low)
        next_ref[...] = (up[1:3].astype(F32) + conv(hcat, 1).reshape(2, COLS, CH)).astype(BF16)

    def backward_output():
        f_low.wait_recv()
        f_top.wait_recv()
        for row in range(4):
            values = fp[row].astype(F32)
            if edge[row] is not None:
                values = values * edge[row]
            for q, shifted in enumerate(lane_shifts(turn(values))):
                ft[q, :, row * COLS:(row + 1) * COLS] = shifted
        total = None
        for p in range(3):
            for q in range(3):
                term = mm(
                    w[0, 2 - p, (2 - q) * CH:(3 - q) * CH, :],
                    ft[q, :, p * COLS:(p + 2) * COLS],
                )
                total = term if total is None else total + term
        ig[...] = g_ref[...].reshape(2 * COLS, CH).astype(F32) + total.T
        for row in range(2):
            grad = ig[row * COLS:(row + 1) * COLS, :]
            high = grad.astype(BF16)
            low = (grad - high.astype(F32)).astype(BF16)
            shown = (nt_dot(c16[...], high) + nt_dot(c16[...], low))[0:8] * wm[row, 0]
            tr2s[row] = shown + pltpu.roll(shown, 4, 0)

    gradient_block((x + 2) % 4)
    early[0] = ring_one(0, orders[0][0], part, rec1, 4 * WIN)
    gradient_block((x + 1) % 4)
    gradient_block((x + 3) % 4)
    gradient_block(x)

    for k in (1, 2):
        early[k] = ring_one(k, orders[k][0], part, rec1, 4 * WIN)
    for k in range(3):
        first_two(k)

    forward_output()
    for k in range(3):
        first_relay(k)

    backward_output()
    back = send(tr2s, tr2r, (1 - g, lat))
    for k in range(3):
        second_start(k)
    for k in range(3):
        third_start(k)
    arrive(back)
    for row in range(2):
        left = split_pair(wm[row, 0] * wm[row, 1] * tr2r[row])
        total = ig[row * COLS:(row + 1) * COLS, :] + tn_dot(left, m16[...])
        fgrad_ref[row] = total.astype(BF16)
    assert len(used) <= base
    for k in range(3):
        third_end(k)
    for copy in used:
        copy.wait_send()


def finish_body(next_in, fgrad_in, grads_in, next_out, fgrad_out, ocean_out, atmos_out, flat, spread):
    next_out[0] = next_in[...]
    fgrad_out[0] = fgrad_in[...]
    atmos_factor = 1.0 / math.sqrt(256 * 128)
    for lane in range(3):
        spread[pl.ds(lane, 32, stride=3), :] = grads_in[1, lane] * atmos_factor
    atmos_out[...] = spread[0:81]
    left = lax.broadcasted_iota(jnp.int32, (14, 128), 1) < 64

    def rows(lane, start):
        return grads_in[0, lane, pl.ds(start, 14, stride=2), :] * (1.0 / 256.0)

    even_0, even_1, odd_0, odd_1 = rows(0, 0), rows(1, 0), rows(0, 1), rows(1, 1)
    odd_0, odd_1 = pltpu.roll(odd_0, 64, 1), pltpu.roll(odd_1, 64, 1)
    flat[pl.ds(0, 14, stride=3), :] = even_0
    flat[pl.ds(1, 14, stride=3), :] = jnp.where(left, even_1, odd_0)
    flat[pl.ds(2, 14, stride=3), :] = jnp.where(left, odd_0, odd_1)
    core = lax.axis_index("lat") % 2

    @pl.when(core == 0)
    def _():
        ocean_out[...] = flat[0:21]

    @pl.when(core == 1)
    def _():
        here = pltpu.roll(flat[20:41], 96, 1)
        after = pltpu.roll(flat[21:42], 96, 1)
        lanes = lax.broadcasted_iota(jnp.int32, (21, 128), 1)
        ocean_out[...] = jnp.where(lanes < 96, here, after)


def local(
    fields, cotangent, ocean_kernels, atmos_kernels, ocean_surface, ocean_coupling,
    atmos_flux, atmos_coupling, row_map, wet_mask,
):
    del row_map
    vmem = pl.BlockSpec(memory_space=pltpu.VMEM)
    hbm = pl.BlockSpec(memory_space=pl.ANY)
    rows4 = pltpu.VMEM((4, COLS, CH), BF16)
    rows2 = pltpu.VMEM((2, COLS, CH), BF16)
    cat4 = pltpu.VMEM((4, COLS, 3 * CH), BF16)
    wide = pltpu.VMEM((2 * COLS, CH), F32)
    small2, small4 = pltpu.VMEM((2, 8, COLS), F32), pltpu.VMEM((4, 8, COLS), F32)

    def buf(*shape):
        return pltpu.VMEM(shape, BF16)

    limits = dict(vmem_limit_bytes=56 * 1024 * 1024)
    next_field, field_grad, grads = pl.pallas_call(
        body,
        out_shape=(
            pltpu.VMEM((2, COLS, CH), BF16),
            pltpu.VMEM((2, COLS, CH), BF16),
            pltpu.VMEM((2, 3, 32, 128), F32),
        ),
        in_specs=[hbm] * 9,
        out_specs=(vmem, vmem, vmem),
        scratch_shapes=[
            buf(4, 192), buf(4, 192), buf(4, CH), buf(4, CH), pltpu.VMEM((2, 256), jnp.int32),
            rows2, rows2, buf(2, 3, 3 * CH, CH), buf(2, 3, 576, 192),
            rows4, rows4, rows4, rows4, rows4, cat4, cat4, cat4,
            buf(3, 3 * CH, CH), buf(3, CH, 4 * COLS),
            pltpu.VMEM((8, CH), F32), pltpu.VMEM((8, CH), F32), buf(16, CH), buf(16, CH),
            pltpu.VMEM((2, 2, 8, COLS), F32), small4, small2, small4, small2, small2, wide, wide,
            rows2, rows2, rows2, rows2, buf(768, CH), buf(768, 256), buf(6, 3 * CH, COLS),
            buf(3, 4, 4 * WIN, 128), buf(3, 2, 2 * WIN, 128), buf(3, 2, 4 * WIN, 128),
            buf(3, 4, WIN, 128), buf(3, WIN, 128), buf(3, 2, WIN, 128),
            pltpu.VMEM((240, 128), F32), buf(3, 8, 32, 128), buf(2, 4, 3, 32, 128),
            pltpu.SemaphoreType.DMA((9,)), pltpu.SemaphoreType.DMA((NSEM,)),
            pltpu.SemaphoreType.DMA((NSEM,)),
        ],
        compiler_params=pltpu.CompilerParams(
            collective_id=0, has_side_effects=True, **limits
        ),
        cost_estimate=pl.CostEstimate(
            flops=4_100_000_000, bytes_accessed=8_000_000, transcendentals=100_000
        ),
    )(
        fields[0], cotangent[0], atmos_kernels.reshape(2, 3, 3 * CH, CH),
        ocean_kernels.reshape(2, 3, 576, 192), ocean_surface.T, ocean_coupling, atmos_flux.T,
        atmos_coupling, wet_mask,
    )
    next_field, field_grad, ocean_rows, atmos_rows = pl.pallas_call(
        finish_body,
        out_shape=(
            jax.ShapeDtypeStruct((1, 2, COLS, CH), BF16),
            jax.ShapeDtypeStruct((1, 2, COLS, CH), BF16),
            jax.ShapeDtypeStruct((21, 128), F32),
            jax.ShapeDtypeStruct((81, 128), F32),
        ),
        in_specs=[vmem, vmem, vmem],
        out_specs=(vmem, vmem, vmem, vmem),
        scratch_shapes=[pltpu.VMEM((56, 128), F32), pltpu.VMEM((104, 128), F32)],
        compiler_params=pltpu.CompilerParams(vmem_limit_bytes=4 * 1024 * 1024),
    )(next_field, field_grad, grads)
    return (next_field, field_grad, ocean_rows.reshape(-1)[:2592], atmos_rows.reshape(-1))


def solution(mesh):
    in_specs = (
        P("grp", "lat", None, None),
        P("grp", "lat", None, None),
        P(),
        P(),
        P(),
        P(),
        P(),
        P(),
        P("lat"),
        P("lat", None),
    )
    out_specs = (
        P("grp", "lat", None, None),
        P("grp", "lat", None, None),
        P(("grp", "lat")),
        P(("grp", "lat")),
    )
    return jax.shard_map(local, mesh=mesh, in_specs=in_specs, out_specs=out_specs, check_vma=False)
```
